32 devices in a mesh: groups: 2 (over x), tp: 4 (over y, core), rep: 4 (over z).
Axes of the slice: x: 2, y: 2, z: 4, core: 2. Of those that a mesh axis runs over, the one named last changes fastest.
Arguments:
- head_outputs: bfloat16 [8, 768, 8192], P(('groups', 'rep'), None, 'tp'), parts along dimension 0, may hold values from -6 to 6
- residual: bfloat16 [8, 768, 8192], P(('groups', 'rep'), 'tp'), parts along dimension 0, may hold values from -6 to 6
- projection: bfloat16 [8192, 8192], P('tp'), may hold values from -0.0625 to 0.0625
- shrink_pool: bfloat16 [128, 16, 8192], P(('groups', 'rep'), None, 'tp'), parts along dimension 0, may hold values from -0.0625 to 0.0625
- expand_pool: bfloat16 [128, 16, 8192], P(('groups', 'rep'), None, 'tp'), parts along dimension 0, may hold values from -0.75 to 0.75
- pool_slot: int32 [128], P('groups'), parts along dimension 0, may hold values from 0 to 63, as said below
- variant_list: int32 [8, 24], P('groups'), parts along dimension 0, may hold values from 0 to 63, as said below
- request_variant: int32 [8, 768], P(('groups', 'rep')), parts along dimension 0, may hold values from 0 to 63, as said below
Outputs:
- hidden_next: bfloat16 [8, 768, 8192], P(('groups', 'rep'), 'tp'), parts along dimension 0
The draws below stay inside these ranges and needn't reach their ends.
There are 2 independent parts, one for each index of `groups`. The reference program is written for one: setup_inputs(seed, part) draws one part's arguments, and reference() takes and returns one part's arrays. A program takes and returns all parts, laid end to end along the dimension named above; an argument that names none is the same for every part. Nothing has to cross between parts.
Inputs may be any that keep to these rules, and one draw needn't show every extreme that they name: A permutation: the factors of variant v are entry pool_slot[v] of shrink_pool and expand_pool. `variant_list`: row r lists 24 distinct variants for replica r. In one row at most 6 entries have the same pool_slot // 16, and every row has some value of it held by exactly 6 entries. `request_variant`: every request's variant is in its replica's row of variant_list; an entry of a list may be named by no request.
All inputs are finite; a program needn't handle non-finite values.
Results may differ from the reference program's by a relative error of at most 0.009.
Values may be sent and summed in bfloat16 or wider, within the bound.
No kernel may reach another device: no remote copies, remote signals or barrier semaphores. Data moves between devices by JAX's collectives and lax.ppermute only.
A program may use at most 192 MiB of HBM per device.

```python
import jax
import jax.numpy as jnp
from jax import lax

D = 8192
RANK = 16
VARIANTS = 64
ROWS = 768
LISTED = 24
POOL_DEV = 16
N_TP = 4
N_REP = 4


def permute_count(subkey, length):
    return jax.random.permutation(subkey, length).astype(jnp.int32)


def shared_batches(key):
    subkeys = jax.random.split(key, 6)
    slot_of = jax.random.permutation(subkeys[0], VARIANTS).astype(jnp.int32)
    at_position = jnp.argsort(slot_of).astype(jnp.int32)
    replicas = VARIANTS // POOL_DEV
    owner_orders = jax.vmap(partial_owner(replicas))(jax.random.split(subkeys[1], replicas))
    entries = jnp.arange(LISTED, dtype=jnp.int32)
    owners = owner_orders[:, entries // 2 % replicas]
    repeats = entries // (2 * replicas) * 2 + entries % 2
    local_orders = jax.vmap(partial_owner(POOL_DEV))(jax.random.split(subkeys[2], replicas))
    local_index = local_orders[:, repeats]
    positions = owners * POOL_DEV + local_index
    shuffles = jax.vmap(partial_owner(LISTED))(jax.random.split(subkeys[3], replicas))
    positions = jnp.take_along_axis(positions, shuffles, axis=1)
    listing = at_position[positions]
    first_draw = jax.random.randint(subkeys[4], (replicas, ROWS), 0, LISTED)
    second = jax.random.randint(subkeys[5], (replicas, ROWS), 0, LISTED)
    chosen = (first_draw * (second + 1) // LISTED).astype(jnp.int32)
    requests = jnp.take_along_axis(listing, chosen, axis=1)
    return (slot_of, listing.astype(jnp.int32), requests.astype(jnp.int32))


def partial_owner(length):

    def permuted(subkey):
        return permute_count(subkey, length)
    return permuted


def draw_pool_slot(key, part):
    drawn = shared_batches(key)
    return drawn[0]


def draw_variant_list(key, part):
    drawn = shared_batches(key)
    return drawn[1]


def draw_request_variant(key, part):
    drawn = shared_batches(key)
    return drawn[2]


def shard_levels(stream_key, dims, pieces, smallest, high):
    gain, own = 1.0, jax.random.fold_in(stream_key, 6)
    for position, shards_of in pieces:
        heights = jnp.exp(jax.random.uniform(jax.random.fold_in(own, position), (shards_of,), jnp.float32, smallest / len(pieces), high / len(pieces)))
        gain = gain * jnp.repeat(heights, dims[position] // shards_of).reshape([-1 if axis == position else 1 for axis in range(len(dims))])
    return gain


def scatter_about(own_key, extent, scale, reach, cuts=(), kind=jnp.bfloat16):
    result = scale * jax.random.normal(own_key, extent, jnp.float32)
    if cuts:
        result = result * shard_levels(own_key, extent, cuts, -0.22, 0.18)
    return jnp.clip(result, -reach, reach).astype(kind)


def setup_inputs(seed: int = 0, part: int = 0) -> dict:
    key_of = jax.random.split(jax.random.key(seed), 9)
    part_splits = jax.random.split(jax.random.fold_in(key_of[8], part), 9)
    return {
        "head_outputs": scatter_about(part_splits[0], (N_REP, ROWS, D), 1.0, 6.0, ((0, 4), (2, 4))),
        "residual": scatter_about(part_splits[1], (N_REP, ROWS, D), 1.0, 6.0, ((0, 4), (1, 4))),
        "projection": scatter_about(key_of[2], (D, D), D ** -0.5, 0.0625, ((0, 4),)),
        "shrink_pool": scatter_about(part_splits[3], (VARIANTS, RANK, D), D ** -0.5, 0.0625, ((0, 4), (2, 4))),
        "expand_pool": scatter_about(part_splits[4], (VARIANTS, RANK, D), (4 * RANK) ** -0.5, 0.75, ((0, 4), (2, 4))),
        "pool_slot": draw_pool_slot(jax.random.fold_in(jax.random.fold_in(key_of[8], part), 71), part),
        "variant_list": draw_variant_list(jax.random.fold_in(jax.random.fold_in(key_of[8], part), 71), part),
        "request_variant": draw_request_variant(jax.random.fold_in(jax.random.fold_in(key_of[8], part), 71), part),
    }


def reference(head_outputs, residual, projection, shrink_pool, expand_pool, pool_slot, variant_list, request_variant):
    width = projection.shape[0]
    block = width // N_TP

    def one_replica(replica):
        features = lax.dynamic_index_in_dim(head_outputs, replica, 0, keepdims=False)
        stream = lax.dynamic_index_in_dim(residual, replica, 0, keepdims=False)
        listing = lax.dynamic_index_in_dim(variant_list, replica, 0, keepdims=False)
        wanted = lax.dynamic_index_in_dim(request_variant, replica, 0, keepdims=False)

        def add_block(step, running):
            begin = (step * block).astype(jnp.int32)
            columns = lax.dynamic_slice_in_dim(features, begin, block, 1)
            weights = lax.dynamic_slice_in_dim(projection, begin, block, 0)
            product = jnp.dot(columns, weights, preferred_element_type=jnp.float32)
            rounded = lax.optimization_barrier(product.astype(jnp.bfloat16))
            return running + rounded.astype(jnp.float32)

        base = lax.fori_loop(jnp.int32(0), jnp.int32(N_TP), add_block, jnp.zeros((ROWS, width), jnp.float32))
        positions = jnp.take(pool_slot, listing, axis=0)
        shrink_rows = jnp.take(shrink_pool, positions, axis=0)
        expand_rows = jnp.take(expand_pool, positions, axis=0)
        scores = jnp.einsum("nd,lrd->nlr", features.astype(jnp.float32), shrink_rows.astype(jnp.float32), precision=lax.Precision.HIGHEST)
        member = (wanted[:, None] == listing[None, :]).astype(jnp.float32)
        shrunk = jnp.sum(scores * member[:, :, None], axis=1).astype(jnp.bfloat16)
        spread = (member[:, :, None] * shrunk[:, None, :].astype(jnp.float32)).astype(jnp.bfloat16)
        spread = spread.reshape(ROWS, LISTED * RANK)
        delta = jnp.dot(spread, expand_rows.reshape(LISTED * RANK, width), preferred_element_type=jnp.float32)
        return (stream.astype(jnp.float32) + base + delta).astype(jnp.bfloat16)

    return lax.map(one_replica, jnp.arange(N_REP, dtype=jnp.int32))
```

```python
import functools
import math

import jax
import jax.numpy as jnp
from jax import lax
from jax.experimental import pallas as pl
from jax.experimental.pallas import tpu as pltpu
from jax.sharding import PartitionSpec as P

ANY = pl.BlockSpec(memory_space=pl.ANY)
SMEM = pl.BlockSpec(memory_space=pltpu.SMEM)
VMEM = pl.BlockSpec(memory_space=pltpu.VMEM)
BF16 = jnp.bfloat16
F32 = jnp.float32


def params(mib=48):
    return pltpu.CompilerParams(vmem_limit_bytes=mib * 2**20)


def sds(shape, dtype=BF16):
    return jax.ShapeDtypeStruct(shape, dtype)


def select_kernel(cuts, n_rep, cap, pool_dev, rank, slot, lists, pos, pool, *rest):
    outs, (idx, sems) = rest[:-2], rest[-2:]
    me = pos[2]
    listed = lists.shape[1]
    copies = []
    for shift in [*range(1, n_rep), 0]:
        target = lax.rem(me + shift, n_rep)
        for k in range(cap):
            idx[shift * cap + k] = 0

        def body(l, count):
            place = slot[lists[target, l]]
            mine = (place // pool_dev == me) & (count < cap)

            @pl.when(mine)
            def _():
                idx[shift * cap + count] = place - me * pool_dev

            return count + mine.astype(jnp.int32)

        lax.fori_loop(0, listed, body, jnp.int32(0), unroll=True)
        for k in range(cap):
            entry = pl.multiple_of(idx[shift * cap + k] * rank, rank)
            for c, (start, stop) in enumerate(cuts):
                copy = pltpu.make_async_copy(
                    pool.at[pl.ds(entry, rank), pl.ds(start, stop - start)],
                    outs[shift * len(cuts) + c].at[pl.ds(k * rank, rank), :],
                    sems.at[(shift * cap + k) * len(cuts) + c],
                )
                copy.start()
                copies.append(copy)
    for copy in copies:
        copy.wait()


def select(slot, lists, pos, pool, cuts, n_rep, cap):
    pool_dev, rank, width = pool.shape
    shapes = [sds((cap * rank, stop - start)) for _ in range(n_rep) for start, stop in cuts]
    return pl.pallas_call(
        functools.partial(select_kernel, cuts, n_rep, cap, pool_dev, rank),
        out_shape=shapes,
        in_specs=[SMEM, SMEM, SMEM, ANY],
        out_specs=[ANY] * len(shapes),
        scratch_shapes=[
            pltpu.SMEM((n_rep * cap,), jnp.int32),
            pltpu.SemaphoreType.DMA((n_rep * cap * len(cuts),)),
        ],
        name="select",
    )(slot, lists, pos, pool.reshape(pool_dev * rank, width))


def gate_kernel(n, *refs):
    pass


def gate(arrays, after):
    n = len(arrays)
    return pl.pallas_call(
        functools.partial(gate_kernel, n),
        out_shape=[sds(a.shape, a.dtype) for a in arrays],
        in_specs=[ANY] * (n + len(after)),
        out_specs=[ANY] * n,
        input_output_aliases={i: i for i in range(n)},
        name="gate",
    )(*arrays, *after)


def product_kernel(split, pos, features, weights, keep, send):
    own = features.shape[0] // 2
    result = jnp.dot(features[...], weights[...], preferred_element_type=F32).astype(BF16)
    low, high = result[:own], result[own:]
    if split:
        low, high = low[None], high[None]

    @pl.when(pos[1] == 0)
    def _():
        keep[...] = low
        send[...] = high

    @pl.when(pos[1] == 1)
    def _():
        keep[...] = high
        send[...] = low


def product(pos, features, projection, other_rows, other_cols, first, count, tile, blocks, after=()):
    rows, depth = features.shape
    width = projection.shape[1]
    half = rows // 2
    own = half // 2
    tiles = count // tile

    def row_block(j, pos):
        return ((1 - pos[0]) if other_rows else pos[0], 0)

    def col_block(j, pos):
        if other_cols is None:
            return (0, j + first // tile)
        chip = (1 - pos[0]) if other_cols else pos[0]
        return (0, chip * (width // 2 // tile) + j + first // tile)

    if blocks > 1:
        per = tiles // blocks
        shape = (blocks, own, count // blocks)
        out_spec = pl.BlockSpec((1, own, tile), lambda j, pos: (j // per, 0, j % per))
    else:
        shape = (own, count)
        out_spec = pl.BlockSpec((own, tile), lambda j, pos: (0, j))
    body = functools.partial(product_kernel, blocks > 1)

    def kernel(pos, features, weights, *rest):
        body(pos, features, weights, *rest[-2:])

    return pl.pallas_call(
        kernel,
        out_shape=[sds(shape)] * 2,
        grid_spec=pltpu.PrefetchScalarGridSpec(
            num_scalar_prefetch=1,
            grid=(tiles,),
            in_specs=[pl.BlockSpec((half, depth), row_block), pl.BlockSpec((depth, tile), col_block)]
            + [ANY] * len(after),
            out_specs=[out_spec] * 2,
        ),
        compiler_params=params(),
        cost_estimate=pl.CostEstimate(
            flops=2 * half * depth * count, bytes_accessed=2 * depth * count, transcendentals=0
        ),
        name="product",
    )(pos, features, projection, *after)


def walk_list(slot, lists, me, n_rep, cap, pool_dev, counts, visit):
    for s in range(n_rep):
        counts[s] = 0

    for l in range(lists.shape[1]):
        variant = lists[me, l]
        owner = slot[variant] // pool_dev
        shift = lax.rem(me - owner + n_rep, n_rep)
        k = counts[shift]
        counts[shift] = k + 1
        visit(variant, shift * cap + jnp.minimum(k, cap - 1))


def score_kernel(n_rep, cap, pool_dev, rank, slot, lists, pos, wanted, features, *rest):
    blocks, (out, scores, counts) = rest[:n_rep], rest[n_rep:]
    size = cap * rank
    for s in range(n_rep):
        scores[pl.ds(s * size, size), :] = lax.dot_general(
            blocks[s][...], features[...], (((1,), (1,)), ((), ())), preferred_element_type=F32
        )
    out[...] = jnp.zeros_like(out)

    def visit(variant, place):
        offset = pl.multiple_of(place * rank, rank)
        out[...] += jnp.where(wanted[...] == variant, scores[pl.ds(offset, rank), :], 0.0)

    walk_list(slot, lists, pos[2], n_rep, cap, pool_dev, counts, visit)


def score(slot, lists, pos, wanted, features, blocks, cap, pool_dev, rank):
    n_rep = len(blocks)
    rows = features.shape[0]
    return pl.pallas_call(
        functools.partial(score_kernel, n_rep, cap, pool_dev, rank),
        out_shape=sds((rank, rows), F32),
        in_specs=[SMEM] * 3 + [VMEM] * (2 + n_rep),
        out_specs=VMEM,
        scratch_shapes=[
            pltpu.VMEM((n_rep * cap * rank, rows), F32),
            pltpu.SMEM((n_rep,), jnp.int32),
        ],
        compiler_params=params(),
        name="score",
    )(slot, lists, pos, wanted, features, *blocks)


def delta_kernel(n_rep, cap, pool_dev, rank, slot, lists, pos, wanted, shrunk, *rest):
    blocks, (keep, send, spread, expand, result, variants, counts) = rest[:n_rep], rest[n_rep:]
    size = cap * rank
    own = keep.shape[1]
    for i in range(n_rep * cap):
        variants[i] = -1

    def visit(variant, place):
        variants[place] = variant

    walk_list(slot, lists, pos[2], n_rep, cap, pool_dev, counts, visit)
    total = jnp.sum(shrunk[...], axis=0).astype(BF16).astype(F32)
    for i in range(n_rep * cap):
        spread[pl.ds(i * rank, rank), :] = jnp.where(wanted[...] == variants[i], total, 0.0).astype(BF16)
    for s in range(n_rep):
        expand[pl.ds(s * size, size), :] = blocks[s][...]
    result[...] = lax.dot_general(
        spread[...], expand[...], (((0,), (0,)), ((), ())), preferred_element_type=F32
    )
    chip, core = pos[0], pos[1]
    for i, y in enumerate((1 - chip, chip)):
        keep[i] = result[pl.ds((2 * y + core) * own, own), :].astype(BF16)
        send[i] = result[pl.ds((2 * y + 1 - core) * own, own), :].astype(BF16)


def delta(slot, lists, pos, wanted, shrunk, blocks, cap, pool_dev, rank, own):
    n_rep = len(blocks)
    rows = wanted.shape[1]
    width = blocks[0].shape[1]
    return pl.pallas_call(
        functools.partial(delta_kernel, n_rep, cap, pool_dev, rank),
        out_shape=[sds((2, own, width))] * 2,
        in_specs=[SMEM] * 3 + [VMEM] * (2 + n_rep),
        out_specs=[VMEM] * 2,
        scratch_shapes=[
            pltpu.VMEM((n_rep * cap * rank, rows), BF16),
            pltpu.VMEM((n_rep * cap * rank, width), BF16),
            pltpu.VMEM((rows, width), F32),
            pltpu.SMEM((n_rep * cap,), jnp.int32),
            pltpu.SMEM((n_rep,), jnp.int32),
        ],
        compiler_params=params(),
        name="delta",
    )(slot, lists, pos, wanted, shrunk, *blocks)


def near_kernel(pos, residual, keep, recv, first, second, mine, theirs, *rest):
    out = rest[-1]
    block = pl.program_id(0)
    total = residual[...].astype(F32) + keep[...].astype(F32) + recv[...].astype(F32)
    total += jnp.where(block == 0, first[...], second[...]).astype(F32)
    total += jnp.where(block == pos[1], mine[0], theirs[0]).astype(F32)
    out[...] = total.astype(BF16)


def far_kernel(pos, residual, keep, recv, piece, *rest):
    out = rest[-1]
    total = residual[...].astype(F32) + keep[...].astype(F32) + recv[...].astype(F32)
    out[...] = (total + piece[0].astype(F32)).astype(BF16)


def finish(pos, out, residual, keep, recv, start, stop, near, pieces):
    own, full = residual.shape
    width = full // 4
    size = stop - start
    tile = math.gcd(size, start, width)

    def place(b, j, pos):
        chip = pos[0] if near else 1 - pos[0]
        return (0, (2 * chip + b) * (width // tile) + start // tile + j)

    whole = pl.BlockSpec((own, tile), place)
    if near:
        first = pl.BlockSpec((own, tile), lambda b, j, pos: (0, start // tile + j))
        second = pl.BlockSpec((1, own, tile), lambda b, j, pos: (1, 0, j))
        specs, kernel = [first, first, second, second], near_kernel
    else:
        specs, kernel = [pl.BlockSpec((1, own, tile), lambda b, j, pos: (b, 0, j))], far_kernel
    operands = [pos, residual, keep, recv, *pieces]
    aliases = {}
    if out is not None:
        specs = specs + [ANY]
        aliases = {len(operands): 0}
        operands.append(out)
    return pl.pallas_call(
        kernel,
        out_shape=sds((own, full)),
        grid_spec=pltpu.PrefetchScalarGridSpec(
            num_scalar_prefetch=1,
            grid=(2, size // tile),
            in_specs=[whole] * 3 + specs,
            out_specs=whole,
        ),
        input_output_aliases=aliases,
        compiler_params=params(),
        cost_estimate=pl.CostEstimate(flops=own * size * 8, bytes_accessed=own * size * 20, transcendentals=0),
        name="near" if near else "far",
    )(*operands)


def paired(
    head_outputs, residual, projection, shrink_pool, expand_pool, pool_slot, variant_list, request_variant
):
    n_rep = lax.axis_size("rep")
    index = lax.axis_index("tp")
    chip, core = index // 2, index % 2
    pos = jnp.stack([chip, core, lax.axis_index("rep")]).astype(jnp.int32)
    features = head_outputs[0]
    rows = features.shape[0]
    own = rows // 4
    pool_dev, rank, width = shrink_pool.shape
    cap = pool_dev // 4 + 2
    stream = residual[0]
    lists = (pool_slot, variant_list, pos)
    sizes = (cap, pool_dev, rank)
    cuts = tuple((width * a // 8, width * b // 8) for a, b in ((0, 3), (3, 6), (6, 8)))
    tile = min(512, width)

    def over_core(x):
        return lax.ppermute(x, "tp", [(0, 1), (1, 0), (2, 3), (3, 2)])

    def over_chip(x):
        return lax.ppermute(x, "tp", [(0, 2), (2, 0), (1, 3), (3, 1)])

    def over_rep(x, shift):
        return lax.ppermute(x, "rep", [(i, (i + shift) % n_rep) for i in range(n_rep)])

    shifts = [s for s in range(1, n_rep) if s != n_rep // 2] + [n_rep // 2]
    chosen = select(*lists, shrink_pool, ((0, width),), n_rep, cap)
    shrink = [chosen[0]] + [None] * (n_rep - 1)
    for s in shifts:
        shrink[s] = over_rep(chosen[s], s)
    chosen_expand = select(*lists, expand_pool, cuts, n_rep, cap)

    early = []
    for b in range(2):
        keep, send = product(pos, features, projection, True, True, b * width, width, tile, 1)
        early.append(over_chip(keep + over_core(send)))
    keep, send = product(pos, features, projection, True, False, 0, 2 * width, tile, 2)
    late = keep + over_core(send)
    base_keep, base_send = product(pos, features, projection, False, None, 0, 4 * width, tile, 1)
    base_recv = over_core(base_send)

    part = score(*lists, request_variant, features, shrink, *sizes)
    shrunk = lax.all_gather(part, "tp")

    done = shrink[1:]
    expands = []
    for c in range(len(cuts)):
        sends = gate([chosen_expand[s * len(cuts) + c] for s in shifts], done)
        block = [chosen_expand[c]] + [None] * (n_rep - 1)
        for s, x in zip(shifts, sends):
            block[s] = over_rep(x, s)
        done = block[1:]
        expands.append(block)

    out = None
    far = []
    for c, (start, stop) in enumerate(cuts):
        mine, send = delta(*lists, request_variant, shrunk, expands[c], *sizes, own)
        theirs = over_core(send)
        first = jnp.where(core == 0, mine[0], theirs[0])
        second = jnp.where(core == 0, theirs[0], mine[0])
        far.append(over_chip(late[:, :, start:stop] + jnp.stack([first, second])))
        out = finish(pos, out, stream, base_keep, base_recv, start, stop, True, [*early, mine, theirs])
    for c, (start, stop) in enumerate(cuts):
        out = finish(pos, out, stream, base_keep, base_recv, start, stop, False, [far[c]])
    return out[None]


def general(
    head_outputs, residual, projection, shrink_pool, expand_pool, pool_slot, variant_list, request_variant
):
    split_count = lax.axis_size("tp")
    split_index = lax.axis_index("tp")
    replica_index = lax.axis_index("rep")
    row_count = head_outputs.shape[1]
    local_width = head_outputs.shape[2]
    rank_size = shrink_pool.shape[1]
    listed = variant_list.shape[1]
    own_rows = row_count // split_count
    flat_size = rank_size * local_width
    features = head_outputs[0]
    wanted = request_variant[0]
    my_list = lax.dynamic_index_in_dim(variant_list, replica_index, 0, keepdims=False)
    my_positions = jnp.take(pool_slot, my_list, axis=0)
    pieces = (
        lax.all_gather(shrink_pool, "rep", axis=0, tiled=True),
        lax.all_gather(expand_pool, "rep", axis=0, tiled=True),
    )
    piece_rows = pieces[0].shape[0]
    matches = (my_positions[:, None] == jnp.arange(piece_rows, dtype=jnp.int32)[None, :]).astype(BF16)
    shrink_sel = jnp.dot(matches, pieces[0].reshape(piece_rows, flat_size), preferred_element_type=F32)
    expand_sel = jnp.dot(matches, pieces[1].reshape(piece_rows, flat_size), preferred_element_type=F32)
    shrink_sel = shrink_sel.astype(BF16).reshape(listed * rank_size, local_width)
    expand_sel = expand_sel.astype(BF16).reshape(listed, rank_size, local_width)
    member = wanted[:, None] == my_list[None, :]
    scores = lax.dot_general(
        features, shrink_sel, (((1,), (1,)), ((), ())), preferred_element_type=F32
    )
    shrunk = jnp.sum(scores.reshape(row_count, listed, rank_size) * member[:, :, None], axis=1)
    own_shrunk = lax.psum_scatter(shrunk.astype(BF16), "tp", scatter_dimension=0, tiled=True)
    own_member = lax.dynamic_slice_in_dim(member, split_index * own_rows, own_rows, 0)
    spread = own_member[:, :, None] * own_shrunk[:, None, :]
    spread = spread.reshape(own_rows, listed * rank_size)
    piece = lax.all_gather(expand_sel, "tp", axis=2, tiled=True)
    delta_rows = jnp.dot(
        spread, piece.reshape(listed * rank_size, piece.shape[2]), preferred_element_type=F32
    )
    base_rows = lax.psum_scatter(
        jnp.dot(features, projection, preferred_element_type=F32).astype(BF16),
        "tp",
        scatter_dimension=0,
        tiled=True,
    ).astype(F32)
    return (residual[0].astype(F32) + base_rows + delta_rows).astype(BF16)[None]


def solution(mesh):
    in_specs = (
        P(("groups", "rep"), None, "tp"),
        P(("groups", "rep"), "tp", None),
        P("tp", None),
        P(("groups", "rep"), None, "tp"),
        P(("groups", "rep"), None, "tp"),
        P("groups"),
        P("groups", None),
        P(("groups", "rep"), None),
    )
    out_specs = P(("groups", "rep"), "tp", None)
    local = paired if mesh.shape["tp"] == 4 else general
    return jax.shard_map(local, mesh=mesh, in_specs=in_specs, out_specs=out_specs, check_vma=False)
```

```python
import functools
import math

import jax
import jax.numpy as jnp
from jax import lax
from jax.experimental import pallas as pl
from jax.experimental.pallas import tpu as pltpu
from jax.sharding import PartitionSpec as P

ANY = pl.BlockSpec(memory_space=pl.ANY)
HBM = pl.BlockSpec(memory_space=pltpu.HBM)
SMEM = pl.BlockSpec(memory_space=pltpu.SMEM)
VMEM = pl.BlockSpec(memory_space=pltpu.VMEM)
BF16 = jnp.bfloat16
F32 = jnp.float32


def order(us):
    return pl.CostEstimate(flops=int(us * 1.15e9) + 1, bytes_accessed=1, transcendentals=0)


def params(mib=48):
    return pltpu.CompilerParams(vmem_limit_bytes=mib * 2**20)


def sds(shape, dtype=BF16):
    return jax.ShapeDtypeStruct(shape, dtype)


TOKEN = sds((8, 128), F32)


def select_kernel(cuts, by_target, n_rep, cap, pool_dev, rank, slot, lists, pos, pool, *rest):
    n_outs = len(cuts) if by_target else n_rep * len(cuts)
    outs, (token, idx, sems) = rest[-3 - n_outs : -3], rest[-3:]
    token[...] = jnp.zeros_like(token)
    me = pos[2]
    listed = lists.shape[1]
    copies = []
    for shift in range(n_rep):
        target = shift if by_target else lax.rem(me + shift, n_rep)
        for k in range(cap):
            idx[shift * cap + k] = 0

        def body(l, count):
            place = slot[lists[target, l]]
            mine = (place // pool_dev == me) & (count < cap)

            @pl.when(mine)
            def _():
                idx[shift * cap + count] = place - me * pool_dev

            return count + mine.astype(jnp.int32)

        lax.fori_loop(0, listed, body, jnp.int32(0), unroll=True)
        for k in range(cap):
            entry = pl.multiple_of(idx[shift * cap + k] * rank, rank)
            for c, (start, stop) in enumerate(cuts):
                if by_target:
                    into = outs[c].at[shift, pl.ds(k * rank, rank), :]
                else:
                    into = outs[shift * len(cuts) + c].at[pl.ds(k * rank, rank), :]
                copy = pltpu.make_async_copy(
                    pool.at[pl.ds(entry, rank), pl.ds(start, stop - start)],
                    into,
                    sems.at[(shift * cap + k) * len(cuts) + c],
                )
                copy.start()
                copies.append(copy)
    for copy in copies:
        copy.wait()


def select(slot, lists, pos, pool, cuts, by_target, n_rep, cap, after=()):
    pool_dev, rank, width = pool.shape
    if by_target:
        shapes = [sds((n_rep, cap * rank, stop - start)) for start, stop in cuts]
    else:
        shapes = [sds((cap * rank, stop - start)) for _ in range(n_rep) for start, stop in cuts]
    return pl.pallas_call(
        functools.partial(select_kernel, cuts, by_target, n_rep, cap, pool_dev, rank),
        out_shape=[*shapes, TOKEN],
        in_specs=[SMEM, SMEM, SMEM, ANY] + [ANY] * len(after),
        out_specs=[HBM] * len(shapes) + [VMEM],
        scratch_shapes=[
            pltpu.SMEM((n_rep * cap,), jnp.int32),
            pltpu.SemaphoreType.DMA((n_rep * cap * len(cuts),)),
        ],
        cost_estimate=order(0),
        name="select",
    )(slot, lists, pos, pool.reshape(pool_dev * rank, width), *after)


def product_columns_kernel(pos, features, weights, out, token):
    token[...] = jnp.zeros_like(token)
    out[...] = jnp.dot(features[...], weights[...], preferred_element_type=F32).astype(BF16)[None]


def product_columns(pos, features, projection, tile, after=()):
    rows, depth = features.shape
    width = projection.shape[1]
    half = rows // 2
    per = width // 4 // tile
    return pl.pallas_call(
        lambda pos, features, weights, *rest: product_columns_kernel(pos, features, weights, *rest[-2:]),
        out_shape=[sds((2, half, width // 4)), TOKEN],
        grid_spec=pltpu.PrefetchScalarGridSpec(
            num_scalar_prefetch=1,
            grid=(2 * per,),
            in_specs=[
                pl.BlockSpec((half, depth), lambda j, pos: (1 - pos[0], 0)),
                pl.BlockSpec(
                    (depth, tile),
                    lambda j, pos: (
                        0,
                        (2 * pos[0] + jnp.where(j < per, pos[1], 1 - pos[1])) * per + lax.rem(j, per),
                    ),
                ),
            ]
            + [ANY] * len(after),
            out_specs=[
                pl.BlockSpec((1, half, tile), lambda j, pos: (j // per, 0, j % per)),
                pl.BlockSpec((8, 128), lambda j, pos: (0, 0)),
            ],
        ),
        compiler_params=params(),
        cost_estimate=order(0),
        name="product",
    )(pos, features, projection, *after)


def product_kernel(split, pos, features, weights, keep, send, token):
    token[...] = jnp.zeros_like(token)
    own = features.shape[0] // 2
    result = jnp.dot(features[...], weights[...], preferred_element_type=F32).astype(BF16)
    low, high = result[:own], result[own:]
    if split:
        low, high = low[None], high[None]

    @pl.when(pos[1] == 0)
    def _():
        keep[...] = low
        send[...] = high

    @pl.when(pos[1] == 1)
    def _():
        keep[...] = high
        send[...] = low


def product(pos, features, projection, other_rows, other_cols, first, count, tile, blocks, after=()):
    rows, depth = features.shape
    width = projection.shape[1]
    half = rows // 2
    own = half // 2
    tiles = count // tile

    def row_block(j, pos):
        return ((1 - pos[0]) if other_rows else pos[0], 0)

    def col_block(j, pos):
        if other_cols is None:
            return (0, j + first // tile)
        chip = (1 - pos[0]) if other_cols else pos[0]
        return (0, chip * (width // 2 // tile) + j + first // tile)

    if blocks > 1:
        per = tiles // blocks
        shape = (blocks, own, count // blocks)
        out_spec = pl.BlockSpec((1, own, tile), lambda j, pos: (j // per, 0, j % per))
    else:
        shape = (own, count)
        out_spec = pl.BlockSpec((own, tile), lambda j, pos: (0, j))
    body = functools.partial(product_kernel, blocks > 1)

    def kernel(pos, features, weights, *rest):
        body(pos, features, weights, *rest[-3:])

    return pl.pallas_call(
        kernel,
        out_shape=[sds(shape), sds(shape), TOKEN],
        grid_spec=pltpu.PrefetchScalarGridSpec(
            num_scalar_prefetch=1,
            grid=(tiles,),
            in_specs=[pl.BlockSpec((half, depth), row_block), pl.BlockSpec((depth, tile), col_block)]
            + [ANY] * len(after),
            out_specs=[out_spec] * 2 + [pl.BlockSpec((8, 128), lambda j, pos: (0, 0))],
        ),
        compiler_params=params(),
        cost_estimate=order(0),
        name="product",
    )(pos, features, projection, *after)


def walk_list(slot, lists, me, n_rep, cap, pool_dev, counts, by_owner, visit):
    for s in range(n_rep):
        counts[s] = 0

    for l in range(lists.shape[1]):
        variant = lists[me, l]
        owner = slot[variant] // pool_dev
        group = owner if by_owner else lax.rem(me - owner + n_rep, n_rep)
        k = counts[group]
        counts[group] = k + 1
        visit(variant, group * cap + jnp.minimum(k, cap - 1))


def score_kernel(n_rep, cap, pool_dev, rank, slot, lists, pos, wanted, features, factors, *rest):
    out, scores, counts = rest[-3:]
    scores[...] = lax.dot_general(
        factors[...], features[...], (((1,), (1,)), ((), ())), preferred_element_type=F32
    )
    out[...] = jnp.zeros_like(out)

    def visit(variant, place):
        offset = pl.multiple_of(place * rank, rank)
        out[...] += jnp.where(wanted[...] == variant, scores[pl.ds(offset, rank), :], 0.0)

    walk_list(slot, lists, pos[2], n_rep, cap, pool_dev, counts, True, visit)


def score(slot, lists, pos, wanted, features, factors, n_rep, cap, pool_dev, rank, after=()):
    rows = features.shape[0]
    return pl.pallas_call(
        functools.partial(score_kernel, n_rep, cap, pool_dev, rank),
        out_shape=sds((rank, rows), F32),
        in_specs=[SMEM] * 3 + [VMEM] * 3 + [ANY] * len(after),
        out_specs=VMEM,
        scratch_shapes=[
            pltpu.VMEM((n_rep * cap * rank, rows), F32),
            pltpu.SMEM((n_rep,), jnp.int32),
        ],
        compiler_params=params(),
        cost_estimate=order(15),
        name="score",
    )(slot, lists, pos, wanted, features, factors, *after)


def delta_kernel(
    n_blocks, n_rep, cap, pool_dev, rank, n_before, slot, lists, pos, wanted, shrunk, late_own, late_recv, *rest
):
    blocks, before = rest[:n_blocks], rest[n_blocks : n_blocks + n_before]
    straight, cross, mine, send, spread, expand, result, variants, counts = rest[-9:]
    size = n_rep * cap * rank // n_blocks
    own, width = straight.shape
    for i in range(n_rep * cap):
        variants[i] = -1

    def visit(variant, place):
        variants[place] = variant

    walk_list(slot, lists, pos[2], n_rep, cap, pool_dev, counts, n_blocks == 1, visit)
    total = jnp.sum(shrunk[...], axis=0).astype(BF16).astype(F32)
    for i in range(n_rep * cap):
        spread[pl.ds(i * rank, rank), :] = jnp.where(wanted[...] == variants[i], total, 0.0).astype(BF16)
    for s in range(n_blocks):
        expand[pl.ds(s * size, size), :] = blocks[s][...]
    result[...] = lax.dot_general(
        spread[...], expand[...], (((0,), (0,)), ((), ())), preferred_element_type=F32
    )
    chip, core = pos[0], pos[1]
    for out, c in ((straight, core), (cross, 1 - core)):
        rows = pl.ds(pl.multiple_of(c * own, own), own)
        base = late_own[rows, :].astype(F32) + late_recv[rows, :].astype(F32)
        out[...] = (base + result[pl.ds((2 - 2 * chip + c) * own, own), :]).astype(BF16)
    start = mine.shape[1] - width
    if before:
        mine[:, :start] = before[0][...]
        send[:, :start] = before[1][...]
    mine[:, start:] = result[pl.ds((2 * chip + core) * own, own), :].astype(BF16)
    send[:, start:] = result[pl.ds((2 * chip + 1 - core) * own, own), :].astype(BF16)


def delta(slot, lists, pos, wanted, shrunk, late, blocks, cut, n_rep, cap, pool_dev, rank, own, before=(), after=()):
    rows = wanted.shape[1]
    start, stop = cut
    width = stop - start
    late_own, late_recv = late
    return pl.pallas_call(
        functools.partial(delta_kernel, len(blocks), n_rep, cap, pool_dev, rank, len(before)),
        out_shape=[sds((own, width))] * 2 + [sds((own, stop))] * 2,
        in_specs=[SMEM] * 3 + [VMEM] * (4 + len(blocks) + len(before)) + [ANY] * len(after),
        out_specs=[VMEM] * 4,
        scratch_shapes=[
            pltpu.VMEM((n_rep * cap * rank, rows), BF16),
            pltpu.VMEM((n_rep * cap * rank, width), BF16),
            pltpu.VMEM((rows, width), F32),
            pltpu.SMEM((n_rep * cap,), jnp.int32),
            pltpu.SMEM((n_rep,), jnp.int32),
        ],
        compiler_params=params(),
        cost_estimate=order(0),
        name="delta",
    )(
        slot, lists, pos, wanted, shrunk, late_own[:, start:stop], late_recv[:, start:stop], *blocks, *before, *after
    )


def gate_kernel(*refs):
    pass


def gate(arrays, after):
    n = len(arrays)
    return pl.pallas_call(
        gate_kernel,
        out_shape=[sds(x.shape, x.dtype) for x in arrays],
        in_specs=[ANY] * (n + len(after)),
        out_specs=[ANY] * n,
        input_output_aliases={i: i for i in range(n)},
        cost_estimate=order(100),
        name="gate",
    )(*arrays, *after)


def near_kernel(pos, residual, keep, recv, first, mine, theirs, *rest):
    out = rest[-1]
    total = residual[...].astype(F32) + keep[...].astype(F32) + recv[...].astype(F32)
    total += first[0].astype(F32)
    total += jnp.where(pl.program_id(0) == pos[1], mine[...], theirs[...]).astype(F32)
    out[...] = total.astype(BF16)


def far_kernel(pos, residual, keep, recv, straight, cross, *rest):
    out = rest[-1]
    total = residual[...].astype(F32) + keep[...].astype(F32) + recv[...].astype(F32)
    total += jnp.where(pl.program_id(0) == pos[1], straight[...], cross[...]).astype(F32)
    out[...] = total.astype(BF16)


def finish(pos, out, residual, base, start, stop, near, pieces, after=()):
    own, full = residual.shape
    width = full // 4
    size = stop - start
    tile = min(1024, math.gcd(size, start, width))

    def place(b, j, pos):
        chip = pos[0] if near else 1 - pos[0]
        return (0, (2 * chip + b) * (width // tile) + start // tile + j)

    whole = pl.BlockSpec((own, tile), place)
    piece = pl.BlockSpec((own, tile), lambda b, j, pos: (0, j))
    if near:
        first = pl.BlockSpec((1, own, tile), lambda b, j, pos: (b, 0, start // tile + j))
        specs, kernel = [first, piece, piece], near_kernel
    else:
        specs, kernel = [piece, piece], far_kernel
    specs = specs + [ANY] * len(after)
    operands = [pos, residual, *base, *pieces, *after]
    aliases = {}
    if out is not None:
        specs = specs + [ANY]
        aliases = {len(operands): 0}
        operands.append(out)
    return pl.pallas_call(
        kernel,
        out_shape=sds((own, full)),
        grid_spec=pltpu.PrefetchScalarGridSpec(
            num_scalar_prefetch=1,
            grid=(2, size // tile),
            in_specs=[whole] * 3 + specs,
            out_specs=whole,
        ),
        input_output_aliases=aliases,
        compiler_params=params(),
        cost_estimate=order(60),
        name="near" if near else "far",
    )(*operands)


def paired(
    head_outputs, residual, projection, shrink_pool, expand_pool, pool_slot, variant_list, request_variant
):
    n_rep = lax.axis_size("rep")
    index = lax.axis_index("tp")
    chip, core = index // 2, index % 2
    pos = jnp.stack([chip, core, lax.axis_index("rep")]).astype(jnp.int32)
    features = head_outputs[0]
    rows = features.shape[0]
    own = rows // 4
    pool_dev, rank, width = shrink_pool.shape
    cap = pool_dev // 4 + 2
    stream = residual[0]
    lists = (pool_slot, variant_list, pos)
    sizes = (cap, pool_dev, rank)
    tile = min(512, width)
    cut = width // 2
    cuts = ((0, cut), (cut, width))

    def over_core(x):
        return lax.ppermute(x, "tp", [(0, 1), (1, 0), (2, 3), (3, 2)])

    def over_chip(x):
        return lax.ppermute(x, "tp", [(0, 2), (2, 0), (1, 3), (3, 1)])

    def over_both(x):
        return lax.ppermute(x, "tp", [(0, 3), (3, 0), (1, 2), (2, 1)])

    def over_rep(x, shift):
        return lax.ppermute(x, "rep", [(i, (i + shift) % n_rep) for i in range(n_rep)])

    shifts = [s for s in range(1, n_rep) if s != n_rep // 2] + [n_rep // 2]
    chosen, token = select(*lists, shrink_pool, ((0, width),), True, n_rep, cap)
    shrink = lax.all_to_all(chosen, "rep", 0, 0, tiled=True).reshape(n_rep * cap * rank, width)

    keep, send, token = product(pos, features, projection, True, True, 0, 2 * width, tile, 2, [token])
    early = keep + over_core(send)
    early_recv = over_chip(early)

    *chosen, token = select(*lists, expand_pool, cuts[:1], False, n_rep, cap, [token])
    first = [chosen[0]] + [None] * (n_rep - 1)
    for s in shifts:
        first[s] = over_rep(chosen[s], s)
    chosen, token = select(*lists, expand_pool, cuts[1:], True, n_rep, cap, [token])
    second = lax.all_to_all(chosen, "rep", 0, 0, tiled=True).reshape(n_rep * cap * rank, cut)

    both, token = product_columns(pos, features, projection, tile, [early, token])
    late = (both[0], over_core(both[1]))
    keep, send, token = product(pos, features, projection, False, None, 0, 4 * width, tile, 1, [token])
    base = (keep, over_core(send))

    part = score(*lists, request_variant, features, shrink, n_rep, *sizes, [token])
    shrunk = lax.all_gather(part, "tp")

    common = (*lists, request_variant, shrunk, late)
    straight, cross, *before = delta(*common, first, cuts[0], n_rep, *sizes, own, (), [early_recv])
    far = [over_chip(straight), over_both(cross)]
    straight, cross, mine, send = delta(*common, [second], cuts[1], n_rep, *sizes, own, before)
    last = [over_chip(straight), over_both(cross)]
    theirs = over_core(send)
    far = gate(far, [mine])
    out = finish(pos, None, stream, base, 0, width, True, [early_recv, mine, theirs], far)
    out = finish(pos, out, stream, base, *cuts[0], False, far)
    out = finish(pos, out, stream, base, *cuts[1], False, last)
    return out[None]


def general(
    head_outputs, residual, projection, shrink_pool, expand_pool, pool_slot, variant_list, request_variant
):
    split_count = lax.axis_size("tp")
    split_index = lax.axis_index("tp")
    replica_index = lax.axis_index("rep")
    row_count = head_outputs.shape[1]
    local_width = head_outputs.shape[2]
    rank_size = shrink_pool.shape[1]
    listed = variant_list.shape[1]
    own_rows = row_count // split_count
    flat_size = rank_size * local_width
    features = head_outputs[0]
    wanted = request_variant[0]
    my_list = lax.dynamic_index_in_dim(variant_list, replica_index, 0, keepdims=False)
    my_positions = jnp.take(pool_slot, my_list, axis=0)
    pieces = (
        lax.all_gather(shrink_pool, "rep", axis=0, tiled=True),
        lax.all_gather(expand_pool, "rep", axis=0, tiled=True),
    )
    piece_rows = pieces[0].shape[0]
    matches = (my_positions[:, None] == jnp.arange(piece_rows, dtype=jnp.int32)[None, :]).astype(BF16)
    shrink_sel = jnp.dot(matches, pieces[0].reshape(piece_rows, flat_size), preferred_element_type=F32)
    expand_sel = jnp.dot(matches, pieces[1].reshape(piece_rows, flat_size), preferred_element_type=F32)
    shrink_sel = shrink_sel.astype(BF16).reshape(listed * rank_size, local_width)
    expand_sel = expand_sel.astype(BF16).reshape(listed, rank_size, local_width)
    member = wanted[:, None] == my_list[None, :]
    scores = lax.dot_general(
        features, shrink_sel, (((1,), (1,)), ((), ())), preferred_element_type=F32
    )
    shrunk = jnp.sum(scores.reshape(row_count, listed, rank_size) * member[:, :, None], axis=1)
    own_shrunk = lax.psum_scatter(shrunk.astype(BF16), "tp", scatter_dimension=0, tiled=True)
    own_member = lax.dynamic_slice_in_dim(member, split_index * own_rows, own_rows, 0)
    spread = own_member[:, :, None] * own_shrunk[:, None, :]
    spread = spread.reshape(own_rows, listed * rank_size)
    piece = lax.all_gather(expand_sel, "tp", axis=2, tiled=True)
    delta_rows = jnp.dot(
        spread, piece.reshape(listed * rank_size, piece.shape[2]), preferred_element_type=F32
    )
    base_rows = lax.psum_scatter(
        jnp.dot(features, projection, preferred_element_type=F32).astype(BF16),
        "tp",
        scatter_dimension=0,
        tiled=True,
    ).astype(F32)
    return (residual[0].astype(F32) + base_rows + delta_rows).astype(BF16)[None]


def solution(mesh):
    in_specs = (
        P(("groups", "rep"), None, "tp"),
        P(("groups", "rep"), "tp", None),
        P("tp", None),
        P(("groups", "rep"), None, "tp"),
        P(("groups", "rep"), None, "tp"),
        P("groups"),
        P("groups", None),
        P(("groups", "rep"), None),
    )
    out_specs = P(("groups", "rep"), "tp", None)
    local = paired if mesh.shape["tp"] == 4 else general
    return jax.shard_map(local, mesh=mesh, in_specs=in_specs, out_specs=out_specs, check_vma=False)
```

```python
import functools
import math

import jax
import jax.numpy as jnp
from jax import lax
from jax.experimental import pallas as pl
from jax.experimental.pallas import tpu as pltpu
from jax.sharding import PartitionSpec as P

ANY = pl.BlockSpec(memory_space=pl.ANY)
HBM = pl.BlockSpec(memory_space=pltpu.HBM)
SMEM = pl.BlockSpec(memory_space=pltpu.SMEM)
VMEM = pl.BlockSpec(memory_space=pltpu.VMEM)
BF16 = jnp.bfloat16
F32 = jnp.float32


def order(us):
    return pl.CostEstimate(flops=int(us * 1.15e9) + 1, bytes_accessed=1, transcendentals=0)


def params(mib=48):
    return pltpu.CompilerParams(vmem_limit_bytes=mib * 2**20)


def sds(shape, dtype=BF16):
    return jax.ShapeDtypeStruct(shape, dtype)


TOKEN = sds((8, 128), F32)


def select_kernel(cuts, by_target, n_rep, cap, pool_dev, rank, slot, lists, pos, pool, *rest):
    n_outs = len(cuts) if by_target else n_rep * len(cuts)
    outs, (token, idx) = rest[-2 - n_outs : -2], rest[-2:]
    token[...] = jnp.zeros_like(token)
    me = pos[2]
    listed = lists.shape[1]
    for shift in range(n_rep):
        target = shift if by_target else lax.rem(me + shift, n_rep)
        for k in range(cap):
            idx[k] = 0

        def body(l, count):
            place = slot[lists[target, l]]
            mine = (place // pool_dev == me) & (count < cap)

            @pl.when(mine)
            def _():
                idx[count] = place - me * pool_dev

            return count + mine.astype(jnp.int32)

        lax.fori_loop(0, listed, body, jnp.int32(0), unroll=True)
        for k in range(cap):
            entry = idx[k]
            for c, (start, stop) in enumerate(cuts):
                if by_target:
                    outs[c][shift, pl.ds(k * rank, rank), :] = pool[entry, :, start:stop]
                else:
                    outs[shift * len(cuts) + c][pl.ds(k * rank, rank), :] = pool[entry, :, start:stop]


def select(slot, lists, pos, pool, cuts, by_target, n_rep, cap, after=()):
    pool_dev, rank, width = pool.shape
    if by_target:
        shapes = [sds((n_rep, cap * rank, stop - start)) for start, stop in cuts]
    else:
        shapes = [sds((cap * rank, stop - start)) for _ in range(n_rep) for start, stop in cuts]
    return pl.pallas_call(
        functools.partial(select_kernel, cuts, by_target, n_rep, cap, pool_dev, rank),
        out_shape=[*shapes, TOKEN],
        in_specs=[SMEM, SMEM, SMEM, VMEM] + [ANY] * len(after),
        out_specs=[VMEM] * len(shapes) + [VMEM],
        scratch_shapes=[pltpu.SMEM((cap,), jnp.int32)],
        compiler_params=params(),
        cost_estimate=order(0),
        name="select",
    )(slot, lists, pos, pool, *after)


def product_columns_kernel(per, pos, features, weights, late, late_send, keep, send, token):
    token[...] = jnp.zeros_like(token)
    j = pl.program_id(0)
    half = features.shape[0] // 2
    own = half // 2
    result = jnp.dot(features[...], weights[...], preferred_element_type=F32).astype(BF16)
    for chip in range(2):
        here = pos[0] == chip
        other = result[(1 - chip) * half : (2 - chip) * half]

        @pl.when(here & (j < per))
        def _():
            late[...] = other

        @pl.when(here & (j >= per))
        def _():
            late_send[...] = other

        for core in range(2):

            @pl.when(here & (pos[1] == core))
            def _():
                keep[...] = result[chip * half + core * own : chip * half + (core + 1) * own][None]
                send[...] = result[chip * half + (1 - core) * own : chip * half + (2 - core) * own][None]


def product_columns(pos, features, projection, tile, after=()):
    rows, depth = features.shape
    width = projection.shape[1] // 4
    half = rows // 2
    per = width // tile

    def block(j, pos):
        return jnp.where(j < per, pos[1], 1 - pos[1])

    rest = pl.BlockSpec((1, half // 2, tile), lambda j, pos: (block(j, pos), 0, lax.rem(j, per)))

    def kernel(pos, features, weights, *rest):
        product_columns_kernel(per, pos, features, weights, *rest[-5:])

    return pl.pallas_call(
        kernel,
        out_shape=[sds((half, width))] * 2 + [sds((2, half // 2, width))] * 2 + [TOKEN],
        grid_spec=pltpu.PrefetchScalarGridSpec(
            num_scalar_prefetch=1,
            grid=(2 * per,),
            in_specs=[
                pl.BlockSpec((rows, depth), lambda j, pos: (0, 0)),
                pl.BlockSpec((depth, tile), lambda j, pos: (0, (2 * pos[0] + block(j, pos)) * per + lax.rem(j, per))),
            ]
            + [ANY] * len(after),
            out_specs=[
                pl.BlockSpec((half, tile), lambda j, pos: (0, jnp.minimum(j, per - 1))),
                pl.BlockSpec((half, tile), lambda j, pos: (0, jnp.maximum(j - per, 0))),
                rest,
                rest,
                pl.BlockSpec((8, 128), lambda j, pos: (0, 0)),
            ],
        ),
        compiler_params=params(),
        cost_estimate=order(0),
        name="product",
    )(pos, features, projection, *after)


def product_kernel(split, pos, features, weights, keep, send, token):
    token[...] = jnp.zeros_like(token)
    own = features.shape[0] // 2
    result = jnp.dot(features[...], weights[...], preferred_element_type=F32).astype(BF16)
    low, high = result[:own], result[own:]
    if split:
        low, high = low[None], high[None]

    @pl.when(pos[1] == 0)
    def _():
        keep[...] = low
        send[...] = high

    @pl.when(pos[1] == 1)
    def _():
        keep[...] = high
        send[...] = low


def product(pos, features, projection, other_rows, other_cols, first, count, tile, blocks, after=()):
    rows, depth = features.shape
    width = projection.shape[1]
    half = rows // 2
    own = half // 2
    tiles = count // tile

    def row_block(j, pos):
        return ((1 - pos[0]) if other_rows else pos[0], 0)

    def col_block(j, pos):
        if other_cols is None:
            return (0, j + first // tile)
        chip = (1 - pos[0]) if other_cols else pos[0]
        return (0, chip * (width // 2 // tile) + j + first // tile)

    if blocks > 1:
        per = tiles // blocks
        shape = (blocks, own, count // blocks)
        out_spec = pl.BlockSpec((1, own, tile), lambda j, pos: (j // per, 0, j % per))
    else:
        shape = (own, count)
        out_spec = pl.BlockSpec((own, tile), lambda j, pos: (0, j))
    body = functools.partial(product_kernel, blocks > 1)

    def kernel(pos, features, weights, *rest):
        body(pos, features, weights, *rest[-3:])

    return pl.pallas_call(
        kernel,
        out_shape=[sds(shape), sds(shape), TOKEN],
        grid_spec=pltpu.PrefetchScalarGridSpec(
            num_scalar_prefetch=1,
            grid=(tiles,),
            in_specs=[pl.BlockSpec((half, depth), row_block), pl.BlockSpec((depth, tile), col_block)]
            + [ANY] * len(after),
            out_specs=[out_spec] * 2 + [pl.BlockSpec((8, 128), lambda j, pos: (0, 0))],
        ),
        compiler_params=params(),
        cost_estimate=order(0),
        name="product",
    )(pos, features, projection, *after)


def walk_list(slot, lists, me, n_rep, cap, pool_dev, counts, by_owner, visit):
    for s in range(n_rep):
        counts[s] = 0

    for l in range(lists.shape[1]):
        variant = lists[me, l]
        owner = slot[variant] // pool_dev
        group = owner if by_owner else lax.rem(me - owner + n_rep, n_rep)
        k = counts[group]
        counts[group] = k + 1
        visit(variant, group * cap + jnp.minimum(k, cap - 1))


def score_kernel(n_rep, cap, pool_dev, rank, slot, lists, pos, wanted, features, factors, *rest):
    out, scores, counts = rest[-3:]
    scores[...] = lax.dot_general(
        factors[...], features[...], (((1,), (1,)), ((), ())), preferred_element_type=F32
    )
    out[...] = jnp.zeros_like(out)

    def visit(variant, place):
        offset = pl.multiple_of(place * rank, rank)
        out[...] += jnp.where(wanted[...] == variant, scores[pl.ds(offset, rank), :], 0.0)

    walk_list(slot, lists, pos[2], n_rep, cap, pool_dev, counts, True, visit)


def score(slot, lists, pos, wanted, features, factors, n_rep, cap, pool_dev, rank, after=()):
    rows = features.shape[0]
    return pl.pallas_call(
        functools.partial(score_kernel, n_rep, cap, pool_dev, rank),
        out_shape=sds((rank, rows), F32),
        in_specs=[SMEM] * 3 + [VMEM] * 3 + [ANY] * len(after),
        out_specs=VMEM,
        scratch_shapes=[
            pltpu.VMEM((n_rep * cap * rank, rows), F32),
            pltpu.SMEM((n_rep,), jnp.int32),
        ],
        compiler_params=params(),
        cost_estimate=order(40),
        name="score",
    )(slot, lists, pos, wanted, features, factors, *after)


def delta_kernel(
    n_blocks, n_rep, cap, pool_dev, rank, n_before, slot, lists, pos, wanted, shrunk, late_own, late_recv, *rest
):
    blocks, before = rest[:n_blocks], rest[n_blocks : n_blocks + n_before]
    straight, cross, mine, send, spread, expand, result, variants, counts = rest[-9:]
    size = n_rep * cap * rank // n_blocks
    own, width = straight.shape
    for i in range(n_rep * cap):
        variants[i] = -1

    def visit(variant, place):
        variants[place] = variant

    walk_list(slot, lists, pos[2], n_rep, cap, pool_dev, counts, n_blocks == 1, visit)
    total = jnp.sum(shrunk[...], axis=0).astype(BF16).astype(F32)
    for i in range(n_rep * cap):
        spread[pl.ds(i * rank, rank), :] = jnp.where(wanted[...] == variants[i], total, 0.0).astype(BF16)
    for s in range(n_blocks):
        expand[pl.ds(s * size, size), :] = blocks[s][...]
    result[...] = lax.dot_general(
        spread[...], expand[...], (((0,), (0,)), ((), ())), preferred_element_type=F32
    )
    chip, core = pos[0], pos[1]
    for out, c in ((straight, core), (cross, 1 - core)):
        rows = pl.ds(pl.multiple_of(c * own, own), own)
        base = late_own[rows, :].astype(F32) + late_recv[rows, :].astype(F32)
        out[...] = (base + result[pl.ds((2 - 2 * chip + c) * own, own), :]).astype(BF16)
    start = mine.shape[1] - width
    if before:
        mine[:, :start] = before[0][...]
        send[:, :start] = before[1][...]
    mine[:, start:] = result[pl.ds((2 * chip + core) * own, own), :].astype(BF16)
    send[:, start:] = result[pl.ds((2 * chip + 1 - core) * own, own), :].astype(BF16)


def delta(slot, lists, pos, wanted, shrunk, late, blocks, cut, n_rep, cap, pool_dev, rank, own, before=(), after=()):
    rows = wanted.shape[1]
    start, stop = cut
    width = stop - start
    late_own, late_recv = late
    return pl.pallas_call(
        functools.partial(delta_kernel, len(blocks), n_rep, cap, pool_dev, rank, len(before)),
        out_shape=[sds((own, width))] * 2 + [sds((own, stop))] * 2,
        in_specs=[SMEM] * 3 + [VMEM] * (4 + len(blocks) + len(before)) + [ANY] * len(after),
        out_specs=[VMEM] * 4,
        scratch_shapes=[
            pltpu.VMEM((n_rep * cap * rank, rows), BF16),
            pltpu.VMEM((n_rep * cap * rank, width), BF16),
            pltpu.VMEM((rows, width), F32),
            pltpu.SMEM((n_rep * cap,), jnp.int32),
            pltpu.SMEM((n_rep,), jnp.int32),
        ],
        compiler_params=params(),
        cost_estimate=order(0),
        name="delta",
    )(
        slot, lists, pos, wanted, shrunk, late_own[:, start:stop], late_recv[:, start:stop], *blocks, *before, *after
    )


def gate_kernel(*refs):
    pass


def gate(arrays, after):
    n = len(arrays)
    return pl.pallas_call(
        gate_kernel,
        out_shape=[sds(x.shape, x.dtype) for x in arrays],
        in_specs=[ANY] * (n + len(after)),
        out_specs=[ANY] * n,
        input_output_aliases={i: i for i in range(n)},
        cost_estimate=order(100),
        name="gate",
    )(*arrays, *after)


def near_kernel(pos, residual, keep, recv, first, second, mine, theirs, *rest):
    out = rest[-1]
    block = pl.program_id(0)
    total = residual[...].astype(F32) + keep[0].astype(F32) + recv[0].astype(F32)
    total += jnp.where(block == 0, first[...], second[...]).astype(F32)
    total += jnp.where(block == pos[1], mine[...], theirs[...]).astype(F32)
    out[...] = total.astype(BF16)


def far_kernel(pos, residual, keep, recv, straight, cross, *rest):
    out = rest[-1]
    total = residual[...].astype(F32) + keep[0].astype(F32) + recv[0].astype(F32)
    total += jnp.where(pl.program_id(0) == pos[1], straight[...], cross[...]).astype(F32)
    out[...] = total.astype(BF16)


def finish(pos, out, residual, base, start, stop, near, pieces, after=()):
    own, full = residual.shape
    width = full // 4
    size = stop - start
    tile = min(1024, math.gcd(size, start, width))

    def place(b, j, pos):
        chip = pos[0] if near else 1 - pos[0]
        return (0, (2 * chip + b) * (width // tile) + start // tile + j)

    whole = pl.BlockSpec((own, tile), place)
    part = pl.BlockSpec((1, own, tile), lambda b, j, pos: (b, 0, start // tile + j))
    piece = pl.BlockSpec((own, tile), lambda b, j, pos: (0, j))
    operands = [pos, residual, *base, *pieces, *after]
    specs = [piece] * len(pieces) + [ANY] * len(after)
    aliases = {}
    if out is not None:
        specs = specs + [ANY]
        aliases = {len(operands): 0}
        operands.append(out)
    return pl.pallas_call(
        near_kernel if near else far_kernel,
        out_shape=sds((own, full)),
        grid_spec=pltpu.PrefetchScalarGridSpec(
            num_scalar_prefetch=1,
            grid=(2, size // tile),
            in_specs=[whole, part, part] + specs,
            out_specs=whole,
        ),
        input_output_aliases=aliases,
        compiler_params=params(),
        cost_estimate=order(60),
        name="near" if near else "far",
    )(*operands)


def paired(
    head_outputs, residual, projection, shrink_pool, expand_pool, pool_slot, variant_list, request_variant
):
    n_rep = lax.axis_size("rep")
    index = lax.axis_index("tp")
    chip, core = index // 2, index % 2
    pos = jnp.stack([chip, core, lax.axis_index("rep")]).astype(jnp.int32)
    features = head_outputs[0]
    rows = features.shape[0]
    own = rows // 4
    pool_dev, rank, width = shrink_pool.shape
    cap = pool_dev // 4 + 2
    stream = residual[0]
    lists = (pool_slot, variant_list, pos)
    sizes = (cap, pool_dev, rank)
    tile = min(1024, width)
    cut = width // 2
    cuts = ((0, cut), (cut, width))

    def over_core(x):
        return lax.ppermute(x, "tp", [(0, 1), (1, 0), (2, 3), (3, 2)])

    def over_chip(x):
        return lax.ppermute(x, "tp", [(0, 2), (2, 0), (1, 3), (3, 1)])

    def over_both(x):
        return lax.ppermute(x, "tp", [(0, 3), (3, 0), (1, 2), (2, 1)])

    def over_rep(x, shift):
        return lax.ppermute(x, "rep", [(i, (i + shift) % n_rep) for i in range(n_rep)])

    shifts = [s for s in range(1, n_rep) if s != n_rep // 2] + [n_rep // 2]
    chosen, token = select(*lists, shrink_pool, ((0, width),), True, n_rep, cap)
    shrink = lax.all_to_all(chosen, "rep", 0, 0, tiled=True).reshape(n_rep * cap * rank, width)

    early = []
    sums = []
    for b in range(2):
        keep, send, token = product(pos, features, projection, True, True, b * width, width, tile, 1, [token])
        sums.append(keep + over_core(send))
        early.append(over_chip(sums[-1]))

    *chosen, token = select(*lists, expand_pool, cuts[:1], False, n_rep, cap, [token])
    first = [chosen[0]] + [None] * (n_rep - 1)
    for s in shifts:
        first[s] = over_rep(chosen[s], s)
    chosen, token = select(*lists, expand_pool, cuts[1:], True, n_rep, cap, [token])
    second = lax.all_to_all(chosen, "rep", 0, 0, tiled=True).reshape(n_rep * cap * rank, cut)

    late_keep, late_send, keep, send, token = product_columns(pos, features, projection, tile, [*sums, token])
    late = (late_keep, over_core(late_send))
    near_base = (keep, over_core(send))

    part = score(*lists, request_variant, features, shrink, n_rep, *sizes, [token, early[0]])
    shrunk = lax.all_gather(part, "tp")

    common = (*lists, request_variant, shrunk, late)
    straight, cross, *before = delta(*common, first, cuts[0], n_rep, *sizes, own, (), [early[1]])
    far = [over_chip(straight), over_both(cross)]
    keep, send, token = product(pos, features, projection, False, True, 0, 2 * width, tile, 2, [before[0]])
    far_base = (keep, over_core(send))
    straight, cross, mine, send = delta(*common, [second], cuts[1], n_rep, *sizes, own, before, [token])
    last = [over_chip(straight), over_both(cross)]
    theirs = over_core(send)
    far = gate(far, [mine])
    out = finish(pos, None, stream, near_base, 0, width, True, [*early, mine, theirs], far)
    out = finish(pos, out, stream, far_base, *cuts[0], False, far)
    out = finish(pos, out, stream, far_base, *cuts[1], False, last)
    return out[None]


def general(
    head_outputs, residual, projection, shrink_pool, expand_pool, pool_slot, variant_list, request_variant
):
    split_count = lax.axis_size("tp")
    split_index = lax.axis_index("tp")
    replica_index = lax.axis_index("rep")
    row_count = head_outputs.shape[1]
    local_width = head_outputs.shape[2]
    rank_size = shrink_pool.shape[1]
    listed = variant_list.shape[1]
    own_rows = row_count // split_count
    flat_size = rank_size * local_width
    features = head_outputs[0]
    wanted = request_variant[0]
    my_list = lax.dynamic_index_in_dim(variant_list, replica_index, 0, keepdims=False)
    my_positions = jnp.take(pool_slot, my_list, axis=0)
    pieces = (
        lax.all_gather(shrink_pool, "rep", axis=0, tiled=True),
        lax.all_gather(expand_pool, "rep", axis=0, tiled=True),
    )
    piece_rows = pieces[0].shape[0]
    matches = (my_positions[:, None] == jnp.arange(piece_rows, dtype=jnp.int32)[None, :]).astype(BF16)
    shrink_sel = jnp.dot(matches, pieces[0].reshape(piece_rows, flat_size), preferred_element_type=F32)
    expand_sel = jnp.dot(matches, pieces[1].reshape(piece_rows, flat_size), preferred_element_type=F32)
    shrink_sel = shrink_sel.astype(BF16).reshape(listed * rank_size, local_width)
    expand_sel = expand_sel.astype(BF16).reshape(listed, rank_size, local_width)
    member = wanted[:, None] == my_list[None, :]
    scores = lax.dot_general(
        features, shrink_sel, (((1,), (1,)), ((), ())), preferred_element_type=F32
    )
    shrunk = jnp.sum(scores.reshape(row_count, listed, rank_size) * member[:, :, None], axis=1)
    own_shrunk = lax.psum_scatter(shrunk.astype(BF16), "tp", scatter_dimension=0, tiled=True)
    own_member = lax.dynamic_slice_in_dim(member, split_index * own_rows, own_rows, 0)
    spread = own_member[:, :, None] * own_shrunk[:, None, :]
    spread = spread.reshape(own_rows, listed * rank_size)
    piece = lax.all_gather(expand_sel, "tp", axis=2, tiled=True)
    delta_rows = jnp.dot(
        spread, piece.reshape(listed * rank_size, piece.shape[2]), preferred_element_type=F32
    )
    base_rows = lax.psum_scatter(
        jnp.dot(features, projection, preferred_element_type=F32).astype(BF16),
        "tp",
        scatter_dimension=0,
        tiled=True,
    ).astype(F32)
    return (residual[0].astype(F32) + base_rows + delta_rows).astype(BF16)[None]


def solution(mesh):
    in_specs = (
        P(("groups", "rep"), None, "tp"),
        P(("groups", "rep"), "tp", None),
        P("tp", None),
        P(("groups", "rep"), None, "tp"),
        P(("groups", "rep"), None, "tp"),
        P("groups"),
        P("groups", None),
        P(("groups", "rep"), None),
    )
    out_specs = P(("groups", "rep"), "tp", None)
    local = paired if mesh.shape["tp"] == 4 else general
    return jax.shard_map(local, mesh=mesh, in_specs=in_specs, out_specs=out_specs, check_vma=False)
```

```python
import functools
import math

import jax
import jax.numpy as jnp
from jax import lax
from jax.experimental import pallas as pl
from jax.experimental.pallas import tpu as pltpu
from jax.sharding import PartitionSpec as P

ANY = pl.BlockSpec(memory_space=pl.ANY)
HBM = pl.BlockSpec(memory_space=pltpu.HBM)
SMEM = pl.BlockSpec(memory_space=pltpu.SMEM)
VMEM = pl.BlockSpec(memory_space=pltpu.VMEM)
BF16 = jnp.bfloat16
F32 = jnp.float32


def order(us):
    return pl.CostEstimate(flops=int(us * 1.15e9) + 1, bytes_accessed=1, transcendentals=0)


def params(mib=48):
    return pltpu.CompilerParams(vmem_limit_bytes=mib * 2**20)


def sds(shape, dtype=BF16):
    return jax.ShapeDtypeStruct(shape, dtype)


TOKEN = sds((8, 128), F32)


def select_kernel(by_shift, by_target, n_rep, cap, pool_dev, rank, slot, lists, pos, pool, *rest):
    token, idx = rest[-2:]
    outs = rest[-2 - n_rep * len(by_shift) - len(by_target) : -2]
    token[...] = jnp.zeros_like(token)
    me = pos[2]
    for shift in range(n_rep):
        target = lax.rem(me + shift, n_rep)
        for k in range(cap):
            idx[k] = 0

        def body(l, count):
            place = slot[lists[target, l]]
            mine = (place // pool_dev == me) & (count < cap)

            @pl.when(mine)
            def _():
                idx[count] = place - me * pool_dev

            return count + mine.astype(jnp.int32)

        lax.fori_loop(0, lists.shape[1], body, jnp.int32(0), unroll=True)
        for k in range(cap):
            entry = idx[k]
            rows = pl.ds(k * rank, rank)
            for c, (start, stop) in enumerate(by_shift):
                outs[c * n_rep + shift][rows, :] = pool[entry, :, start:stop]
            for c, (start, stop) in enumerate(by_target):
                outs[len(by_shift) * n_rep + c][target, rows, :] = pool[entry, :, start:stop]


def select(slot, lists, pos, pool, by_shift, by_target, n_rep, cap, after=()):
    pool_dev, rank, width = pool.shape
    shapes = [sds((cap * rank, stop - start)) for start, stop in by_shift for _ in range(n_rep)]
    shapes += [sds((n_rep, cap * rank, stop - start)) for start, stop in by_target]
    return pl.pallas_call(
        functools.partial(select_kernel, by_shift, by_target, n_rep, cap, pool_dev, rank),
        out_shape=[*shapes, TOKEN],
        in_specs=[SMEM, SMEM, SMEM, VMEM] + [ANY] * len(after),
        out_specs=[VMEM] * len(shapes) + [VMEM],
        scratch_shapes=[pltpu.SMEM((cap,), jnp.int32)],
        compiler_params=params(16),
        cost_estimate=order(0),
        name="select",
    )(slot, lists, pos, pool, *after)


def product_columns_kernel(per, pos, features, weights, late, late_send, token):
    token[...] = jnp.zeros_like(token)
    j = pl.program_id(0)
    result = jnp.dot(features[...], weights[...], preferred_element_type=F32).astype(BF16)

    @pl.when(j < per)
    def _():
        late[...] = result

    @pl.when(j >= per)
    def _():
        late_send[...] = result


def product_columns(pos, features, projection, tile, after=()):
    rows, depth = features.shape
    width = projection.shape[1] // 4
    half = rows // 2
    per = width // tile

    def kernel(pos, features, weights, *rest):
        product_columns_kernel(per, pos, features, weights, *rest[-3:])

    return pl.pallas_call(
        kernel,
        out_shape=[sds((half, width))] * 2 + [TOKEN],
        grid_spec=pltpu.PrefetchScalarGridSpec(
            num_scalar_prefetch=1,
            grid=(2 * per,),
            in_specs=[
                pl.BlockSpec((half, depth), lambda j, pos: (1 - pos[0], 0)),
                pl.BlockSpec(
                    (depth, tile),
                    lambda j, pos: (
                        0,
                        (2 * pos[0] + jnp.where(j < per, pos[1], 1 - pos[1])) * per + lax.rem(j, per),
                    ),
                ),
            ]
            + [ANY] * len(after),
            out_specs=[
                pl.BlockSpec((half, tile), lambda j, pos: (0, jnp.minimum(j, per - 1))),
                pl.BlockSpec((half, tile), lambda j, pos: (0, jnp.maximum(j - per, 0))),
                pl.BlockSpec((8, 128), lambda j, pos: (0, 0)),
            ],
        ),
        compiler_params=params(),
        cost_estimate=order(0),
        name="product",
    )(pos, features, projection, *after)


def product_kernel(split, pos, features, weights, keep, send, token):
    token[...] = jnp.zeros_like(token)
    own = features.shape[0] // 2
    result = jnp.dot(features[...], weights[...], preferred_element_type=F32).astype(BF16)
    low, high = result[:own], result[own:]
    if split:
        low, high = low[None], high[None]

    @pl.when(pos[1] == 0)
    def _():
        keep[...] = low
        send[...] = high

    @pl.when(pos[1] == 1)
    def _():
        keep[...] = high
        send[...] = low


def product(pos, features, projection, other_rows, other_cols, first, count, tile, blocks, after=()):
    rows, depth = features.shape
    width = projection.shape[1]
    half = rows // 2
    own = half // 2
    tiles = count // tile

    def row_block(j, pos):
        return ((1 - pos[0]) if other_rows else pos[0], 0)

    def col_block(j, pos):
        if other_cols is None:
            return (0, j + first // tile)
        chip = (1 - pos[0]) if other_cols else pos[0]
        return (0, chip * (width // 2 // tile) + j + first // tile)

    if blocks > 1:
        per = tiles // blocks
        shape = (blocks, own, count // blocks)
        out_spec = pl.BlockSpec((1, own, tile), lambda j, pos: (j // per, 0, j % per))
    else:
        shape = (own, count)
        out_spec = pl.BlockSpec((own, tile), lambda j, pos: (0, j))
    body = functools.partial(product_kernel, blocks > 1)

    def kernel(pos, features, weights, *rest):
        body(pos, features, weights, *rest[-3:])

    return pl.pallas_call(
        kernel,
        out_shape=[sds(shape), sds(shape), TOKEN],
        grid_spec=pltpu.PrefetchScalarGridSpec(
            num_scalar_prefetch=1,
            grid=(tiles,),
            in_specs=[pl.BlockSpec((half, depth), row_block), pl.BlockSpec((depth, tile), col_block)]
            + [ANY] * len(after),
            out_specs=[out_spec] * 2 + [pl.BlockSpec((8, 128), lambda j, pos: (0, 0))],
        ),
        compiler_params=params(),
        cost_estimate=order(0),
        name="product",
    )(pos, features, projection, *after)


def walk_list(slot, lists, me, n_rep, cap, pool_dev, counts, by_owner, visit):
    for s in range(n_rep):
        counts[s] = 0

    for l in range(lists.shape[1]):
        variant = lists[me, l]
        owner = slot[variant] // pool_dev
        group = owner if by_owner else lax.rem(me - owner + n_rep, n_rep)
        k = counts[group]
        counts[group] = k + 1
        visit(variant, group * cap + jnp.minimum(k, cap - 1))


def score_kernel(n_rep, cap, pool_dev, rank, slot, lists, pos, wanted, features, factors, *rest):
    out, scores, counts = rest[-3:]
    scores[...] = lax.dot_general(
        factors[...], features[...], (((1,), (1,)), ((), ())), preferred_element_type=F32
    )
    out[...] = jnp.zeros_like(out)

    def visit(variant, place):
        offset = pl.multiple_of(place * rank, rank)
        out[...] += jnp.where(wanted[...] == variant, scores[pl.ds(offset, rank), :], 0.0)

    walk_list(slot, lists, pos[2], n_rep, cap, pool_dev, counts, True, visit)


def score(slot, lists, pos, wanted, features, factors, n_rep, cap, pool_dev, rank, after=()):
    rows = features.shape[0]
    return pl.pallas_call(
        functools.partial(score_kernel, n_rep, cap, pool_dev, rank),
        out_shape=sds((rank, rows), F32),
        in_specs=[SMEM] * 3 + [VMEM] * 3 + [ANY] * len(after),
        out_specs=VMEM,
        scratch_shapes=[
            pltpu.VMEM((n_rep * cap * rank, rows), F32),
            pltpu.SMEM((n_rep,), jnp.int32),
        ],
        compiler_params=params(),
        cost_estimate=order(40),
        name="score",
    )(slot, lists, pos, wanted, features, factors, *after)


def delta_kernel(
    n_blocks, n_rep, cap, pool_dev, rank, n_before, slot, lists, pos, wanted, shrunk, late_own, late_recv, *rest
):
    blocks, before = rest[:n_blocks], rest[n_blocks : n_blocks + n_before]
    straight, cross, mine, send, spread, expand, result, variants, counts = rest[-9:]
    size = n_rep * cap * rank // n_blocks
    own, width = straight.shape
    for i in range(n_rep * cap):
        variants[i] = -1

    def visit(variant, place):
        variants[place] = variant

    walk_list(slot, lists, pos[2], n_rep, cap, pool_dev, counts, n_blocks == 1, visit)
    total = jnp.sum(shrunk[...], axis=0).astype(BF16).astype(F32)
    for i in range(n_rep * cap):
        spread[pl.ds(i * rank, rank), :] = jnp.where(wanted[...] == variants[i], total, 0.0).astype(BF16)
    for s in range(n_blocks):
        expand[pl.ds(s * size, size), :] = blocks[s][...]
    result[...] = lax.dot_general(
        spread[...], expand[...], (((0,), (0,)), ((), ())), preferred_element_type=F32
    )
    chip, core = pos[0], pos[1]
    for out, c in ((straight, core), (cross, 1 - core)):
        rows = pl.ds(pl.multiple_of(c * own, own), own)
        base = late_own[rows, :].astype(F32) + late_recv[rows, :].astype(F32)
        out[...] = (base + result[pl.ds((2 - 2 * chip + c) * own, own), :]).astype(BF16)
    start = mine.shape[1] - width
    if before:
        mine[:, :start] = before[0][...]
        send[:, :start] = before[1][...]
    mine[:, start:] = result[pl.ds((2 * chip + core) * own, own), :].astype(BF16)
    send[:, start:] = result[pl.ds((2 * chip + 1 - core) * own, own), :].astype(BF16)


def delta(slot, lists, pos, wanted, shrunk, late, blocks, cut, n_rep, cap, pool_dev, rank, own, before=(), after=()):
    rows = wanted.shape[1]
    start, stop = cut
    width = stop - start
    return pl.pallas_call(
        functools.partial(delta_kernel, len(blocks), n_rep, cap, pool_dev, rank, len(before)),
        out_shape=[sds((own, width))] * 2 + [sds((own, stop))] * 2,
        grid=(1,),
        in_specs=[SMEM] * 3
        + [VMEM] * 2
        + [pl.BlockSpec((2 * own, width), lambda i: (0, start // width))] * 2
        + [VMEM] * (len(blocks) + len(before))
        + [ANY] * len(after),
        out_specs=[VMEM] * 4,
        scratch_shapes=[
            pltpu.VMEM((n_rep * cap * rank, rows), BF16),
            pltpu.VMEM((n_rep * cap * rank, width), BF16),
            pltpu.VMEM((rows, width), F32),
            pltpu.SMEM((n_rep * cap,), jnp.int32),
            pltpu.SMEM((n_rep,), jnp.int32),
        ],
        compiler_params=params(),
        cost_estimate=order(0),
        name="delta",
    )(slot, lists, pos, wanted, shrunk, *late, *blocks, *before, *after)


def gate_kernel(*refs):
    pass


def gate(arrays, after):
    n = len(arrays)
    return pl.pallas_call(
        gate_kernel,
        out_shape=[sds(x.shape, x.dtype) for x in arrays],
        in_specs=[ANY] * (n + len(after)),
        out_specs=[ANY] * n,
        input_output_aliases={i: i for i in range(n)},
        cost_estimate=order(100),
        name="gate",
    )(*arrays, *after)


def near_kernel(pos, residual, keep, recv, first, second, mine, theirs, *rest):
    out = rest[-1]
    block = pl.program_id(0)
    total = residual[...].astype(F32) + keep[0].astype(F32) + recv[0].astype(F32)
    total += jnp.where(block == 0, first[...], second[...]).astype(F32)
    total += jnp.where(block == pos[1], mine[...], theirs[...]).astype(F32)
    out[...] = total.astype(BF16)


def far_kernel(pos, residual, keep, recv, straight, cross, *rest):
    out = rest[-1]
    total = residual[...].astype(F32) + keep[0].astype(F32) + recv[0].astype(F32)
    total += jnp.where(pl.program_id(0) == pos[1], straight[...], cross[...]).astype(F32)
    out[...] = total.astype(BF16)


def finish(pos, out, residual, base, start, stop, near, pieces, after=()):
    own, full = residual.shape
    width = full // 4
    size = stop - start
    tile = min(1024, math.gcd(size, start, width))

    def place(b, j, pos):
        chip = pos[0] if near else 1 - pos[0]
        return (0, (2 * chip + b) * (width // tile) + start // tile + j)

    whole = pl.BlockSpec((own, tile), place)
    part = pl.BlockSpec((1, own, tile), lambda b, j, pos: (b, 0, start // tile + j))
    piece = pl.BlockSpec((own, tile), lambda b, j, pos: (0, j))
    operands = [pos, residual, *base, *pieces, *after]
    specs = [piece] * len(pieces) + [ANY] * len(after)
    aliases = {}
    if out is not None:
        specs = specs + [ANY]
        aliases = {len(operands): 0}
        operands.append(out)
    return pl.pallas_call(
        near_kernel if near else far_kernel,
        out_shape=sds((own, full)),
        grid_spec=pltpu.PrefetchScalarGridSpec(
            num_scalar_prefetch=1,
            grid=(2, size // tile),
            in_specs=[whole, part, part] + specs,
            out_specs=whole,
        ),
        input_output_aliases=aliases,
        compiler_params=params(),
        cost_estimate=order(60),
        name="near" if near else "far",
    )(*operands)


def paired(
    head_outputs, residual, projection, shrink_pool, expand_pool, pool_slot, variant_list, request_variant
):
    n_rep = lax.axis_size("rep")
    index = lax.axis_index("tp")
    chip, core = index // 2, index % 2
    pos = jnp.stack([chip, core, lax.axis_index("rep")]).astype(jnp.int32)
    features = head_outputs[0]
    rows = features.shape[0]
    own = rows // 4
    pool_dev, rank, width = shrink_pool.shape
    cap = pool_dev // 4 + 2
    stream = residual[0]
    lists = (pool_slot, variant_list, pos)
    sizes = (cap, pool_dev, rank)
    tile = min(1024, width)
    cut = width // 2
    cuts = ((0, cut), (cut, width))

    def over_core(x):
        return lax.ppermute(x, "tp", [(0, 1), (1, 0), (2, 3), (3, 2)])

    def over_chip(x):
        return lax.ppermute(x, "tp", [(0, 2), (2, 0), (1, 3), (3, 1)])

    def over_both(x):
        return lax.ppermute(x, "tp", [(0, 3), (3, 0), (1, 2), (2, 1)])

    def over_rep(x, shift):
        return lax.ppermute(x, "rep", [(i, (i + shift) % n_rep) for i in range(n_rep)])

    shifts = [s for s in range(1, n_rep) if s != n_rep // 2] + [n_rep // 2]
    chosen, token = select(*lists, shrink_pool, (), ((0, width),), n_rep, cap)
    shrink = lax.all_to_all(chosen, "rep", 0, 0, tiled=True).reshape(n_rep * cap * rank, width)

    early = []
    sums = []
    for b in range(2):
        keep, send, token = product(pos, features, projection, True, True, b * width, width, tile, 1, [token])
        sums.append(keep + over_core(send))
        early.append(over_chip(sums[-1]))

    *chosen, second, token = select(*lists, expand_pool, cuts[:1], cuts[1:], n_rep, cap, [token])
    first = [chosen[0]] + [None] * (n_rep - 1)
    for s in shifts:
        first[s] = over_rep(chosen[s], s)
    second = lax.all_to_all(second, "rep", 0, 0, tiled=True).reshape(n_rep * cap * rank, cut)

    keep, send, token = product_columns(pos, features, projection, tile, [*sums, token])
    late = (keep, over_core(send))

    part = score(*lists, request_variant, features, shrink, n_rep, *sizes, [token, early[0]])
    shrunk = lax.all_gather(part, "tp")

    common = (*lists, request_variant, shrunk, late)
    straight, cross, *before = delta(*common, first, cuts[0], n_rep, *sizes, own, (), [early[1]])
    far = [over_chip(straight), over_both(cross)]
    keep, send, token = product(pos, features, projection, False, False, 0, 2 * width, tile, 2, [before[0]])
    near_base = (keep, over_core(send))
    straight, cross, mine, send = delta(*common, [second], cuts[1], n_rep, *sizes, own, before, [token])
    last = [over_chip(straight), over_both(cross)]
    theirs = over_core(send)
    keep, send, token = product(pos, features, projection, False, True, 0, 2 * width, tile, 2, [mine])
    far_base = (keep, over_core(send))
    far = gate(far, [token])
    out = finish(pos, None, stream, near_base, 0, width, True, [*early, mine, theirs], far)
    out = finish(pos, out, stream, far_base, *cuts[0], False, far)
    out = finish(pos, out, stream, far_base, *cuts[1], False, last)
    return out[None]


def general(
    head_outputs, residual, projection, shrink_pool, expand_pool, pool_slot, variant_list, request_variant
):
    split_count = lax.axis_size("tp")
    split_index = lax.axis_index("tp")
    replica_index = lax.axis_index("rep")
    row_count = head_outputs.shape[1]
    local_width = head_outputs.shape[2]
    rank_size = shrink_pool.shape[1]
    listed = variant_list.shape[1]
    own_rows = row_count // split_count
    flat_size = rank_size * local_width
    features = head_outputs[0]
    wanted = request_variant[0]
    my_list = lax.dynamic_index_in_dim(variant_list, replica_index, 0, keepdims=False)
    my_positions = jnp.take(pool_slot, my_list, axis=0)
    pieces = (
        lax.all_gather(shrink_pool, "rep", axis=0, tiled=True),
        lax.all_gather(expand_pool, "rep", axis=0, tiled=True),
    )
    piece_rows = pieces[0].shape[0]
    matches = (my_positions[:, None] == jnp.arange(piece_rows, dtype=jnp.int32)[None, :]).astype(BF16)
    shrink_sel = jnp.dot(matches, pieces[0].reshape(piece_rows, flat_size), preferred_element_type=F32)
    expand_sel = jnp.dot(matches, pieces[1].reshape(piece_rows, flat_size), preferred_element_type=F32)
    shrink_sel = shrink_sel.astype(BF16).reshape(listed * rank_size, local_width)
    expand_sel = expand_sel.astype(BF16).reshape(listed, rank_size, local_width)
    member = wanted[:, None] == my_list[None, :]
    scores = lax.dot_general(
        features, shrink_sel, (((1,), (1,)), ((), ())), preferred_element_type=F32
    )
    shrunk = jnp.sum(scores.reshape(row_count, listed, rank_size) * member[:, :, None], axis=1)
    own_shrunk = lax.psum_scatter(shrunk.astype(BF16), "tp", scatter_dimension=0, tiled=True)
    own_member = lax.dynamic_slice_in_dim(member, split_index * own_rows, own_rows, 0)
    spread = own_member[:, :, None] * own_shrunk[:, None, :]
    spread = spread.reshape(own_rows, listed * rank_size)
    piece = lax.all_gather(expand_sel, "tp", axis=2, tiled=True)
    delta_rows = jnp.dot(
        spread, piece.reshape(listed * rank_size, piece.shape[2]), preferred_element_type=F32
    )
    base_rows = lax.psum_scatter(
        jnp.dot(features, projection, preferred_element_type=F32).astype(BF16),
        "tp",
        scatter_dimension=0,
        tiled=True,
    ).astype(F32)
    return (residual[0].astype(F32) + base_rows + delta_rows).astype(BF16)[None]


def solution(mesh):
    in_specs = (
        P(("groups", "rep"), None, "tp"),
        P(("groups", "rep"), "tp", None),
        P("tp", None),
        P(("groups", "rep"), None, "tp"),
        P(("groups", "rep"), None, "tp"),
        P("groups"),
        P("groups", None),
        P(("groups", "rep"), None),
    )
    out_specs = P(("groups", "rep"), "tp", None)
    local = paired if mesh.shape["tp"] == 4 else general
    return jax.shard_map(local, mesh=mesh, in_specs=in_specs, out_specs=out_specs, check_vma=False)
```

```python
import functools
import math

import jax
import jax.numpy as jnp
from jax import lax
from jax.experimental import pallas as pl
from jax.experimental.pallas import tpu as pltpu
from jax.sharding import PartitionSpec as P

ANY = pl.BlockSpec(memory_space=pl.ANY)
HBM = pl.BlockSpec(memory_space=pltpu.HBM)
SMEM = pl.BlockSpec(memory_space=pltpu.SMEM)
VMEM = pl.BlockSpec(memory_space=pltpu.VMEM)
BF16 = jnp.bfloat16
F32 = jnp.float32


def order(us):
    return pl.CostEstimate(flops=int(us * 1.15e9) + 1, bytes_accessed=1, transcendentals=0)


def params(mib=48):
    return pltpu.CompilerParams(vmem_limit_bytes=mib * 2**20)


def sds(shape, dtype=BF16):
    return jax.ShapeDtypeStruct(shape, dtype)


def in_hbm(shape, dtype=BF16):
    return pltpu.HBM(shape, dtype)


def pin(*arrays):
    return [pltpu.with_memory_space_constraint(x, pltpu.HBM) for x in arrays]


TOKEN = in_hbm((8, 128), F32)


def select_kernel(by_shift, by_target, n_rep, cap, pool_dev, rank, slot, lists, pos, pool, *rest):
    token, idx = rest[-2:]
    outs = rest[-2 - n_rep * len(by_shift) - len(by_target) : -2]
    token[...] = jnp.zeros_like(token)
    me = pos[2]
    for shift in range(n_rep):
        target = lax.rem(me + shift, n_rep)
        for k in range(cap):
            idx[k] = 0

        def body(l, count):
            place = slot[lists[target, l]]
            mine = (place // pool_dev == me) & (count < cap)

            @pl.when(mine)
            def _():
                idx[count] = place - me * pool_dev

            return count + mine.astype(jnp.int32)

        lax.fori_loop(0, lists.shape[1], body, jnp.int32(0), unroll=True)
        for k in range(cap):
            entry = idx[k]
            rows = pl.ds(k * rank, rank)
            for c, (start, stop) in enumerate(by_shift):
                outs[c * n_rep + shift][rows, :] = pool[entry, :, start:stop]
            for c, (start, stop) in enumerate(by_target):
                outs[len(by_shift) * n_rep + c][target, rows, :] = pool[entry, :, start:stop]


def select(slot, lists, pos, pool, by_shift, by_target, n_rep, cap, after=()):
    pool_dev, rank, width = pool.shape
    shapes = [in_hbm((cap * rank, stop - start)) for start, stop in by_shift for _ in range(n_rep)]
    shapes += [in_hbm((n_rep, cap * rank, stop - start)) for start, stop in by_target]
    return pl.pallas_call(
        functools.partial(select_kernel, by_shift, by_target, n_rep, cap, pool_dev, rank),
        out_shape=[*shapes, TOKEN],
        in_specs=[SMEM, SMEM, SMEM, VMEM] + [ANY] * len(after),
        out_specs=[VMEM] * len(shapes) + [VMEM],
        scratch_shapes=[pltpu.SMEM((cap,), jnp.int32)],
        compiler_params=params(16),
        cost_estimate=order(0),
        name="select",
    )(*pin(slot, lists, pos, pool), *pin(*after))


def product_columns_kernel(per, pos, features, weights, late, late_send, keep, send, token):
    token[...] = jnp.zeros_like(token)
    j = pl.program_id(0)
    half = features.shape[0] // 2
    own = half // 2
    result = jnp.dot(features[...], weights[...], preferred_element_type=F32).astype(BF16)
    for chip in range(2):
        here = pos[0] == chip
        other = result[(1 - chip) * half : (2 - chip) * half]

        @pl.when(here & (j < per))
        def _():
            late[...] = other

        @pl.when(here & (j >= per))
        def _():
            late_send[...] = other

        for core in range(2):

            @pl.when(here & (pos[1] == core))
            def _():
                keep[...] = result[chip * half + core * own : chip * half + (core + 1) * own][None]
                send[...] = result[chip * half + (1 - core) * own : chip * half + (2 - core) * own][None]


def product_columns(pos, features, projection, tile, after=()):
    rows, depth = features.shape
    width = projection.shape[1] // 4
    half = rows // 2
    per = width // tile

    def block(j, pos):
        return jnp.where(j < per, pos[1], 1 - pos[1])

    rest = pl.BlockSpec((1, half // 2, tile), lambda j, pos: (block(j, pos), 0, lax.rem(j, per)))

    def kernel(pos, features, weights, *rest):
        product_columns_kernel(per, pos, features, weights, *rest[-5:])

    return pl.pallas_call(
        kernel,
        out_shape=[in_hbm((half, width))] * 2 + [in_hbm((2, half // 2, width))] * 2 + [TOKEN],
        grid_spec=pltpu.PrefetchScalarGridSpec(
            num_scalar_prefetch=1,
            grid=(2 * per,),
            in_specs=[
                pl.BlockSpec((rows, depth), lambda j, pos: (0, 0)),
                pl.BlockSpec((depth, tile), lambda j, pos: (0, (2 * pos[0] + block(j, pos)) * per + lax.rem(j, per))),
            ]
            + [ANY] * len(after),
            out_specs=[
                pl.BlockSpec((half, tile), lambda j, pos: (0, jnp.minimum(j, per - 1))),
                pl.BlockSpec((half, tile), lambda j, pos: (0, jnp.maximum(j - per, 0))),
                rest,
                rest,
                pl.BlockSpec((8, 128), lambda j, pos: (0, 0)),
            ],
        ),
        compiler_params=params(),
        cost_estimate=order(0),
        name="product",
    )(*pin(pos), features, projection, *pin(*after))


def product_kernel(split, pos, features, weights, keep, send, token):
    token[...] = jnp.zeros_like(token)
    own = features.shape[0] // 2
    result = jnp.dot(features[...], weights[...], preferred_element_type=F32).astype(BF16)
    low, high = result[:own], result[own:]
    if split:
        low, high = low[None], high[None]

    @pl.when(pos[1] == 0)
    def _():
        keep[...] = low
        send[...] = high

    @pl.when(pos[1] == 1)
    def _():
        keep[...] = high
        send[...] = low


def product(pos, features, projection, other_rows, other_cols, first, count, tile, blocks, after=()):
    rows, depth = features.shape
    width = projection.shape[1]
    half = rows // 2
    own = half // 2
    tiles = count // tile

    def row_block(j, pos):
        return ((1 - pos[0]) if other_rows else pos[0], 0)

    def col_block(j, pos):
        if other_cols is None:
            return (0, j + first // tile)
        chip = (1 - pos[0]) if other_cols else pos[0]
        return (0, chip * (width // 2 // tile) + j + first // tile)

    if blocks > 1:
        per = tiles // blocks
        shape = (blocks, own, count // blocks)
        out_spec = pl.BlockSpec((1, own, tile), lambda j, pos: (j // per, 0, j % per))
    else:
        shape = (own, count)
        out_spec = pl.BlockSpec((own, tile), lambda j, pos: (0, j))
    body = functools.partial(product_kernel, blocks > 1)

    def kernel(pos, features, weights, *rest):
        body(pos, features, weights, *rest[-3:])

    return pl.pallas_call(
        kernel,
        out_shape=[in_hbm(shape) if blocks > 1 else sds(shape)] * 2 + [TOKEN],
        grid_spec=pltpu.PrefetchScalarGridSpec(
            num_scalar_prefetch=1,
            grid=(tiles,),
            in_specs=[pl.BlockSpec((half, depth), row_block), pl.BlockSpec((depth, tile), col_block)]
            + [ANY] * len(after),
            out_specs=[out_spec] * 2 + [pl.BlockSpec((8, 128), lambda j, pos: (0, 0))],
        ),
        compiler_params=params(),
        cost_estimate=order(0),
        name="product",
    )(*pin(pos), features, projection, *pin(*after))


def walk_list(slot, lists, me, n_rep, cap, pool_dev, counts, by_owner, visit):
    for s in range(n_rep):
        counts[s] = 0

    for l in range(lists.shape[1]):
        variant = lists[me, l]
        owner = slot[variant] // pool_dev
        group = owner if by_owner else lax.rem(me - owner + n_rep, n_rep)
        k = counts[group]
        counts[group] = k + 1
        visit(variant, group * cap + jnp.minimum(k, cap - 1))


def score_kernel(n_rep, cap, pool_dev, rank, slot, lists, pos, wanted, features, factors, *rest):
    out, scores, counts = rest[-3:]
    scores[...] = lax.dot_general(
        factors[...], features[...], (((1,), (1,)), ((), ())), preferred_element_type=F32
    )
    out[...] = jnp.zeros_like(out)

    def visit(variant, place):
        offset = pl.multiple_of(place * rank, rank)
        out[...] += jnp.where(wanted[...] == variant, scores[pl.ds(offset, rank), :], 0.0)

    walk_list(slot, lists, pos[2], n_rep, cap, pool_dev, counts, True, visit)


def score(slot, lists, pos, wanted, features, factors, n_rep, cap, pool_dev, rank, after=()):
    rows = features.shape[0]
    return pl.pallas_call(
        functools.partial(score_kernel, n_rep, cap, pool_dev, rank),
        out_shape=sds((rank, rows), F32),
        in_specs=[SMEM] * 3 + [VMEM] * 3 + [ANY] * len(after),
        out_specs=VMEM,
        scratch_shapes=[
            pltpu.VMEM((n_rep * cap * rank, rows), F32),
            pltpu.SMEM((n_rep,), jnp.int32),
        ],
        compiler_params=params(),
        cost_estimate=order(40),
        name="score",
    )(*pin(slot, lists, pos, wanted), features, *pin(factors), *pin(*after))


def delta_kernel(
    n_blocks, n_rep, cap, pool_dev, rank, n_before, slot, lists, pos, wanted, shrunk, late_own, late_recv, *rest
):
    blocks, before = rest[:n_blocks], rest[n_blocks : n_blocks + n_before]
    straight, cross, mine, send, spread, expand, result, variants, counts = rest[-9:]
    size = n_rep * cap * rank // n_blocks
    own, width = straight.shape
    for i in range(n_rep * cap):
        variants[i] = -1

    def visit(variant, place):
        variants[place] = variant

    walk_list(slot, lists, pos[2], n_rep, cap, pool_dev, counts, n_blocks == 1, visit)
    total = jnp.sum(shrunk[...], axis=0).astype(BF16).astype(F32)
    for i in range(n_rep * cap):
        spread[pl.ds(i * rank, rank), :] = jnp.where(wanted[...] == variants[i], total, 0.0).astype(BF16)
    for s in range(n_blocks):
        expand[pl.ds(s * size, size), :] = blocks[s][...]
    result[...] = lax.dot_general(
        spread[...], expand[...], (((0,), (0,)), ((), ())), preferred_element_type=F32
    )
    chip, core = pos[0], pos[1]
    for out, c in ((straight, core), (cross, 1 - core)):
        rows = pl.ds(pl.multiple_of(c * own, own), own)
        base = late_own[rows, :].astype(F32) + late_recv[rows, :].astype(F32)
        out[...] = (base + result[pl.ds((2 - 2 * chip + c) * own, own), :]).astype(BF16)
    start = mine.shape[1] - width
    if before:
        mine[:, :start] = before[0][...]
        send[:, :start] = before[1][...]
    mine[:, start:] = result[pl.ds((2 * chip + core) * own, own), :].astype(BF16)
    send[:, start:] = result[pl.ds((2 * chip + 1 - core) * own, own), :].astype(BF16)


def delta(slot, lists, pos, wanted, shrunk, late, blocks, cut, n_rep, cap, pool_dev, rank, own, before=(), after=()):
    rows = wanted.shape[1]
    start, stop = cut
    width = stop - start
    return pl.pallas_call(
        functools.partial(delta_kernel, len(blocks), n_rep, cap, pool_dev, rank, len(before)),
        out_shape=[in_hbm((own, width))] * 2 + [in_hbm((own, stop))] * 2,
        grid=(1,),
        in_specs=[SMEM] * 3
        + [VMEM] * 2
        + [pl.BlockSpec((2 * own, width), lambda i: (0, start // width))] * 2
        + [VMEM] * (len(blocks) + len(before))
        + [ANY] * len(after),
        out_specs=[VMEM] * 4,
        scratch_shapes=[
            pltpu.VMEM((n_rep * cap * rank, rows), BF16),
            pltpu.VMEM((n_rep * cap * rank, width), BF16),
            pltpu.VMEM((rows, width), F32),
            pltpu.SMEM((n_rep * cap,), jnp.int32),
            pltpu.SMEM((n_rep,), jnp.int32),
        ],
        compiler_params=params(),
        cost_estimate=order(0),
        name="delta",
    )(*pin(slot, lists, pos, wanted), shrunk, *pin(late[0]), late[1], *pin(blocks[0]), *blocks[1:], *pin(*before), *pin(*after))


def gate_kernel(*refs):
    pass


def gate(arrays, after):
    n = len(arrays)
    return pl.pallas_call(
        gate_kernel,
        out_shape=[sds(x.shape, x.dtype) for x in arrays],
        in_specs=[ANY] * (n + len(after)),
        out_specs=[ANY] * n,
        input_output_aliases={i: i for i in range(n)},
        cost_estimate=order(100),
        name="gate",
    )(*arrays, *pin(*after))


def near_kernel(pos, residual, keep, recv, first, second, mine, theirs, *rest):
    out = rest[-1]
    block = pl.program_id(0)
    total = residual[...].astype(F32) + keep[0].astype(F32) + recv[0].astype(F32)
    total += jnp.where(block == 0, first[...], second[...]).astype(F32)
    total += jnp.where(block == pos[1], mine[...], theirs[...]).astype(F32)
    out[...] = total.astype(BF16)


def far_kernel(pos, residual, keep, recv, straight, cross, *rest):
    out = rest[-1]
    total = residual[...].astype(F32) + keep[0].astype(F32) + recv[0].astype(F32)
    total += jnp.where(pl.program_id(0) == pos[1], straight[...], cross[...]).astype(F32)
    out[...] = total.astype(BF16)


def finish(pos, out, residual, base, start, stop, near, pieces, after=()):
    own, full = residual.shape
    width = full // 4
    size = stop - start
    tile = min(1024, math.gcd(size, start, width))

    def place(b, j, pos):
        chip = pos[0] if near else 1 - pos[0]
        return (0, (2 * chip + b) * (width // tile) + start // tile + j)

    whole = pl.BlockSpec((own, tile), place)
    part = pl.BlockSpec((1, own, tile), lambda b, j, pos: (b, 0, start // tile + j))
    piece = pl.BlockSpec((own, tile), lambda b, j, pos: (0, j))
    operands = [*pin(pos, residual, *base), *pieces, *pin(*after)]
    specs = [piece] * len(pieces) + [ANY] * len(after)
    aliases = {}
    if out is not None:
        specs = specs + [ANY]
        aliases = {len(operands): 0}
        operands.append(out)
    return pl.pallas_call(
        near_kernel if near else far_kernel,
        out_shape=sds((own, full)),
        grid_spec=pltpu.PrefetchScalarGridSpec(
            num_scalar_prefetch=1,
            grid=(2, size // tile),
            in_specs=[whole, part, part] + specs,
            out_specs=whole,
        ),
        input_output_aliases=aliases,
        compiler_params=params(),
        cost_estimate=order(60),
        name="near" if near else "far",
    )(*operands)


def paired(
    head_outputs, residual, projection, shrink_pool, expand_pool, pool_slot, variant_list, request_variant
):
    n_rep = lax.axis_size("rep")
    index = lax.axis_index("tp")
    chip, core = index // 2, index % 2
    pos = jnp.stack([chip, core, lax.axis_index("rep")]).astype(jnp.int32)
    features = head_outputs[0]
    rows = features.shape[0]
    own = rows // 4
    pool_dev, rank, width = shrink_pool.shape
    cap = pool_dev // 4 + 2
    stream = residual[0]
    lists = (pool_slot, variant_list, pos)
    sizes = (cap, pool_dev, rank)
    tile = min(1024, width)
    cut = width // 2
    cuts = ((0, cut), (cut, width))

    def over_core(x):
        return lax.ppermute(x, "tp", [(0, 1), (1, 0), (2, 3), (3, 2)])

    def over_chip(x):
        return lax.ppermute(x, "tp", [(0, 2), (2, 0), (1, 3), (3, 1)])

    def over_both(x):
        return lax.ppermute(x, "tp", [(0, 3), (3, 0), (1, 2), (2, 1)])

    def over_rep(x, shift):
        return lax.ppermute(x, "rep", [(i, (i + shift) % n_rep) for i in range(n_rep)])

    shifts = [s for s in range(1, n_rep) if s != n_rep // 2] + [n_rep // 2]
    chosen, token = select(*lists, shrink_pool, (), ((0, width),), n_rep, cap)
    shrink = lax.all_to_all(chosen, "rep", 0, 0, tiled=True).reshape(n_rep * cap * rank, width)

    early = []
    sums = []
    for b in range(2):
        keep, send, token = product(pos, features, projection, True, True, b * width, width, tile, 1, [token])
        sums.append(keep + over_core(send))
        early.append(over_chip(sums[-1]))

    *chosen, second, token = select(*lists, expand_pool, cuts[:1], cuts[1:], n_rep, cap, [token])
    first = [chosen[0]] + [None] * (n_rep - 1)
    for s in shifts:
        first[s] = over_rep(chosen[s], s)
    second = lax.all_to_all(second, "rep", 0, 0, tiled=True).reshape(n_rep * cap * rank, cut)

    late_keep, late_send, keep, send, token = product_columns(pos, features, projection, tile, [*sums, token])
    late = (late_keep, over_core(late_send))
    near_base = (keep, over_core(send))

    part = score(*lists, request_variant, features, shrink, n_rep, *sizes, [token, early[0]])
    shrunk = lax.all_gather(part, "tp")

    common = (*lists, request_variant, shrunk, late)
    straight, cross, *before = delta(*common, first, cuts[0], n_rep, *sizes, own, (), [early[1]])
    far = [over_chip(straight), over_both(cross)]
    keep, send, token = product(pos, features, projection, False, True, 0, 2 * width, tile, 2, [before[0]])
    far_base = (keep, over_core(send))
    straight, cross, mine, send = delta(*common, [second], cuts[1], n_rep, *sizes, own, before, [token])
    last = [over_chip(straight), over_both(cross)]
    theirs = over_core(send)
    far = gate(far, [mine])
    out = finish(pos, None, stream, near_base, 0, width, True, [*early, mine, theirs], far)
    out = finish(pos, out, stream, far_base, *cuts[0], False, far)
    out = finish(pos, out, stream, far_base, *cuts[1], False, last)
    return out[None]


def general(
    head_outputs, residual, projection, shrink_pool, expand_pool, pool_slot, variant_list, request_variant
):
    split_count = lax.axis_size("tp")
    split_index = lax.axis_index("tp")
    replica_index = lax.axis_index("rep")
    row_count = head_outputs.shape[1]
    local_width = head_outputs.shape[2]
    rank_size = shrink_pool.shape[1]
    listed = variant_list.shape[1]
    own_rows = row_count // split_count
    flat_size = rank_size * local_width
    features = head_outputs[0]
    wanted = request_variant[0]
    my_list = lax.dynamic_index_in_dim(variant_list, replica_index, 0, keepdims=False)
    my_positions = jnp.take(pool_slot, my_list, axis=0)
    pieces = (
        lax.all_gather(shrink_pool, "rep", axis=0, tiled=True),
        lax.all_gather(expand_pool, "rep", axis=0, tiled=True),
    )
    piece_rows = pieces[0].shape[0]
    matches = (my_positions[:, None] == jnp.arange(piece_rows, dtype=jnp.int32)[None, :]).astype(BF16)
    shrink_sel = jnp.dot(matches, pieces[0].reshape(piece_rows, flat_size), preferred_element_type=F32)
    expand_sel = jnp.dot(matches, pieces[1].reshape(piece_rows, flat_size), preferred_element_type=F32)
    shrink_sel = shrink_sel.astype(BF16).reshape(listed * rank_size, local_width)
    expand_sel = expand_sel.astype(BF16).reshape(listed, rank_size, local_width)
    member = wanted[:, None] == my_list[None, :]
    scores = lax.dot_general(
        features, shrink_sel, (((1,), (1,)), ((), ())), preferred_element_type=F32
    )
    shrunk = jnp.sum(scores.reshape(row_count, listed, rank_size) * member[:, :, None], axis=1)
    own_shrunk = lax.psum_scatter(shrunk.astype(BF16), "tp", scatter_dimension=0, tiled=True)
    own_member = lax.dynamic_slice_in_dim(member, split_index * own_rows, own_rows, 0)
    spread = own_member[:, :, None] * own_shrunk[:, None, :]
    spread = spread.reshape(own_rows, listed * rank_size)
    piece = lax.all_gather(expand_sel, "tp", axis=2, tiled=True)
    delta_rows = jnp.dot(
        spread, piece.reshape(listed * rank_size, piece.shape[2]), preferred_element_type=F32
    )
    base_rows = lax.psum_scatter(
        jnp.dot(features, projection, preferred_element_type=F32).astype(BF16),
        "tp",
        scatter_dimension=0,
        tiled=True,
    ).astype(F32)
    return (residual[0].astype(F32) + base_rows + delta_rows).astype(BF16)[None]


def solution(mesh):
    in_specs = (
        P(("groups", "rep"), None, "tp"),
        P(("groups", "rep"), "tp", None),
        P("tp", None),
        P(("groups", "rep"), None, "tp"),
        P(("groups", "rep"), None, "tp"),
        P("groups"),
        P("groups", None),
        P(("groups", "rep"), None),
    )
    out_specs = P(("groups", "rep"), "tp", None)
    local = paired if mesh.shape["tp"] == 4 else general
    return jax.shard_map(local, mesh=mesh, in_specs=in_specs, out_specs=out_specs, check_vma=False)
```

```python
import functools
import math

import jax
import jax.numpy as jnp
from jax import lax
from jax.experimental import pallas as pl
from jax.experimental.pallas import tpu as pltpu
from jax.sharding import PartitionSpec as P

ANY = pl.BlockSpec(memory_space=pl.ANY)
HBM = pl.BlockSpec(memory_space=pltpu.HBM)
SMEM = pl.BlockSpec(memory_space=pltpu.SMEM)
VMEM = pl.BlockSpec(memory_space=pltpu.VMEM)
BF16 = jnp.bfloat16
F32 = jnp.float32
TILE = 512


def order(us):
    return pl.CostEstimate(flops=int(us * 1.15e9) + 1, bytes_accessed=1, transcendentals=0)


def params(mib=48):
    return pltpu.CompilerParams(vmem_limit_bytes=mib * 2**20)


def sds(shape, dtype=BF16):
    return jax.ShapeDtypeStruct(shape, dtype)


def in_hbm(shape, dtype=BF16):
    return pltpu.HBM(shape, dtype)


def pin(*arrays):
    return [pltpu.with_memory_space_constraint(x, pltpu.HBM) for x in arrays]


TOKEN = in_hbm((8, 128), F32)


def select_kernel(by_shift, by_target, n_rep, cap, pool_dev, rank, slot, lists, pos, pool, *rest):
    token, idx = rest[-2:]
    outs = rest[-2 - n_rep * len(by_shift) - len(by_target) : -2]
    token[...] = jnp.zeros_like(token)
    me = pos[2]
    for shift in range(n_rep):
        target = lax.rem(me + shift, n_rep)
        for k in range(cap):
            idx[k] = 0

        def body(l, count):
            place = slot[lists[target, l]]
            mine = (place // pool_dev == me) & (count < cap)

            @pl.when(mine)
            def _():
                idx[count] = place - me * pool_dev

            return count + mine.astype(jnp.int32)

        lax.fori_loop(0, lists.shape[1], body, jnp.int32(0), unroll=True)
        for k in range(cap):
            entry = idx[k]
            rows = pl.ds(k * rank, rank)
            for c, (start, stop) in enumerate(by_shift):
                outs[c * n_rep + shift][rows, :] = pool[entry, :, start:stop]
            for c, (start, stop) in enumerate(by_target):
                outs[len(by_shift) * n_rep + c][target, rows, :] = pool[entry, :, start:stop]


def select(slot, lists, pos, pool, by_shift, by_target, n_rep, cap, after=()):
    pool_dev, rank, width = pool.shape
    shapes = [in_hbm((cap * rank, stop - start)) for start, stop in by_shift for _ in range(n_rep)]
    shapes += [in_hbm((n_rep, cap * rank, stop - start)) for start, stop in by_target]
    return pl.pallas_call(
        functools.partial(select_kernel, by_shift, by_target, n_rep, cap, pool_dev, rank),
        out_shape=[*shapes, TOKEN],
        in_specs=[SMEM, SMEM, SMEM, VMEM] + [ANY] * len(after),
        out_specs=[VMEM] * len(shapes) + [VMEM],
        scratch_shapes=[pltpu.SMEM((cap,), jnp.int32)],
        compiler_params=params(16),
        cost_estimate=order(0),
        name="select",
    )(*pin(slot, lists, pos, pool), *pin(*after))


def product_all_kernel(pos, features, weights, early, early_send, keep, send, token):
    token[...] = jnp.zeros_like(token)
    half = features.shape[0] // 2
    own = half // 2
    result = jnp.dot(features[...], weights[...], preferred_element_type=F32).astype(BF16)
    for chip in range(2):
        other, mine = (1 - chip) * half, chip * half
        for core in range(2):
            a, b = core * own, (1 - core) * own

            @pl.when((pos[0] == chip) & (pos[1] == core))
            def _():
                early[...] = result[other + a : other + a + own]
                early_send[...] = result[other + b : other + b + own]
                keep[0] = result[mine + a : mine + a + own]
                send[0] = result[mine + b : mine + b + own]


def product_all(pos, features, projection, block, tile, filled=(), after=()):
    rows, depth = features.shape
    width = projection.shape[1] // 4
    own = rows // 4
    per = width // tile

    def kernel(pos, features, weights, *rest):
        product_all_kernel(pos, features, weights, *rest[-5:])

    flat = pl.BlockSpec((own, tile), lambda j, pos: (0, j))
    part = pl.BlockSpec((1, own, tile), lambda j, pos: (block, 0, j))
    return pl.pallas_call(
        kernel,
        out_shape=[sds((own, width))] * 2 + [in_hbm((2, own, width))] * 2 + [TOKEN],
        grid_spec=pltpu.PrefetchScalarGridSpec(
            num_scalar_prefetch=1,
            grid=(per,),
            in_specs=[
                pl.BlockSpec((rows, depth), lambda j, pos: (0, 0)),
                pl.BlockSpec((depth, tile), lambda j, pos: (0, (2 * (1 - pos[0]) + block) * per + j)),
            ]
            + [ANY] * (len(filled) + len(after)),
            out_specs=[flat, flat, part, part, pl.BlockSpec((8, 128), lambda j, pos: (0, 0))],
        ),
        input_output_aliases={3 + i: 2 + i for i in range(len(filled))},
        compiler_params=params(),
        cost_estimate=order(0),
        name="product",
    )(*pin(pos), features, projection, *pin(*filled, *after))


def product_columns_kernel(per, pos, features, weights, late, late_send, token):
    token[...] = jnp.zeros_like(token)
    j = pl.program_id(0)
    result = jnp.dot(features[...], weights[...], preferred_element_type=F32).astype(BF16)

    @pl.when(j < per)
    def _():
        late[...] = result

    @pl.when(j >= per)
    def _():
        late_send[...] = result


def product_columns(pos, features, projection, tile, after=()):
    rows, depth = features.shape
    width = projection.shape[1] // 4
    half = rows // 2
    per = width // tile

    def kernel(pos, features, weights, *rest):
        product_columns_kernel(per, pos, features, weights, *rest[-3:])

    return pl.pallas_call(
        kernel,
        out_shape=[in_hbm((half, width))] * 2 + [TOKEN],
        grid_spec=pltpu.PrefetchScalarGridSpec(
            num_scalar_prefetch=1,
            grid=(2 * per,),
            in_specs=[
                pl.BlockSpec((half, depth), lambda j, pos: (1 - pos[0], 0)),
                pl.BlockSpec(
                    (depth, tile),
                    lambda j, pos: (
                        0,
                        (2 * pos[0] + jnp.where(j < per, pos[1], 1 - pos[1])) * per + lax.rem(j, per),
                    ),
                ),
            ]
            + [ANY] * len(after),
            out_specs=[
                pl.BlockSpec((half, tile), lambda j, pos: (0, jnp.minimum(j, per - 1))),
                pl.BlockSpec((half, tile), lambda j, pos: (0, jnp.maximum(j - per, 0))),
                pl.BlockSpec((8, 128), lambda j, pos: (0, 0)),
            ],
        ),
        compiler_params=params(),
        cost_estimate=order(0),
        name="product",
    )(*pin(pos), features, projection, *pin(*after))


def product_kernel(split, pos, features, weights, keep, send, token):
    token[...] = jnp.zeros_like(token)
    own = features.shape[0] // 2
    result = jnp.dot(features[...], weights[...], preferred_element_type=F32).astype(BF16)
    low, high = result[:own], result[own:]
    if split:
        low, high = low[None], high[None]

    @pl.when(pos[1] == 0)
    def _():
        keep[...] = low
        send[...] = high

    @pl.when(pos[1] == 1)
    def _():
        keep[...] = high
        send[...] = low


def product(pos, features, projection, other_rows, other_cols, first, count, tile, blocks, after=()):
    rows, depth = features.shape
    width = projection.shape[1]
    half = rows // 2
    own = half // 2
    tiles = count // tile

    def row_block(j, pos):
        return ((1 - pos[0]) if other_rows else pos[0], 0)

    def col_block(j, pos):
        if other_cols is None:
            return (0, j + first // tile)
        chip = (1 - pos[0]) if other_cols else pos[0]
        return (0, chip * (width // 2 // tile) + j + first // tile)

    if blocks > 1:
        per = tiles // blocks
        shape = (blocks, own, count // blocks)
        out_spec = pl.BlockSpec((1, own, tile), lambda j, pos: (j // per, 0, j % per))
    else:
        shape = (own, count)
        out_spec = pl.BlockSpec((own, tile), lambda j, pos: (0, j))
    body = functools.partial(product_kernel, blocks > 1)

    def kernel(pos, features, weights, *rest):
        body(pos, features, weights, *rest[-3:])

    return pl.pallas_call(
        kernel,
        out_shape=[in_hbm(shape) if blocks > 1 else sds(shape)] * 2 + [TOKEN],
        grid_spec=pltpu.PrefetchScalarGridSpec(
            num_scalar_prefetch=1,
            grid=(tiles,),
            in_specs=[pl.BlockSpec((half, depth), row_block), pl.BlockSpec((depth, tile), col_block)]
            + [ANY] * len(after),
            out_specs=[out_spec] * 2 + [pl.BlockSpec((8, 128), lambda j, pos: (0, 0))],
        ),
        compiler_params=params(),
        cost_estimate=order(0),
        name="product",
    )(*pin(pos), features, projection, *pin(*after))


def walk_list(slot, lists, me, n_rep, cap, pool_dev, counts, by_owner, visit):
    for s in range(n_rep):
        counts[s] = 0

    for l in range(lists.shape[1]):
        variant = lists[me, l]
        owner = slot[variant] // pool_dev
        group = owner if by_owner else lax.rem(me - owner + n_rep, n_rep)
        k = counts[group]
        counts[group] = k + 1
        visit(variant, group * cap + jnp.minimum(k, cap - 1))


def score_kernel(n_rep, cap, pool_dev, rank, slot, lists, pos, wanted, features, factors, *rest):
    out, scores, counts = rest[-3:]
    scores[...] = lax.dot_general(
        factors[...], features[...], (((1,), (1,)), ((), ())), preferred_element_type=F32
    )
    out[...] = jnp.zeros_like(out)

    def visit(variant, place):
        offset = pl.multiple_of(place * rank, rank)
        out[...] += jnp.where(wanted[...] == variant, scores[pl.ds(offset, rank), :], 0.0)

    walk_list(slot, lists, pos[2], n_rep, cap, pool_dev, counts, True, visit)


def score(slot, lists, pos, wanted, features, factors, n_rep, cap, pool_dev, rank, after=()):
    rows = features.shape[0]
    return pl.pallas_call(
        functools.partial(score_kernel, n_rep, cap, pool_dev, rank),
        out_shape=sds((rank, rows), F32),
        in_specs=[SMEM] * 3 + [VMEM] * 3 + [ANY] * len(after),
        out_specs=VMEM,
        scratch_shapes=[
            pltpu.VMEM((n_rep * cap * rank, rows), F32),
            pltpu.SMEM((n_rep,), jnp.int32),
        ],
        compiler_params=params(),
        cost_estimate=order(40),
        name="score",
    )(*pin(slot, lists, pos, wanted), features, *pin(factors), *pin(*after))


def delta_kernel(
    n_blocks, n_rep, cap, pool_dev, rank, n_before, slot, lists, pos, wanted, shrunk, late_own, late_recv, *rest
):
    blocks, before = rest[:n_blocks], rest[n_blocks : n_blocks + n_before]
    straight, cross, mine, send, spread, expand, result, variants, counts = rest[-9:]
    size = n_rep * cap * rank // n_blocks
    own, width = straight.shape
    for i in range(n_rep * cap):
        variants[i] = -1

    def visit(variant, place):
        variants[place] = variant

    walk_list(slot, lists, pos[2], n_rep, cap, pool_dev, counts, n_blocks == 1, visit)
    total = jnp.sum(shrunk[...], axis=0).astype(BF16).astype(F32)
    for i in range(n_rep * cap):
        spread[pl.ds(i * rank, rank), :] = jnp.where(wanted[...] == variants[i], total, 0.0).astype(BF16)
    for s in range(n_blocks):
        expand[pl.ds(s * size, size), :] = blocks[s][...]
    result[...] = lax.dot_general(
        spread[...], expand[...], (((0,), (0,)), ((), ())), preferred_element_type=F32
    )
    chip, core = pos[0], pos[1]
    for out, c in ((straight, core), (cross, 1 - core)):
        rows = pl.ds(pl.multiple_of(c * own, own), own)
        base = late_own[rows, :].astype(F32) + late_recv[rows, :].astype(F32)
        out[...] = (base + result[pl.ds((2 - 2 * chip + c) * own, own), :]).astype(BF16)
    start = mine.shape[1] - width
    if before:
        mine[:, :start] = before[0][...]
        send[:, :start] = before[1][...]
    mine[:, start:] = result[pl.ds((2 * chip + core) * own, own), :].astype(BF16)
    send[:, start:] = result[pl.ds((2 * chip + 1 - core) * own, own), :].astype(BF16)


def delta(slot, lists, pos, wanted, shrunk, late, blocks, cut, n_rep, cap, pool_dev, rank, own, before=(), after=()):
    rows = wanted.shape[1]
    start, stop = cut
    width = stop - start
    return pl.pallas_call(
        functools.partial(delta_kernel, len(blocks), n_rep, cap, pool_dev, rank, len(before)),
        out_shape=[in_hbm((own, width))] * 2 + [in_hbm((own, stop))] * 2,
        grid=(1,),
        in_specs=[SMEM] * 3
        + [VMEM] * 2
        + [pl.BlockSpec((2 * own, width), lambda i: (0, start // width))] * 2
        + [VMEM] * (len(blocks) + len(before))
        + [ANY] * len(after),
        out_specs=[VMEM] * 4,
        scratch_shapes=[
            pltpu.VMEM((n_rep * cap * rank, rows), BF16),
            pltpu.VMEM((n_rep * cap * rank, width), BF16),
            pltpu.VMEM((rows, width), F32),
            pltpu.SMEM((n_rep * cap,), jnp.int32),
            pltpu.SMEM((n_rep,), jnp.int32),
        ],
        compiler_params=params(),
        cost_estimate=order(0),
        name="delta",
    )(*pin(slot, lists, pos, wanted), shrunk, *pin(late[0]), late[1], *pin(blocks[0]), *blocks[1:], *pin(*before), *pin(*after))


def gate_kernel(*refs):
    pass


def gate(arrays, after, us=0):
    n = len(arrays)
    return pl.pallas_call(
        gate_kernel,
        out_shape=[in_hbm(x.shape, x.dtype) for x in arrays],
        in_specs=[ANY] * (n + len(after)),
        out_specs=[ANY] * n,
        input_output_aliases={i: i for i in range(n)},
        cost_estimate=order(us),
        name="gate",
    )(*pin(*arrays, *after))


def near_kernel(pos, residual, keep, recv, first, second, mine, theirs, *rest):
    out = rest[-1]
    block = pl.program_id(0)
    total = residual[...].astype(F32) + keep[0].astype(F32) + recv[0].astype(F32)
    total += jnp.where(block == 0, first[...], second[...]).astype(F32)
    total += jnp.where(block == pos[1], mine[...], theirs[...]).astype(F32)
    out[...] = total.astype(BF16)


def far_kernel(pos, residual, keep, recv, straight, cross, *rest):
    out = rest[-1]
    total = residual[...].astype(F32) + keep[0].astype(F32) + recv[0].astype(F32)
    total += jnp.where(pl.program_id(0) == pos[1], straight[...], cross[...]).astype(F32)
    out[...] = total.astype(BF16)


def finish(pos, out, residual, base, start, stop, near, pieces, after=()):
    own, full = residual.shape
    width = full // 4
    size = stop - start
    tile = min(TILE, math.gcd(size, start, width))
    count = size // tile
    skip = start // tile

    def place(b, j, pos):
        chip = pos[0] if near else 1 - pos[0]
        return (0, (2 * chip + b) * (width // tile) + skip + j)

    whole = pl.BlockSpec((own, tile), place)
    halves = [
        lambda b, j, pos: (0, skip + jnp.where(b == 0, j, count - 1)),
        lambda b, j, pos: (0, skip + jnp.where(b == 1, j, 0)),
    ]
    by_block = [pl.BlockSpec((own, tile), f) for f in halves]

    def by_core(offset):
        def index(b, j, pos):
            half = pos[1] ^ offset
            return (0, jnp.where(b == half, j, jnp.where(half == 0, count - 1, 0)))

        return pl.BlockSpec((own, tile), index)

    part = pl.BlockSpec((1, own, tile), lambda b, j, pos: (b, 0, skip + j))
    specs = [part, part, *(by_block if near else []), by_core(0), by_core(1)]
    specs = specs + [ANY] * len(after)
    operands = [*pin(pos, residual, *base), *pieces, *pin(*after)]
    aliases = {}
    if out is not None:
        specs = specs + [ANY]
        aliases = {len(operands): 0}
        operands.append(out)
    return pl.pallas_call(
        near_kernel if near else far_kernel,
        out_shape=sds((own, full)),
        grid_spec=pltpu.PrefetchScalarGridSpec(
            num_scalar_prefetch=1,
            grid=(2, count),
            in_specs=[whole, *specs],
            out_specs=whole,
        ),
        input_output_aliases=aliases,
        compiler_params=params(),
        cost_estimate=order(60),
        name="near" if near else "far",
    )(*operands)


def paired(
    head_outputs, residual, projection, shrink_pool, expand_pool, pool_slot, variant_list, request_variant
):
    n_rep = lax.axis_size("rep")
    index = lax.axis_index("tp")
    chip, core = index // 2, index % 2
    pos = jnp.stack([chip, core, lax.axis_index("rep")]).astype(jnp.int32)
    features = head_outputs[0]
    rows = features.shape[0]
    own = rows // 4
    pool_dev, rank, width = shrink_pool.shape
    cap = pool_dev // 4 + 2
    stream = residual[0]
    lists = (pool_slot, variant_list, pos)
    sizes = (cap, pool_dev, rank)
    tile = min(1024, width)
    cut = width // 2
    cuts = ((0, cut), (cut, width))

    def over_core(x):
        return lax.ppermute(x, "tp", [(0, 1), (1, 0), (2, 3), (3, 2)])

    def over_chip(x):
        return lax.ppermute(x, "tp", [(0, 2), (2, 0), (1, 3), (3, 1)])

    def over_both(x):
        return lax.ppermute(x, "tp", [(0, 3), (3, 0), (1, 2), (2, 1)])

    def over_rep(x, shift):
        return lax.ppermute(x, "rep", [(i, (i + shift) % n_rep) for i in range(n_rep)])

    shifts = [s for s in range(1, n_rep) if s != n_rep // 2] + [n_rep // 2]
    chosen, token = select(*lists, shrink_pool, (), ((0, width),), n_rep, cap)
    shrink = lax.all_to_all(chosen, "rep", 0, 0, tiled=True).reshape(n_rep * cap * rank, width)

    early = []
    sums = []
    filled = ()
    for b in range(2):
        keep, send, *filled, token = product_all(pos, features, projection, b, tile, filled, [token])
        sums.append(keep + over_core(send))
        early.append(over_chip(sums[-1]))

    *chosen, second, token = select(*lists, expand_pool, cuts[:1], cuts[1:], n_rep, cap, [token])
    first = [chosen[0]] + [None] * (n_rep - 1)
    for s in shifts:
        first[s] = over_rep(chosen[s], s)
    second = lax.all_to_all(second, "rep", 0, 0, tiled=True).reshape(n_rep * cap * rank, cut)

    keep, send, token = product_columns(pos, features, projection, tile, [*sums, token])
    late = (keep, over_core(send))

    part = score(*lists, request_variant, features, shrink, n_rep, *sizes, [token, early[0]])
    shrunk = lax.all_gather(part, "tp")

    common = (*lists, request_variant, shrunk, late)
    straight, cross, *before = delta(*common, first, cuts[0], n_rep, *sizes, own, (), [early[1]])
    far = [over_chip(straight), over_both(cross)]
    far_base = (filled[0], over_core(filled[1]))
    keep, send, token = product(pos, features, projection, False, False, 0, 2 * width, tile, 2, [before[0]])
    near_base = (keep, over_core(send))
    straight, cross, mine, send = delta(*common, [second], cuts[1], n_rep, *sizes, own, before, [token])
    last = [over_chip(straight), over_both(cross)]
    theirs = over_core(send)
    far = gate(far, [mine], 100)
    out = finish(pos, None, stream, near_base, 0, width, True, [*early, mine, theirs], far)
    out = finish(pos, out, stream, far_base, *cuts[0], False, far)
    out = finish(pos, out, stream, far_base, *cuts[1], False, last)
    return out[None]


def general(
    head_outputs, residual, projection, shrink_pool, expand_pool, pool_slot, variant_list, request_variant
):
    split_count = lax.axis_size("tp")
    split_index = lax.axis_index("tp")
    replica_index = lax.axis_index("rep")
    row_count = head_outputs.shape[1]
    local_width = head_outputs.shape[2]
    rank_size = shrink_pool.shape[1]
    listed = variant_list.shape[1]
    own_rows = row_count // split_count
    flat_size = rank_size * local_width
    features = head_outputs[0]
    wanted = request_variant[0]
    my_list = lax.dynamic_index_in_dim(variant_list, replica_index, 0, keepdims=False)
    my_positions = jnp.take(pool_slot, my_list, axis=0)
    pieces = (
        lax.all_gather(shrink_pool, "rep", axis=0, tiled=True),
        lax.all_gather(expand_pool, "rep", axis=0, tiled=True),
    )
    piece_rows = pieces[0].shape[0]
    matches = (my_positions[:, None] == jnp.arange(piece_rows, dtype=jnp.int32)[None, :]).astype(BF16)
    shrink_sel = jnp.dot(matches, pieces[0].reshape(piece_rows, flat_size), preferred_element_type=F32)
    expand_sel = jnp.dot(matches, pieces[1].reshape(piece_rows, flat_size), preferred_element_type=F32)
    shrink_sel = shrink_sel.astype(BF16).reshape(listed * rank_size, local_width)
    expand_sel = expand_sel.astype(BF16).reshape(listed, rank_size, local_width)
    member = wanted[:, None] == my_list[None, :]
    scores = lax.dot_general(
        features, shrink_sel, (((1,), (1,)), ((), ())), preferred_element_type=F32
    )
    shrunk = jnp.sum(scores.reshape(row_count, listed, rank_size) * member[:, :, None], axis=1)
    own_shrunk = lax.psum_scatter(shrunk.astype(BF16), "tp", scatter_dimension=0, tiled=True)
    own_member = lax.dynamic_slice_in_dim(member, split_index * own_rows, own_rows, 0)
    spread = own_member[:, :, None] * own_shrunk[:, None, :]
    spread = spread.reshape(own_rows, listed * rank_size)
    piece = lax.all_gather(expand_sel, "tp", axis=2, tiled=True)
    delta_rows = jnp.dot(
        spread, piece.reshape(listed * rank_size, piece.shape[2]), preferred_element_type=F32
    )
    base_rows = lax.psum_scatter(
        jnp.dot(features, projection, preferred_element_type=F32).astype(BF16),
        "tp",
        scatter_dimension=0,
        tiled=True,
    ).astype(F32)
    return (residual[0].astype(F32) + base_rows + delta_rows).astype(BF16)[None]


def solution(mesh):
    in_specs = (
        P(("groups", "rep"), None, "tp"),
        P(("groups", "rep"), "tp", None),
        P("tp", None),
        P(("groups", "rep"), None, "tp"),
        P(("groups", "rep"), None, "tp"),
        P("groups"),
        P("groups", None),
        P(("groups", "rep"), None),
    )
    out_specs = P(("groups", "rep"), "tp", None)
    local = paired if mesh.shape["tp"] == 4 else general
    return jax.shard_map(local, mesh=mesh, in_specs=in_specs, out_specs=out_specs, check_vma=False)
```

```python
import functools
import math

import jax
import jax.numpy as jnp
from jax import lax
from jax.experimental import pallas as pl
from jax.experimental.pallas import tpu as pltpu
from jax.sharding import PartitionSpec as P

ANY = pl.BlockSpec(memory_space=pl.ANY)
HBM = pl.BlockSpec(memory_space=pltpu.HBM)
SMEM = pl.BlockSpec(memory_space=pltpu.SMEM)
VMEM = pl.BlockSpec(memory_space=pltpu.VMEM)
BF16 = jnp.bfloat16
F32 = jnp.float32
TILE = 1024


def order(us):
    return pl.CostEstimate(flops=int(us * 1.15e9) + 1, bytes_accessed=1, transcendentals=0)


def params(mib=48):
    return pltpu.CompilerParams(vmem_limit_bytes=mib * 2**20)


def sds(shape, dtype=BF16):
    return jax.ShapeDtypeStruct(shape, dtype)


def in_hbm(shape, dtype=BF16):
    return pltpu.HBM(shape, dtype)


def pin(*arrays):
    return [pltpu.with_memory_space_constraint(x, pltpu.HBM) for x in arrays]


TOKEN = in_hbm((8, 128), F32)


def select_kernel(by_shift, by_target, n_rep, cap, pool_dev, rank, slot, lists, pool, *rest):
    token, idx = rest[-2:]
    outs = rest[-2 - n_rep * len(by_shift) - len(by_target) : -2]
    token[...] = jnp.zeros_like(token)
    me = lax.axis_index("rep")
    for shift in range(n_rep):
        target = lax.rem(me + shift, n_rep)
        for k in range(cap):
            idx[k] = 0

        def body(l, count):
            place = slot[lists[target, l]]
            mine = (place // pool_dev == me) & (count < cap)

            @pl.when(mine)
            def _():
                idx[count] = place - me * pool_dev

            return count + mine.astype(jnp.int32)

        lax.fori_loop(0, lists.shape[1], body, jnp.int32(0), unroll=True)
        for k in range(cap):
            entry = idx[k]
            rows = pl.ds(k * rank, rank)
            for c, (start, stop) in enumerate(by_shift):
                outs[c * n_rep + shift][rows, :] = pool[entry, :, start:stop]
            for c, (start, stop) in enumerate(by_target):
                outs[len(by_shift) * n_rep + c][target, rows, :] = pool[entry, :, start:stop]


def select(slot, lists, pool, by_shift, by_target, n_rep, cap, after=()):
    pool_dev, rank, width = pool.shape
    shapes = [in_hbm((cap * rank, stop - start)) for start, stop in by_shift for _ in range(n_rep)]
    shapes += [in_hbm((n_rep, cap * rank, stop - start)) for start, stop in by_target]
    return pl.pallas_call(
        functools.partial(select_kernel, by_shift, by_target, n_rep, cap, pool_dev, rank),
        out_shape=[*shapes, TOKEN],
        in_specs=[SMEM, SMEM, VMEM] + [ANY] * len(after),
        out_specs=[VMEM] * len(shapes) + [VMEM],
        scratch_shapes=[pltpu.SMEM((cap,), jnp.int32)],
        compiler_params=params(16),
        cost_estimate=order(0),
        name="select",
    )(*pin(slot, lists, pool), *pin(*after))


def product_early_kernel(per, pos, features, weights, keep0, send0, keep1, send1, token):
    token[...] = jnp.zeros_like(token)
    j = pl.program_id(0)
    own = features.shape[0] // 2
    result = jnp.dot(features[...], weights[...], preferred_element_type=F32).astype(BF16)
    for core in range(2):
        a, b = core * own, (1 - core) * own
        for block, keep, send in ((0, keep0, send0), (1, keep1, send1)):

            @pl.when((pos[1] == core) & (j // per == block))
            def _():
                keep[...] = result[a : a + own]
                send[...] = result[b : b + own]


def product_early(pos, features, projection, tile, after=()):
    rows, depth = features.shape
    width = projection.shape[1] // 4
    half = rows // 2
    per = width // tile

    def kernel(pos, features, weights, *rest):
        product_early_kernel(per, pos, features, weights, *rest[-5:])

    low = pl.BlockSpec((half // 2, tile), lambda j, pos: (0, jnp.minimum(j, per - 1)))
    high = pl.BlockSpec((half // 2, tile), lambda j, pos: (0, jnp.maximum(j - per, 0)))
    return pl.pallas_call(
        kernel,
        out_shape=[sds((half // 2, width))] * 4 + [TOKEN],
        grid_spec=pltpu.PrefetchScalarGridSpec(
            num_scalar_prefetch=1,
            grid=(2 * per,),
            in_specs=[
                pl.BlockSpec((half, depth), lambda j, pos: (1 - pos[0], 0)),
                pl.BlockSpec((depth, tile), lambda j, pos: (0, 2 * (1 - pos[0]) * per + j)),
            ]
            + [ANY] * len(after),
            out_specs=[low, low, high, high, pl.BlockSpec((8, 128), lambda j, pos: (0, 0))],
        ),
        compiler_params=params(),
        cost_estimate=order(0),
        name="product",
    )(*pin(pos), features, projection, *pin(*after))


def product_columns_kernel(per, pos, features, weights, late, late_send, keep, send, token):
    token[...] = jnp.zeros_like(token)
    j = pl.program_id(0)
    half = features.shape[0] // 2
    own = half // 2
    result = jnp.dot(features[...], weights[...], preferred_element_type=F32).astype(BF16)
    for chip in range(2):
        here = pos[0] == chip
        other = result[(1 - chip) * half : (2 - chip) * half]

        @pl.when(here & (j < per))
        def _():
            late[...] = other

        @pl.when(here & (j >= per))
        def _():
            late_send[...] = other

        for core in range(2):

            @pl.when(here & (pos[1] == core))
            def _():
                keep[...] = result[chip * half + core * own : chip * half + (core + 1) * own][None]
                send[...] = result[chip * half + (1 - core) * own : chip * half + (2 - core) * own][None]


def product_columns(pos, features, projection, tile, after=()):
    rows, depth = features.shape
    width = projection.shape[1] // 4
    half = rows // 2
    per = width // tile

    def block(j, pos):
        return jnp.where(j < per, pos[1], 1 - pos[1])

    rest = pl.BlockSpec((1, half // 2, tile), lambda j, pos: (block(j, pos), 0, lax.rem(j, per)))

    def kernel(pos, features, weights, *rest):
        product_columns_kernel(per, pos, features, weights, *rest[-5:])

    return pl.pallas_call(
        kernel,
        out_shape=[in_hbm((half, width))] * 2 + [in_hbm((2, half // 2, width))] * 2 + [TOKEN],
        grid_spec=pltpu.PrefetchScalarGridSpec(
            num_scalar_prefetch=1,
            grid=(2 * per,),
            in_specs=[
                pl.BlockSpec((rows, depth), lambda j, pos: (0, 0)),
                pl.BlockSpec((depth, tile), lambda j, pos: (0, (2 * pos[0] + block(j, pos)) * per + lax.rem(j, per))),
            ]
            + [ANY] * len(after),
            out_specs=[
                pl.BlockSpec((half, tile), lambda j, pos: (0, jnp.minimum(j, per - 1))),
                pl.BlockSpec((half, tile), lambda j, pos: (0, jnp.maximum(j - per, 0))),
                rest,
                rest,
                pl.BlockSpec((8, 128), lambda j, pos: (0, 0)),
            ],
        ),
        compiler_params=params(),
        cost_estimate=order(0),
        name="product",
    )(*pin(pos), features, projection, *pin(*after))


def product_kernel(split, pos, features, weights, keep, send, token):
    token[...] = jnp.zeros_like(token)
    own = features.shape[0] // 2
    result = jnp.dot(features[...], weights[...], preferred_element_type=F32).astype(BF16)
    low, high = result[:own], result[own:]
    if split:
        low, high = low[None], high[None]

    @pl.when(pos[1] == 0)
    def _():
        keep[...] = low
        send[...] = high

    @pl.when(pos[1] == 1)
    def _():
        keep[...] = high
        send[...] = low


def product(pos, features, projection, other_rows, other_cols, first, count, tile, blocks, after=()):
    rows, depth = features.shape
    width = projection.shape[1]
    half = rows // 2
    own = half // 2
    tiles = count // tile

    def row_block(j, pos):
        return ((1 - pos[0]) if other_rows else pos[0], 0)

    def col_block(j, pos):
        if other_cols is None:
            return (0, j + first // tile)
        chip = (1 - pos[0]) if other_cols else pos[0]
        return (0, chip * (width // 2 // tile) + j + first // tile)

    if blocks > 1:
        per = tiles // blocks
        shape = (blocks, own, count // blocks)
        out_spec = pl.BlockSpec((1, own, tile), lambda j, pos: (j // per, 0, j % per))
    else:
        shape = (own, count)
        out_spec = pl.BlockSpec((own, tile), lambda j, pos: (0, j))
    body = functools.partial(product_kernel, blocks > 1)

    def kernel(pos, features, weights, *rest):
        body(pos, features, weights, *rest[-3:])

    return pl.pallas_call(
        kernel,
        out_shape=[in_hbm(shape) if blocks > 1 else sds(shape)] * 2 + [TOKEN],
        grid_spec=pltpu.PrefetchScalarGridSpec(
            num_scalar_prefetch=1,
            grid=(tiles,),
            in_specs=[pl.BlockSpec((half, depth), row_block), pl.BlockSpec((depth, tile), col_block)]
            + [ANY] * len(after),
            out_specs=[out_spec] * 2 + [pl.BlockSpec((8, 128), lambda j, pos: (0, 0))],
        ),
        compiler_params=params(),
        cost_estimate=order(0),
        name="product",
    )(*pin(pos), features, projection, *pin(*after))


def walk_list(slot, lists, me, n_rep, cap, pool_dev, counts, by_owner, visit):
    for s in range(n_rep):
        counts[s] = 0

    for l in range(lists.shape[1]):
        variant = lists[me, l]
        owner = slot[variant] // pool_dev
        group = owner if by_owner else lax.rem(me - owner + n_rep, n_rep)
        k = counts[group]
        counts[group] = k + 1
        visit(variant, group * cap + jnp.minimum(k, cap - 1))


def score_kernel(n_rep, cap, pool_dev, rank, slot, lists, pos, wanted, features, factors, *rest):
    out, scores, counts = rest[-3:]
    scores[...] = lax.dot_general(
        factors[...], features[...], (((1,), (1,)), ((), ())), preferred_element_type=F32
    )
    out[...] = jnp.zeros_like(out)

    def visit(variant, place):
        offset = pl.multiple_of(place * rank, rank)
        out[...] += jnp.where(wanted[...] == variant, scores[pl.ds(offset, rank), :], 0.0)

    walk_list(slot, lists, pos[2], n_rep, cap, pool_dev, counts, True, visit)


def score(slot, lists, pos, wanted, features, factors, n_rep, cap, pool_dev, rank, after=()):
    rows = features.shape[0]
    return pl.pallas_call(
        functools.partial(score_kernel, n_rep, cap, pool_dev, rank),
        out_shape=sds((rank, rows), F32),
        in_specs=[SMEM] * 3 + [VMEM] * 3 + [ANY] * len(after),
        out_specs=VMEM,
        scratch_shapes=[
            pltpu.VMEM((n_rep * cap * rank, rows), F32),
            pltpu.SMEM((n_rep,), jnp.int32),
        ],
        compiler_params=params(),
        cost_estimate=order(40),
        name="score",
    )(*pin(slot, lists, pos, wanted), features, *pin(factors), *pin(*after))


def delta_kernel(
    n_blocks, n_rep, cap, pool_dev, rank, n_before, slot, lists, pos, wanted, shrunk, late_own, late_recv, *rest
):
    blocks, before = rest[:n_blocks], rest[n_blocks : n_blocks + n_before]
    straight, cross, mine, send, spread, expand, result, variants, counts = rest[-9:]
    size = n_rep * cap * rank // n_blocks
    own, width = straight.shape
    for i in range(n_rep * cap):
        variants[i] = -1

    def visit(variant, place):
        variants[place] = variant

    walk_list(slot, lists, pos[2], n_rep, cap, pool_dev, counts, n_blocks == 1, visit)
    total = jnp.sum(shrunk[...], axis=0).astype(BF16).astype(F32)
    for i in range(n_rep * cap):
        spread[pl.ds(i * rank, rank), :] = jnp.where(wanted[...] == variants[i], total, 0.0).astype(BF16)
    for s in range(n_blocks):
        expand[pl.ds(s * size, size), :] = blocks[s][...]
    result[...] = lax.dot_general(
        spread[...], expand[...], (((0,), (0,)), ((), ())), preferred_element_type=F32
    )
    chip, core = pos[0], pos[1]
    for out, c in ((straight, core), (cross, 1 - core)):
        rows = pl.ds(pl.multiple_of(c * own, own), own)
        base = late_own[rows, :].astype(F32) + late_recv[rows, :].astype(F32)
        out[...] = (base + result[pl.ds((2 - 2 * chip + c) * own, own), :]).astype(BF16)
    start = mine.shape[1] - width
    if before:
        mine[:, :start] = before[0][...]
        send[:, :start] = before[1][...]
    mine[:, start:] = result[pl.ds((2 * chip + core) * own, own), :].astype(BF16)
    send[:, start:] = result[pl.ds((2 * chip + 1 - core) * own, own), :].astype(BF16)


def delta(slot, lists, pos, wanted, shrunk, late, blocks, cut, n_rep, cap, pool_dev, rank, own, before=(), after=()):
    rows = wanted.shape[1]
    start, stop = cut
    width = stop - start
    return pl.pallas_call(
        functools.partial(delta_kernel, len(blocks), n_rep, cap, pool_dev, rank, len(before)),
        out_shape=[in_hbm((own, width))] * 2 + [in_hbm((own, stop))] * 2,
        grid=(1,),
        in_specs=[SMEM] * 3
        + [VMEM] * 2
        + [pl.BlockSpec((2 * own, width), lambda i: (0, start // width))] * 2
        + [VMEM] * (len(blocks) + len(before))
        + [ANY] * len(after),
        out_specs=[VMEM] * 4,
        scratch_shapes=[
            pltpu.VMEM((n_rep * cap * rank, rows), BF16),
            pltpu.VMEM((n_rep * cap * rank, width), BF16),
            pltpu.VMEM((rows, width), F32),
            pltpu.SMEM((n_rep * cap,), jnp.int32),
            pltpu.SMEM((n_rep,), jnp.int32),
        ],
        compiler_params=params(),
        cost_estimate=order(0),
        name="delta",
    )(*pin(slot, lists, pos, wanted), shrunk, *pin(late[0]), late[1], *pin(blocks[0]), *blocks[1:], *pin(*before), *pin(*after))


def gate_kernel(*refs):
    pass


def gate(arrays, after):
    n = len(arrays)
    return pl.pallas_call(
        gate_kernel,
        out_shape=[sds(x.shape, x.dtype) for x in arrays],
        in_specs=[ANY] * (n + len(after)),
        out_specs=[ANY] * n,
        input_output_aliases={i: i for i in range(n)},
        cost_estimate=order(100),
        name="gate",
    )(*arrays, *pin(*after))


def near_kernel(pos, residual, keep, recv, first, second, mine, theirs, *rest):
    out = rest[-1]
    block = pl.program_id(0)
    total = residual[...].astype(F32) + keep[0].astype(F32) + recv[0].astype(F32)
    total += jnp.where(block == 0, first[...], second[...]).astype(F32)
    total += jnp.where(block == pos[1], mine[...], theirs[...]).astype(F32)
    out[...] = total.astype(BF16)


def far_kernel(pos, residual, keep, recv, straight, cross, *rest):
    out = rest[-1]
    total = residual[...].astype(F32) + keep[0].astype(F32) + recv[0].astype(F32)
    total += jnp.where(pl.program_id(0) == pos[1], straight[...], cross[...]).astype(F32)
    out[...] = total.astype(BF16)


def finish(pos, out, residual, base, start, stop, near, pieces, after=()):
    own, full = residual.shape
    width = full // 4
    size = stop - start
    tile = min(TILE, math.gcd(size, start, width))
    count = size // tile
    skip = start // tile

    def place(b, j, pos):
        chip = pos[0] if near else 1 - pos[0]
        return (0, (2 * chip + b) * (width // tile) + skip + j)

    whole = pl.BlockSpec((own, tile), place)
    halves = [
        lambda b, j, pos: (0, skip + jnp.where(b == 0, j, count - 1)),
        lambda b, j, pos: (0, skip + jnp.where(b == 1, j, 0)),
    ]
    by_block = [pl.BlockSpec((own, tile), f) for f in halves]

    def by_core(offset):
        def index(b, j, pos):
            half = pos[1] ^ offset
            return (0, jnp.where(b == half, j, jnp.where(half == 0, count - 1, 0)))

        return pl.BlockSpec((own, tile), index)

    part = pl.BlockSpec((1, own, tile), lambda b, j, pos: (b, 0, skip + j))
    specs = [part, part, *(by_block if near else []), by_core(0), by_core(1)]
    specs = specs + [ANY] * len(after)
    operands = [*pin(pos, residual, *base), *pieces, *pin(*after)]
    aliases = {}
    if out is not None:
        specs = specs + [ANY]
        aliases = {len(operands): 0}
        operands.append(out)
    return pl.pallas_call(
        near_kernel if near else far_kernel,
        out_shape=sds((own, full)),
        grid_spec=pltpu.PrefetchScalarGridSpec(
            num_scalar_prefetch=1,
            grid=(2, count),
            in_specs=[whole, *specs],
            out_specs=whole,
        ),
        input_output_aliases=aliases,
        compiler_params=params(),
        cost_estimate=order(60),
        name="near" if near else "far",
    )(*operands)


def paired(
    head_outputs, residual, projection, shrink_pool, expand_pool, pool_slot, variant_list, request_variant
):
    n_rep = lax.axis_size("rep")
    index = lax.axis_index("tp")
    chip, core = index // 2, index % 2
    pos = jnp.stack([chip, core, lax.axis_index("rep")]).astype(jnp.int32)
    features = head_outputs[0]
    rows = features.shape[0]
    own = rows // 4
    pool_dev, rank, width = shrink_pool.shape
    cap = pool_dev // 4 + 2
    stream = residual[0]
    lists = (pool_slot, variant_list, pos)
    sizes = (cap, pool_dev, rank)
    tile = min(1024, width)
    cut = width // 2
    cuts = ((0, cut), (cut, width))

    def over_core(x):
        return lax.ppermute(x, "tp", [(0, 1), (1, 0), (2, 3), (3, 2)])

    def over_chip(x):
        return lax.ppermute(x, "tp", [(0, 2), (2, 0), (1, 3), (3, 1)])

    def over_both(x):
        return lax.ppermute(x, "tp", [(0, 3), (3, 0), (1, 2), (2, 1)])

    def over_rep(x, shift):
        return lax.ppermute(x, "rep", [(i, (i + shift) % n_rep) for i in range(n_rep)])

    shifts = [s for s in range(1, n_rep) if s != n_rep // 2] + [n_rep // 2]
    chosen, token = select(pool_slot, variant_list, shrink_pool, (), ((0, width),), n_rep, cap)
    shrink = lax.all_to_all(chosen, "rep", 0, 0, tiled=True).reshape(n_rep * cap * rank, width)

    keep0, send0, keep1, send1, token = product_early(pos, features, projection, tile, [token])
    sums = [keep0 + over_core(send0), keep1 + over_core(send1)]
    early = [over_chip(x) for x in sums]

    *chosen, second, token = select(pool_slot, variant_list, expand_pool, cuts[:1], cuts[1:], n_rep, cap, sums)
    first = [chosen[0]] + [None] * (n_rep - 1)
    for s in shifts:
        first[s] = over_rep(chosen[s], s)
    second = lax.all_to_all(second, "rep", 0, 0, tiled=True).reshape(n_rep * cap * rank, cut)

    late_keep, late_send, keep, send, token = product_columns(pos, features, projection, tile, [*sums, token])
    late = (late_keep, over_core(late_send))
    near_base = (keep, over_core(send))

    part = score(*lists, request_variant, features, shrink, n_rep, *sizes, [token, early[0]])
    shrunk = lax.all_gather(part, "tp")

    common = (*lists, request_variant, shrunk, late)
    straight, cross, *before = delta(*common, first, cuts[0], n_rep, *sizes, own, (), [early[1]])
    far = [over_chip(straight), over_both(cross)]
    straight, cross, mine, send = delta(*common, [second], cuts[1], n_rep, *sizes, own, before)
    last = [over_chip(straight), over_both(cross)]
    theirs = over_core(send)
    keep, send, token = product(pos, features, projection, False, True, 0, 2 * width, tile, 2, [mine])
    far_base = (keep, over_core(send))
    far = gate(far, [token])
    out = finish(pos, None, stream, near_base, 0, width, True, [*early, mine, theirs], far)
    out = finish(pos, out, stream, far_base, *cuts[0], False, far)
    out = finish(pos, out, stream, far_base, *cuts[1], False, last)
    return out[None]


def general(
    head_outputs, residual, projection, shrink_pool, expand_pool, pool_slot, variant_list, request_variant
):
    split_count = lax.axis_size("tp")
    split_index = lax.axis_index("tp")
    replica_index = lax.axis_index("rep")
    row_count = head_outputs.shape[1]
    local_width = head_outputs.shape[2]
    rank_size = shrink_pool.shape[1]
    listed = variant_list.shape[1]
    own_rows = row_count // split_count
    flat_size = rank_size * local_width
    features = head_outputs[0]
    wanted = request_variant[0]
    my_list = lax.dynamic_index_in_dim(variant_list, replica_index, 0, keepdims=False)
    my_positions = jnp.take(pool_slot, my_list, axis=0)
    pieces = (
        lax.all_gather(shrink_pool, "rep", axis=0, tiled=True),
        lax.all_gather(expand_pool, "rep", axis=0, tiled=True),
    )
    piece_rows = pieces[0].shape[0]
    matches = (my_positions[:, None] == jnp.arange(piece_rows, dtype=jnp.int32)[None, :]).astype(BF16)
    shrink_sel = jnp.dot(matches, pieces[0].reshape(piece_rows, flat_size), preferred_element_type=F32)
    expand_sel = jnp.dot(matches, pieces[1].reshape(piece_rows, flat_size), preferred_element_type=F32)
    shrink_sel = shrink_sel.astype(BF16).reshape(listed * rank_size, local_width)
    expand_sel = expand_sel.astype(BF16).reshape(listed, rank_size, local_width)
    member = wanted[:, None] == my_list[None, :]
    scores = lax.dot_general(
        features, shrink_sel, (((1,), (1,)), ((), ())), preferred_element_type=F32
    )
    shrunk = jnp.sum(scores.reshape(row_count, listed, rank_size) * member[:, :, None], axis=1)
    own_shrunk = lax.psum_scatter(shrunk.astype(BF16), "tp", scatter_dimension=0, tiled=True)
    own_member = lax.dynamic_slice_in_dim(member, split_index * own_rows, own_rows, 0)
    spread = own_member[:, :, None] * own_shrunk[:, None, :]
    spread = spread.reshape(own_rows, listed * rank_size)
    piece = lax.all_gather(expand_sel, "tp", axis=2, tiled=True)
    delta_rows = jnp.dot(
        spread, piece.reshape(listed * rank_size, piece.shape[2]), preferred_element_type=F32
    )
    base_rows = lax.psum_scatter(
        jnp.dot(features, projection, preferred_element_type=F32).astype(BF16),
        "tp",
        scatter_dimension=0,
        tiled=True,
    ).astype(F32)
    return (residual[0].astype(F32) + base_rows + delta_rows).astype(BF16)[None]


def solution(mesh):
    in_specs = (
        P(("groups", "rep"), None, "tp"),
        P(("groups", "rep"), "tp", None),
        P("tp", None),
        P(("groups", "rep"), None, "tp"),
        P(("groups", "rep"), None, "tp"),
        P("groups"),
        P("groups", None),
        P(("groups", "rep"), None),
    )
    out_specs = P(("groups", "rep"), "tp", None)
    local = paired if mesh.shape["tp"] == 4 else general
    return jax.shard_map(local, mesh=mesh, in_specs=in_specs, out_specs=out_specs, check_vma=False)
```

```python
import functools
import math

import jax
import jax.numpy as jnp
from jax import lax
from jax.experimental import pallas as pl
from jax.experimental.pallas import tpu as pltpu
from jax.sharding import PartitionSpec as P

ANY = pl.BlockSpec(memory_space=pl.ANY)
HBM = pl.BlockSpec(memory_space=pltpu.HBM)
SMEM = pl.BlockSpec(memory_space=pltpu.SMEM)
VMEM = pl.BlockSpec(memory_space=pltpu.VMEM)
BF16 = jnp.bfloat16
F32 = jnp.float32
TILE = 1024


def order(us):
    return pl.CostEstimate(flops=int(us * 1.15e9) + 1, bytes_accessed=1, transcendentals=0)


def position():
    index = lax.axis_index("tp")
    return lax.div(index, 2), lax.rem(index, 2), lax.axis_index("rep")


def placed(spec):
    if spec.index_map is None:
        return spec
    return pl.BlockSpec(spec.block_shape, lambda *ids: spec.index_map(*ids, position()))


def grid_spec(grid, in_specs, out_specs):
    specs = out_specs if isinstance(out_specs, list) else [out_specs]
    specs = [placed(x) for x in specs]
    return pl.GridSpec(
        grid=grid,
        in_specs=[placed(x) for x in in_specs],
        out_specs=specs if isinstance(out_specs, list) else specs[0],
    )


def params(mib=48):
    return pltpu.CompilerParams(vmem_limit_bytes=mib * 2**20)


def sds(shape, dtype=BF16):
    return jax.ShapeDtypeStruct(shape, dtype)


def in_hbm(shape, dtype=BF16):
    return pltpu.HBM(shape, dtype)


def pin(*arrays):
    return [pltpu.with_memory_space_constraint(x, pltpu.HBM) for x in arrays]


TOKEN = in_hbm((8, 128), F32)


def select_kernel(by_shift, by_target, n_rep, cap, pool_dev, rank, slot, lists, pool, *rest):
    token, idx = rest[-2:]
    outs = rest[-2 - n_rep * len(by_shift) - len(by_target) : -2]
    token[...] = jnp.zeros_like(token)
    me = lax.axis_index("rep")
    for shift in range(n_rep):
        target = lax.rem(me + shift, n_rep)
        for k in range(cap):
            idx[k] = 0

        def body(l, count):
            place = slot[lists[target, l]]
            mine = (place // pool_dev == me) & (count < cap)

            @pl.when(mine)
            def _():
                idx[count] = place - me * pool_dev

            return count + mine.astype(jnp.int32)

        lax.fori_loop(0, lists.shape[1], body, jnp.int32(0), unroll=True)
        for k in range(cap):
            entry = idx[k]
            rows = pl.ds(k * rank, rank)
            for c, (start, stop) in enumerate(by_shift):
                outs[c * n_rep + shift][rows, :] = pool[entry, :, start:stop]
            for c, (start, stop) in enumerate(by_target):
                outs[len(by_shift) * n_rep + c][target, rows, :] = pool[entry, :, start:stop]


def select(slot, lists, pool, by_shift, by_target, n_rep, cap, after=()):
    pool_dev, rank, width = pool.shape
    shapes = [in_hbm((cap * rank, stop - start)) for start, stop in by_shift for _ in range(n_rep)]
    shapes += [in_hbm((n_rep, cap * rank, stop - start)) for start, stop in by_target]
    return pl.pallas_call(
        functools.partial(select_kernel, by_shift, by_target, n_rep, cap, pool_dev, rank),
        out_shape=[*shapes, TOKEN],
        in_specs=[SMEM, SMEM, VMEM] + [ANY] * len(after),
        out_specs=[VMEM] * len(shapes) + [VMEM],
        scratch_shapes=[pltpu.SMEM((cap,), jnp.int32)],
        compiler_params=params(16),
        cost_estimate=order(0),
        name="select",
    )(*pin(slot, lists, pool), *pin(*after))


def product_early_kernel(per, pos, features, weights, keep0, send0, keep1, send1, token):
    token[...] = jnp.zeros_like(token)
    j = pl.program_id(0)
    own = features.shape[0] // 2
    result = jnp.dot(features[...], weights[...], preferred_element_type=F32).astype(BF16)
    for core in range(2):
        a, b = core * own, (1 - core) * own
        for block, keep, send in ((0, keep0, send0), (1, keep1, send1)):

            @pl.when((pos[1] == core) & (j // per == block))
            def _():
                keep[...] = result[a : a + own]
                send[...] = result[b : b + own]


def product_early(features, projection, tile, after=()):
    rows, depth = features.shape
    width = projection.shape[1] // 4
    half = rows // 2
    per = width // tile

    def kernel(features, weights, *rest):
        product_early_kernel(per, position(), features, weights, *rest[-5:])

    low = pl.BlockSpec((half // 2, tile), lambda j, pos: (0, jnp.minimum(j, per - 1)))
    high = pl.BlockSpec((half // 2, tile), lambda j, pos: (0, jnp.maximum(j - per, 0)))
    return pl.pallas_call(
        kernel,
        out_shape=[sds((half // 2, width))] * 4 + [TOKEN],
        grid_spec=grid_spec(
            grid=(2 * per,),
            in_specs=[
                pl.BlockSpec((half, depth), lambda j, pos: (1 - pos[0], 0)),
                pl.BlockSpec((depth, tile), lambda j, pos: (0, 2 * (1 - pos[0]) * per + j)),
            ]
            + [ANY] * len(after),
            out_specs=[low, low, high, high, pl.BlockSpec((8, 128), lambda j, pos: (0, 0))],
        ),
        compiler_params=params(),
        cost_estimate=order(0),
        name="product",
    )(features, projection, *pin(*after))


def product_columns_kernel(per, pos, features, weights, late, late_send, keep, send, token):
    token[...] = jnp.zeros_like(token)
    j = pl.program_id(0)
    half = features.shape[0] // 2
    own = half // 2
    result = jnp.dot(features[...], weights[...], preferred_element_type=F32).astype(BF16)
    for chip in range(2):
        here = pos[0] == chip
        other = result[(1 - chip) * half : (2 - chip) * half]

        @pl.when(here & (j < per))
        def _():
            late[...] = other

        @pl.when(here & (j >= per))
        def _():
            late_send[...] = other

        for core in range(2):

            @pl.when(here & (pos[1] == core))
            def _():
                keep[...] = result[chip * half + core * own : chip * half + (core + 1) * own][None]
                send[...] = result[chip * half + (1 - core) * own : chip * half + (2 - core) * own][None]


def product_columns(features, projection, tile, after=()):
    rows, depth = features.shape
    width = projection.shape[1] // 4
    half = rows // 2
    per = width // tile

    def block(j, pos):
        return jnp.where(j < per, pos[1], 1 - pos[1])

    rest = pl.BlockSpec((1, half // 2, tile), lambda j, pos: (block(j, pos), 0, lax.rem(j, per)))

    def kernel(features, weights, *rest):
        product_columns_kernel(per, position(), features, weights, *rest[-5:])

    return pl.pallas_call(
        kernel,
        out_shape=[in_hbm((half, width))] * 2 + [in_hbm((2, half // 2, width))] * 2 + [TOKEN],
        grid_spec=grid_spec(
            grid=(2 * per,),
            in_specs=[
                pl.BlockSpec((rows, depth), lambda j, pos: (0, 0)),
                pl.BlockSpec((depth, tile), lambda j, pos: (0, (2 * pos[0] + block(j, pos)) * per + lax.rem(j, per))),
            ]
            + [ANY] * len(after),
            out_specs=[
                pl.BlockSpec((half, tile), lambda j, pos: (0, jnp.minimum(j, per - 1))),
                pl.BlockSpec((half, tile), lambda j, pos: (0, jnp.maximum(j - per, 0))),
                rest,
                rest,
                pl.BlockSpec((8, 128), lambda j, pos: (0, 0)),
            ],
        ),
        compiler_params=params(),
        cost_estimate=order(0),
        name="product",
    )(features, projection, *pin(*after))


def product_kernel(split, pos, features, weights, keep, send, token):
    token[...] = jnp.zeros_like(token)
    own = features.shape[0] // 2
    result = jnp.dot(features[...], weights[...], preferred_element_type=F32).astype(BF16)
    low, high = result[:own], result[own:]
    if split:
        low, high = low[None], high[None]

    @pl.when(pos[1] == 0)
    def _():
        keep[...] = low
        send[...] = high

    @pl.when(pos[1] == 1)
    def _():
        keep[...] = high
        send[...] = low


def product(features, projection, other_rows, other_cols, first, count, tile, blocks, after=()):
    rows, depth = features.shape
    width = projection.shape[1]
    half = rows // 2
    own = half // 2
    tiles = count // tile

    def row_block(j, pos):
        return ((1 - pos[0]) if other_rows else pos[0], 0)

    def col_block(j, pos):
        if other_cols is None:
            return (0, j + first // tile)
        chip = (1 - pos[0]) if other_cols else pos[0]
        return (0, chip * (width // 2 // tile) + j + first // tile)

    if blocks > 1:
        per = tiles // blocks
        shape = (blocks, own, count // blocks)
        out_spec = pl.BlockSpec((1, own, tile), lambda j, pos: (j // per, 0, j % per))
    else:
        shape = (own, count)
        out_spec = pl.BlockSpec((own, tile), lambda j, pos: (0, j))
    body = functools.partial(product_kernel, blocks > 1)

    def kernel(features, weights, *rest):
        body(position(), features, weights, *rest[-3:])

    return pl.pallas_call(
        kernel,
        out_shape=[in_hbm(shape) if blocks > 1 else sds(shape)] * 2 + [TOKEN],
        grid_spec=grid_spec(
            grid=(tiles,),
            in_specs=[pl.BlockSpec((half, depth), row_block), pl.BlockSpec((depth, tile), col_block)]
            + [ANY] * len(after),
            out_specs=[out_spec] * 2 + [pl.BlockSpec((8, 128), lambda j, pos: (0, 0))],
        ),
        compiler_params=params(),
        cost_estimate=order(0),
        name="product",
    )(features, projection, *pin(*after))


def walk_list(slot, lists, me, n_rep, cap, pool_dev, counts, by_owner, visit):
    for s in range(n_rep):
        counts[s] = 0

    for l in range(lists.shape[1]):
        variant = lists[me, l]
        owner = slot[variant] // pool_dev
        group = owner if by_owner else lax.rem(me - owner + n_rep, n_rep)
        k = counts[group]
        counts[group] = k + 1
        visit(variant, group * cap + jnp.minimum(k, cap - 1))


def score_kernel(n_rep, cap, pool_dev, rank, slot, lists, wanted, features, factors, *rest):
    out, scores, counts = rest[-3:]
    scores[...] = lax.dot_general(
        factors[...], features[...], (((1,), (1,)), ((), ())), preferred_element_type=F32
    )
    out[...] = jnp.zeros_like(out)

    def visit(variant, place):
        offset = pl.multiple_of(place * rank, rank)
        out[...] += jnp.where(wanted[...] == variant, scores[pl.ds(offset, rank), :], 0.0)

    walk_list(slot, lists, position()[2], n_rep, cap, pool_dev, counts, True, visit)


def score(slot, lists, wanted, features, factors, n_rep, cap, pool_dev, rank, after=()):
    rows = features.shape[0]
    return pl.pallas_call(
        functools.partial(score_kernel, n_rep, cap, pool_dev, rank),
        out_shape=sds((rank, rows), F32),
        in_specs=[SMEM] * 2 + [VMEM] * 3 + [ANY] * len(after),
        out_specs=VMEM,
        scratch_shapes=[
            pltpu.VMEM((n_rep * cap * rank, rows), F32),
            pltpu.SMEM((n_rep,), jnp.int32),
        ],
        compiler_params=params(),
        cost_estimate=order(40),
        name="score",
    )(*pin(slot, lists, wanted), features, *pin(factors), *pin(*after))


def delta_kernel(
    n_blocks, n_rep, cap, pool_dev, rank, n_before, slot, lists, wanted, shrunk, late_own, late_recv, *rest
):
    blocks, before = rest[:n_blocks], rest[n_blocks : n_blocks + n_before]
    straight, cross, mine, send, spread, expand, result, variants, counts = rest[-9:]
    size = n_rep * cap * rank // n_blocks
    own, width = straight.shape
    for i in range(n_rep * cap):
        variants[i] = -1

    def visit(variant, place):
        variants[place] = variant

    walk_list(slot, lists, position()[2], n_rep, cap, pool_dev, counts, n_blocks == 1, visit)
    total = jnp.sum(shrunk[...], axis=0).astype(BF16).astype(F32)
    for i in range(n_rep * cap):
        spread[pl.ds(i * rank, rank), :] = jnp.where(wanted[...] == variants[i], total, 0.0).astype(BF16)
    for s in range(n_blocks):
        expand[pl.ds(s * size, size), :] = blocks[s][...]
    result[...] = lax.dot_general(
        spread[...], expand[...], (((0,), (0,)), ((), ())), preferred_element_type=F32
    )
    chip, core, _ = position()
    for out, c in ((straight, core), (cross, 1 - core)):
        rows = pl.ds(pl.multiple_of(c * own, own), own)
        base = late_own[rows, :].astype(F32) + late_recv[rows, :].astype(F32)
        out[...] = (base + result[pl.ds((2 - 2 * chip + c) * own, own), :]).astype(BF16)
    start = mine.shape[1] - width
    if before:
        mine[:, :start] = before[0][...]
        send[:, :start] = before[1][...]
    mine[:, start:] = result[pl.ds((2 * chip + core) * own, own), :].astype(BF16)
    send[:, start:] = result[pl.ds((2 * chip + 1 - core) * own, own), :].astype(BF16)


def delta(slot, lists, wanted, shrunk, late, blocks, cut, n_rep, cap, pool_dev, rank, own, before=(), after=()):
    rows = wanted.shape[1]
    start, stop = cut
    width = stop - start
    return pl.pallas_call(
        functools.partial(delta_kernel, len(blocks), n_rep, cap, pool_dev, rank, len(before)),
        out_shape=[in_hbm((own, width))] * 2 + [in_hbm((own, stop))] * 2,
        grid=(1,),
        in_specs=[SMEM] * 2
        + [VMEM] * 2
        + [pl.BlockSpec((2 * own, width), lambda i: (0, start // width))] * 2
        + [VMEM] * (len(blocks) + len(before))
        + [ANY] * len(after),
        out_specs=[VMEM] * 4,
        scratch_shapes=[
            pltpu.VMEM((n_rep * cap * rank, rows), BF16),
            pltpu.VMEM((n_rep * cap * rank, width), BF16),
            pltpu.VMEM((rows, width), F32),
            pltpu.SMEM((n_rep * cap,), jnp.int32),
            pltpu.SMEM((n_rep,), jnp.int32),
        ],
        compiler_params=params(),
        cost_estimate=order(0),
        name="delta",
    )(*pin(slot, lists, wanted), shrunk, *pin(late[0]), late[1], *pin(blocks[0]), *blocks[1:], *pin(*before), *pin(*after))


def gate_kernel(*refs):
    pass


def gate(arrays, after):
    n = len(arrays)
    return pl.pallas_call(
        gate_kernel,
        out_shape=[sds(x.shape, x.dtype) for x in arrays],
        in_specs=[ANY] * (n + len(after)),
        out_specs=[ANY] * n,
        input_output_aliases={i: i for i in range(n)},
        cost_estimate=order(100),
        name="gate",
    )(*arrays, *pin(*after))


def near_kernel(residual, keep, recv, first, second, mine, theirs, *rest):
    out = rest[-1]
    block = pl.program_id(0)
    total = residual[...].astype(F32) + keep[0].astype(F32) + recv[0].astype(F32)
    total += jnp.where(block == 0, first[...], second[...]).astype(F32)
    total += jnp.where(block == position()[1], mine[...], theirs[...]).astype(F32)
    out[...] = total.astype(BF16)


def far_kernel(residual, keep, recv, straight, cross, *rest):
    out = rest[-1]
    total = residual[...].astype(F32) + keep[0].astype(F32) + recv[0].astype(F32)
    total += jnp.where(pl.program_id(0) == position()[1], straight[...], cross[...]).astype(F32)
    out[...] = total.astype(BF16)


def finish(out, residual, base, start, stop, near, pieces, after=()):
    own, full = residual.shape
    width = full // 4
    size = stop - start
    tile = min(TILE, math.gcd(size, start, width))
    count = size // tile
    skip = start // tile

    def place(b, j, pos):
        chip = pos[0] if near else 1 - pos[0]
        return (0, (2 * chip + b) * (width // tile) + skip + j)

    whole = pl.BlockSpec((own, tile), place)
    halves = [
        lambda b, j, pos: (0, skip + jnp.where(b == 0, j, count - 1)),
        lambda b, j, pos: (0, skip + jnp.where(b == 1, j, 0)),
    ]
    by_block = [pl.BlockSpec((own, tile), f) for f in halves]

    def by_core(offset):
        def index(b, j, pos):
            half = pos[1] ^ offset
            return (0, jnp.where(b == half, j, jnp.where(half == 0, count - 1, 0)))

        return pl.BlockSpec((own, tile), index)

    part = pl.BlockSpec((1, own, tile), lambda b, j, pos: (b, 0, skip + j))
    specs = [part, part, *(by_block if near else []), by_core(0), by_core(1)]
    specs = specs + [ANY] * len(after)
    operands = [*pin(residual, *base), *pieces, *pin(*after)]
    aliases = {}
    if out is not None:
        specs = specs + [ANY]
        aliases = {len(operands): 0}
        operands.append(out)
    return pl.pallas_call(
        near_kernel if near else far_kernel,
        out_shape=sds((own, full)),
        grid_spec=grid_spec(
            grid=(2, count),
            in_specs=[whole, *specs],
            out_specs=whole,
        ),
        input_output_aliases=aliases,
        compiler_params=params(),
        cost_estimate=order(60),
        name="near" if near else "far",
    )(*operands)


def paired(
    head_outputs, residual, projection, shrink_pool, expand_pool, pool_slot, variant_list, request_variant
):
    n_rep = lax.axis_size("rep")
    features = head_outputs[0]
    rows = features.shape[0]
    own = rows // 4
    pool_dev, rank, width = shrink_pool.shape
    cap = pool_dev // 4 + 2
    stream = residual[0]
    lists = (pool_slot, variant_list)
    sizes = (cap, pool_dev, rank)
    tile = min(1024, width)
    cut = width // 2
    cuts = ((0, cut), (cut, width))

    def over_core(x):
        return lax.ppermute(x, "tp", [(0, 1), (1, 0), (2, 3), (3, 2)])

    def over_chip(x):
        return lax.ppermute(x, "tp", [(0, 2), (2, 0), (1, 3), (3, 1)])

    def over_both(x):
        return lax.ppermute(x, "tp", [(0, 3), (3, 0), (1, 2), (2, 1)])

    def over_rep(x, shift):
        return lax.ppermute(x, "rep", [(i, (i + shift) % n_rep) for i in range(n_rep)])

    shifts = [s for s in range(1, n_rep) if s != n_rep // 2] + [n_rep // 2]
    chosen, token = select(pool_slot, variant_list, shrink_pool, (), ((0, width),), n_rep, cap)
    shrink = lax.all_to_all(chosen, "rep", 0, 0, tiled=True).reshape(n_rep * cap * rank, width)

    keep0, send0, keep1, send1, token = product_early(features, projection, tile, [token])
    sums = [keep0 + over_core(send0), keep1 + over_core(send1)]
    early = [over_chip(x) for x in sums]

    *chosen, second, token = select(pool_slot, variant_list, expand_pool, cuts[:1], cuts[1:], n_rep, cap, sums)
    first = [chosen[0]] + [None] * (n_rep - 1)
    for s in shifts:
        first[s] = over_rep(chosen[s], s)
    second = lax.all_to_all(second, "rep", 0, 0, tiled=True).reshape(n_rep * cap * rank, cut)

    late_keep, late_send, keep, send, token = product_columns(features, projection, tile, [*sums, token])
    late = (late_keep, over_core(late_send))
    near_base = (keep, over_core(send))

    part = score(*lists, request_variant, features, shrink, n_rep, *sizes, [token, early[0]])
    shrunk = lax.all_gather(part, "tp")

    common = (*lists, request_variant, shrunk, late)
    straight, cross, *before = delta(*common, first, cuts[0], n_rep, *sizes, own, (), [early[1]])
    far = [over_chip(straight), over_both(cross)]
    straight, cross, mine, send = delta(*common, [second], cuts[1], n_rep, *sizes, own, before, [near_base[1]])
    last = [over_chip(straight), over_both(cross)]
    theirs = over_core(send)
    keep, send, token = product(features, projection, False, True, 0, 2 * width, tile, 2, [mine])
    far_base = (keep, over_core(send))
    far = gate(far, [token])
    out = finish(None, stream, near_base, 0, width, True, [*early, mine, theirs], far)
    out = finish(out, stream, far_base, *cuts[0], False, far)
    out = finish(out, stream, far_base, *cuts[1], False, last)
    return out[None]


def general(
    head_outputs, residual, projection, shrink_pool, expand_pool, pool_slot, variant_list, request_variant
):
    split_count = lax.axis_size("tp")
    split_index = lax.axis_index("tp")
    replica_index = lax.axis_index("rep")
    row_count = head_outputs.shape[1]
    local_width = head_outputs.shape[2]
    rank_size = shrink_pool.shape[1]
    listed = variant_list.shape[1]
    own_rows = row_count // split_count
    flat_size = rank_size * local_width
    features = head_outputs[0]
    wanted = request_variant[0]
    my_list = lax.dynamic_index_in_dim(variant_list, replica_index, 0, keepdims=False)
    my_positions = jnp.take(pool_slot, my_list, axis=0)
    pieces = (
        lax.all_gather(shrink_pool, "rep", axis=0, tiled=True),
        lax.all_gather(expand_pool, "rep", axis=0, tiled=True),
    )
    piece_rows = pieces[0].shape[0]
    matches = (my_positions[:, None] == jnp.arange(piece_rows, dtype=jnp.int32)[None, :]).astype(BF16)
    shrink_sel = jnp.dot(matches, pieces[0].reshape(piece_rows, flat_size), preferred_element_type=F32)
    expand_sel = jnp.dot(matches, pieces[1].reshape(piece_rows, flat_size), preferred_element_type=F32)
    shrink_sel = shrink_sel.astype(BF16).reshape(listed * rank_size, local_width)
    expand_sel = expand_sel.astype(BF16).reshape(listed, rank_size, local_width)
    member = wanted[:, None] == my_list[None, :]
    scores = lax.dot_general(
        features, shrink_sel, (((1,), (1,)), ((), ())), preferred_element_type=F32
    )
    shrunk = jnp.sum(scores.reshape(row_count, listed, rank_size) * member[:, :, None], axis=1)
    own_shrunk = lax.psum_scatter(shrunk.astype(BF16), "tp", scatter_dimension=0, tiled=True)
    own_member = lax.dynamic_slice_in_dim(member, split_index * own_rows, own_rows, 0)
    spread = own_member[:, :, None] * own_shrunk[:, None, :]
    spread = spread.reshape(own_rows, listed * rank_size)
    piece = lax.all_gather(expand_sel, "tp", axis=2, tiled=True)
    delta_rows = jnp.dot(
        spread, piece.reshape(listed * rank_size, piece.shape[2]), preferred_element_type=F32
    )
    base_rows = lax.psum_scatter(
        jnp.dot(features, projection, preferred_element_type=F32).astype(BF16),
        "tp",
        scatter_dimension=0,
        tiled=True,
    ).astype(F32)
    return (residual[0].astype(F32) + base_rows + delta_rows).astype(BF16)[None]


def solution(mesh):
    in_specs = (
        P(("groups", "rep"), None, "tp"),
        P(("groups", "rep"), "tp", None),
        P("tp", None),
        P(("groups", "rep"), None, "tp"),
        P(("groups", "rep"), None, "tp"),
        P("groups"),
        P("groups", None),
        P(("groups", "rep"), None),
    )
    out_specs = P(("groups", "rep"), "tp", None)
    local = paired if mesh.shape["tp"] == 4 else general
    return jax.shard_map(local, mesh=mesh, in_specs=in_specs, out_specs=out_specs, check_vma=False)
```

```python
import functools
import math

import jax
import jax.numpy as jnp
from jax import lax
from jax.experimental import pallas as pl
from jax.experimental.pallas import tpu as pltpu
from jax.sharding import PartitionSpec as P

ANY = pl.BlockSpec(memory_space=pl.ANY)
HBM = pl.BlockSpec(memory_space=pltpu.HBM)
SMEM = pl.BlockSpec(memory_space=pltpu.SMEM)
VMEM = pl.BlockSpec(memory_space=pltpu.VMEM)
BF16 = jnp.bfloat16
F32 = jnp.float32
TILE = 1024


def order(us):
    return pl.CostEstimate(flops=int(us * 1.15e9) + 1, bytes_accessed=1, transcendentals=0)


def position():
    index = lax.axis_index("tp")
    return lax.div(index, 2), lax.rem(index, 2), lax.axis_index("rep")


def placed(spec):
    if spec.index_map is None:
        return spec
    return pl.BlockSpec(spec.block_shape, lambda *ids: spec.index_map(*ids, position()))


def grid_spec(grid, in_specs, out_specs):
    specs = out_specs if isinstance(out_specs, list) else [out_specs]
    specs = [placed(x) for x in specs]
    return pl.GridSpec(
        grid=grid,
        in_specs=[placed(x) for x in in_specs],
        out_specs=specs if isinstance(out_specs, list) else specs[0],
    )


def params(mib=48):
    return pltpu.CompilerParams(vmem_limit_bytes=mib * 2**20)


def sds(shape, dtype=BF16):
    return jax.ShapeDtypeStruct(shape, dtype)


def in_hbm(shape, dtype=BF16):
    return pltpu.HBM(shape, dtype)


def pin(*arrays):
    return [pltpu.with_memory_space_constraint(x, pltpu.HBM) for x in arrays]


TOKEN = in_hbm((8, 128), F32)


def select_kernel(by_shift, by_target, named, n_rep, cap, pool_dev, rank, slot, lists, pool, *rest):
    token, idx, counts = rest[-3:]
    outs = rest[: -3]
    outs = outs[-(n_rep * len(by_shift) + len(by_target) + named) :]
    token[...] = jnp.zeros_like(token)
    me = lax.axis_index("rep")
    base = me * pool_dev
    for shift in range(n_rep):
        target = lax.rem(me + shift, n_rep)
        for k in range(cap + 1):
            idx[k] = 0
        count = jnp.int32(0)
        for l in range(lists.shape[1]):
            place = slot[lists[target, l]] - base
            idx[jnp.minimum(count, cap)] = place
            count = count + jnp.where((place >= 0) & (place < pool_dev), 1, 0)
        for k in range(cap):
            entry = jnp.clip(idx[k], 0, pool_dev - 1)
            rows = pl.ds(k * rank, rank)
            for c, (start, stop) in enumerate(by_shift):
                outs[c * n_rep + shift][rows, :] = pool[entry, :, start:stop]
            for c, (start, stop) in enumerate(by_target):
                outs[len(by_shift) * n_rep + c][target, rows, :] = pool[entry, :, start:stop]
    if named:
        names = outs[-1]
        for i in range(n_rep * cap):
            names[i] = -1
        for s in range(n_rep):
            counts[s] = 0
        for l in range(lists.shape[1]):
            variant = lists[me, l]
            owner = slot[variant] // pool_dev
            k = counts[owner]
            counts[owner] = k + 1
            names[owner * cap + jnp.minimum(k, cap - 1)] = variant


def select(slot, lists, pool, by_shift, by_target, named, n_rep, cap, after=()):
    pool_dev, rank, width = pool.shape
    shapes = [in_hbm((cap * rank, stop - start)) for start, stop in by_shift for _ in range(n_rep)]
    shapes += [in_hbm((n_rep, cap * rank, stop - start)) for start, stop in by_target]
    specs = [VMEM] * len(shapes)
    if named:
        shapes.append(in_hbm((n_rep * cap,), jnp.int32))
        specs.append(SMEM)
    return pl.pallas_call(
        functools.partial(select_kernel, by_shift, by_target, int(named), n_rep, cap, pool_dev, rank),
        out_shape=[*shapes, TOKEN],
        in_specs=[SMEM, SMEM, VMEM] + [ANY] * len(after),
        out_specs=[*specs, VMEM],
        scratch_shapes=[pltpu.SMEM((cap + 1,), jnp.int32), pltpu.SMEM((n_rep,), jnp.int32)],
        compiler_params=params(16),
        cost_estimate=order(0),
        name="select",
    )(*pin(slot, lists, pool), *pin(*after))


def product_early_kernel(per, pos, features, weights, keep0, send0, keep1, send1, token):
    token[...] = jnp.zeros_like(token)
    j = pl.program_id(0)
    own = features.shape[0] // 2
    result = jnp.dot(features[...], weights[...], preferred_element_type=F32).astype(BF16)
    for core in range(2):
        a, b = core * own, (1 - core) * own
        for block, keep, send in ((0, keep0, send0), (1, keep1, send1)):

            @pl.when((pos[1] == core) & (j // per == block))
            def _():
                keep[...] = result[a : a + own]
                send[...] = result[b : b + own]


def product_early(features, projection, tile, after=()):
    rows, depth = features.shape
    width = projection.shape[1] // 4
    half = rows // 2
    per = width // tile

    def kernel(features, weights, *rest):
        product_early_kernel(per, position(), features, weights, *rest[-5:])

    low = pl.BlockSpec((half // 2, tile), lambda j, pos: (0, jnp.minimum(j, per - 1)))
    high = pl.BlockSpec((half // 2, tile), lambda j, pos: (0, jnp.maximum(j - per, 0)))
    return pl.pallas_call(
        kernel,
        out_shape=[sds((half // 2, width))] * 4 + [TOKEN],
        grid_spec=grid_spec(
            grid=(2 * per,),
            in_specs=[
                pl.BlockSpec((half, depth), lambda j, pos: (1 - pos[0], 0)),
                pl.BlockSpec((depth, tile), lambda j, pos: (0, 2 * (1 - pos[0]) * per + j)),
            ]
            + [ANY] * len(after),
            out_specs=[low, low, high, high, pl.BlockSpec((8, 128), lambda j, pos: (0, 0))],
        ),
        compiler_params=params(),
        cost_estimate=order(0),
        name="product",
    )(features, projection, *pin(*after))


def product_columns_kernel(per, pos, features, weights, late, late_send, keep, send, token):
    token[...] = jnp.zeros_like(token)
    j = pl.program_id(0)
    half = features.shape[0] // 2
    own = half // 2
    result = jnp.dot(features[...], weights[...], preferred_element_type=F32).astype(BF16)
    for chip in range(2):
        here = pos[0] == chip
        other = result[(1 - chip) * half : (2 - chip) * half]

        @pl.when(here & (j < per))
        def _():
            late[...] = other

        @pl.when(here & (j >= per))
        def _():
            late_send[...] = other

        for core in range(2):

            @pl.when(here & (pos[1] == core))
            def _():
                keep[...] = result[chip * half + core * own : chip * half + (core + 1) * own][None]
                send[...] = result[chip * half + (1 - core) * own : chip * half + (2 - core) * own][None]


def product_columns(features, projection, tile, after=()):
    rows, depth = features.shape
    width = projection.shape[1] // 4
    half = rows // 2
    per = width // tile

    def block(j, pos):
        return jnp.where(j < per, pos[1], 1 - pos[1])

    rest = pl.BlockSpec((1, half // 2, tile), lambda j, pos: (block(j, pos), 0, lax.rem(j, per)))

    def kernel(features, weights, *rest):
        product_columns_kernel(per, position(), features, weights, *rest[-5:])

    return pl.pallas_call(
        kernel,
        out_shape=[in_hbm((half, width))] * 2 + [in_hbm((2, half // 2, width))] * 2 + [TOKEN],
        grid_spec=grid_spec(
            grid=(2 * per,),
            in_specs=[
                pl.BlockSpec((rows, depth), lambda j, pos: (0, 0)),
                pl.BlockSpec((depth, tile), lambda j, pos: (0, (2 * pos[0] + block(j, pos)) * per + lax.rem(j, per))),
            ]
            + [ANY] * len(after),
            out_specs=[
                pl.BlockSpec((half, tile), lambda j, pos: (0, jnp.minimum(j, per - 1))),
                pl.BlockSpec((half, tile), lambda j, pos: (0, jnp.maximum(j - per, 0))),
                rest,
                rest,
                pl.BlockSpec((8, 128), lambda j, pos: (0, 0)),
            ],
        ),
        compiler_params=params(),
        cost_estimate=order(0),
        name="product",
    )(features, projection, *pin(*after))


def product_kernel(split, pos, features, weights, keep, send, token):
    token[...] = jnp.zeros_like(token)
    own = features.shape[0] // 2
    result = jnp.dot(features[...], weights[...], preferred_element_type=F32).astype(BF16)
    low, high = result[:own], result[own:]
    if split:
        low, high = low[None], high[None]

    @pl.when(pos[1] == 0)
    def _():
        keep[...] = low
        send[...] = high

    @pl.when(pos[1] == 1)
    def _():
        keep[...] = high
        send[...] = low


def product(features, projection, other_rows, other_cols, first, count, tile, blocks, after=()):
    rows, depth = features.shape
    width = projection.shape[1]
    half = rows // 2
    own = half // 2
    tiles = count // tile

    def row_block(j, pos):
        return ((1 - pos[0]) if other_rows else pos[0], 0)

    def col_block(j, pos):
        if other_cols is None:
            return (0, j + first // tile)
        chip = (1 - pos[0]) if other_cols else pos[0]
        return (0, chip * (width // 2 // tile) + j + first // tile)

    if blocks > 1:
        per = tiles // blocks
        shape = (blocks, own, count // blocks)
        out_spec = pl.BlockSpec((1, own, tile), lambda j, pos: (j // per, 0, j % per))
    else:
        shape = (own, count)
        out_spec = pl.BlockSpec((own, tile), lambda j, pos: (0, j))
    body = functools.partial(product_kernel, blocks > 1)

    def kernel(features, weights, *rest):
        body(position(), features, weights, *rest[-3:])

    return pl.pallas_call(
        kernel,
        out_shape=[in_hbm(shape) if blocks > 1 else sds(shape)] * 2 + [TOKEN],
        grid_spec=grid_spec(
            grid=(tiles,),
            in_specs=[pl.BlockSpec((half, depth), row_block), pl.BlockSpec((depth, tile), col_block)]
            + [ANY] * len(after),
            out_specs=[out_spec] * 2 + [pl.BlockSpec((8, 128), lambda j, pos: (0, 0))],
        ),
        compiler_params=params(),
        cost_estimate=order(0),
        name="product",
    )(features, projection, *pin(*after))


def score_kernel(rank, names, wanted, features, factors, *rest):
    out, scores = rest[-2:]
    scores[...] = lax.dot_general(
        factors[...], features[...], (((1,), (1,)), ((), ())), preferred_element_type=F32
    )
    total = jnp.zeros(out.shape, F32)
    for i in range(factors.shape[0] // rank):
        total += jnp.where(wanted[...] == names[i], scores[i * rank : (i + 1) * rank, :], 0.0)
    out[...] = total


def score(names, wanted, features, factors, rank, after=()):
    rows = features.shape[0]
    return pl.pallas_call(
        functools.partial(score_kernel, rank),
        out_shape=sds((rank, rows), F32),
        in_specs=[SMEM] + [VMEM] * 3 + [ANY] * len(after),
        out_specs=VMEM,
        scratch_shapes=[pltpu.VMEM((factors.shape[0], rows), F32)],
        compiler_params=params(),
        cost_estimate=order(40),
        name="score",
    )(*pin(names, wanted), features, *pin(factors), *pin(*after))


def delta_kernel(n_blocks, n_rep, cap, rank, n_before, names, wanted, shrunk, late_own, late_recv, *rest):
    blocks, before = rest[:n_blocks], rest[n_blocks : n_blocks + n_before]
    straight, cross, mine, send, member, expand, result = rest[-7:]
    chip, core, me = position()
    listed = n_rep * cap
    size = listed * rank // n_blocks
    own, width = straight.shape
    member[...] = jnp.zeros_like(member)
    for i in range(listed):
        if n_blocks == 1:
            name = names[i]
        else:
            name = names[lax.rem(me - i // cap + n_rep, n_rep) * cap + i % cap]
        member[i : i + 1, :] = jnp.where(wanted[...] == name, 1.0, 0.0)
    total = jnp.sum(shrunk[...], axis=0).astype(BF16)
    entry = lax.broadcasted_iota(jnp.int32, (member.shape[0], listed * rank), 0)
    column = lax.broadcasted_iota(jnp.int32, (member.shape[0], listed * rank), 1)
    to_entry = jnp.where(column // rank == entry, 1.0, 0.0).astype(BF16)
    part = lax.broadcasted_iota(jnp.int32, (rank, listed * rank), 0)
    column = lax.broadcasted_iota(jnp.int32, (rank, listed * rank), 1)
    to_part = jnp.where(lax.rem(column, rank) == part, 1.0, 0.0).astype(BF16)
    turned = (((0,), (0,)), ((), ()))
    named = lax.dot_general(member[...].astype(BF16), to_entry, turned, preferred_element_type=F32)
    copied = lax.dot_general(total, to_part, turned, preferred_element_type=F32)
    spread = (named * copied).astype(BF16)
    for s in range(n_blocks):
        expand[pl.ds(s * size, size), :] = blocks[s][...]
    result[...] = jnp.dot(spread, expand[...], preferred_element_type=F32)
    for out, c in ((straight, core), (cross, 1 - core)):
        rows = pl.ds(pl.multiple_of(c * own, own), own)
        base = late_own[rows, :].astype(F32) + late_recv[rows, :].astype(F32)
        out[...] = (base + result[pl.ds((2 - 2 * chip + c) * own, own), :]).astype(BF16)
    start = mine.shape[1] - width
    if before:
        mine[:, :start] = before[0][...]
        send[:, :start] = before[1][...]
    mine[:, start:] = result[pl.ds((2 * chip + core) * own, own), :].astype(BF16)
    send[:, start:] = result[pl.ds((2 * chip + 1 - core) * own, own), :].astype(BF16)


def delta(names, wanted, shrunk, late, blocks, cut, n_rep, cap, rank, own, before=(), after=()):
    rows = wanted.shape[1]
    start, stop = cut
    width = stop - start
    listed = n_rep * cap
    return pl.pallas_call(
        functools.partial(delta_kernel, len(blocks), n_rep, cap, rank, len(before)),
        out_shape=[in_hbm((own, width))] * 2 + [in_hbm((own, stop))] * 2,
        grid=(1,),
        in_specs=[SMEM]
        + [VMEM] * 2
        + [pl.BlockSpec((2 * own, width), lambda i: (0, start // width))] * 2
        + [VMEM] * (len(blocks) + len(before))
        + [ANY] * len(after),
        out_specs=[VMEM] * 4,
        scratch_shapes=[
            pltpu.VMEM((-(-listed // 16) * 16, rows), F32),
            pltpu.VMEM((listed * rank, width), BF16),
            pltpu.VMEM((rows, width), F32),
        ],
        compiler_params=params(),
        cost_estimate=order(0),
        name="delta",
    )(*pin(names, wanted), shrunk, *pin(late[0]), late[1], *pin(blocks[0]), *blocks[1:], *pin(*before), *pin(*after))


def gate_kernel(*refs):
    pass


def gate(arrays, after):
    n = len(arrays)
    return pl.pallas_call(
        gate_kernel,
        out_shape=[sds(x.shape, x.dtype) for x in arrays],
        in_specs=[ANY] * (n + len(after)),
        out_specs=[ANY] * n,
        input_output_aliases={i: i for i in range(n)},
        cost_estimate=order(100),
        name="gate",
    )(*arrays, *pin(*after))


def near_kernel(residual, keep, recv, first, second, mine, theirs, *rest):
    out = rest[-1]
    block = pl.program_id(0)
    total = residual[...].astype(F32) + keep[0].astype(F32) + recv[0].astype(F32)
    total += jnp.where(block == 0, first[...], second[...]).astype(F32)
    total += jnp.where(block == position()[1], mine[...], theirs[...]).astype(F32)
    out[...] = total.astype(BF16)


def far_kernel(residual, keep, recv, straight, cross, *rest):
    out = rest[-1]
    total = residual[...].astype(F32) + keep[0].astype(F32) + recv[0].astype(F32)
    total += jnp.where(pl.program_id(0) == position()[1], straight[...], cross[...]).astype(F32)
    out[...] = total.astype(BF16)


def finish(out, residual, base, start, stop, near, pieces, after=()):
    own, full = residual.shape
    width = full // 4
    size = stop - start
    tile = min(TILE, math.gcd(size, start, width))
    count = size // tile
    skip = start // tile

    def place(b, j, pos):
        chip = pos[0] if near else 1 - pos[0]
        return (0, (2 * chip + b) * (width // tile) + skip + j)

    whole = pl.BlockSpec((own, tile), place)
    halves = [
        lambda b, j, pos: (0, skip + jnp.where(b == 0, j, count - 1)),
        lambda b, j, pos: (0, skip + jnp.where(b == 1, j, 0)),
    ]
    by_block = [pl.BlockSpec((own, tile), f) for f in halves]

    def by_core(offset):
        def index(b, j, pos):
            half = pos[1] ^ offset
            return (0, jnp.where(b == half, j, jnp.where(half == 0, count - 1, 0)))

        return pl.BlockSpec((own, tile), index)

    part = pl.BlockSpec((1, own, tile), lambda b, j, pos: (b, 0, skip + j))
    specs = [part, part, *(by_block if near else []), by_core(0), by_core(1)]
    specs = specs + [ANY] * len(after)
    operands = [*pin(residual, *base), *pieces, *pin(*after)]
    aliases = {}
    if out is not None:
        specs = specs + [ANY]
        aliases = {len(operands): 0}
        operands.append(out)
    return pl.pallas_call(
        near_kernel if near else far_kernel,
        out_shape=sds((own, full)),
        grid_spec=grid_spec(
            grid=(2, count),
            in_specs=[whole, *specs],
            out_specs=whole,
        ),
        input_output_aliases=aliases,
        compiler_params=params(),
        cost_estimate=order(60),
        name="near" if near else "far",
    )(*operands)


def paired(
    head_outputs, residual, projection, shrink_pool, expand_pool, pool_slot, variant_list, request_variant
):
    n_rep = lax.axis_size("rep")
    features = head_outputs[0]
    rows = features.shape[0]
    own = rows // 4
    pool_dev, rank, width = shrink_pool.shape
    cap = pool_dev // 4 + 2
    stream = residual[0]
    sizes = (cap, rank)
    tile = min(1024, width)
    cut = width // 2
    cuts = ((0, cut), (cut, width))

    def over_core(x):
        return lax.ppermute(x, "tp", [(0, 1), (1, 0), (2, 3), (3, 2)])

    def over_chip(x):
        return lax.ppermute(x, "tp", [(0, 2), (2, 0), (1, 3), (3, 1)])

    def over_both(x):
        return lax.ppermute(x, "tp", [(0, 3), (3, 0), (1, 2), (2, 1)])

    def over_rep(x, shift):
        return lax.ppermute(x, "rep", [(i, (i + shift) % n_rep) for i in range(n_rep)])

    shifts = [s for s in range(1, n_rep) if s != n_rep // 2] + [n_rep // 2]
    chosen, token = select(pool_slot, variant_list, shrink_pool, (), ((0, width),), False, n_rep, cap)
    shrink = lax.all_to_all(chosen, "rep", 0, 0, tiled=True).reshape(n_rep * cap * rank, width)

    keep0, send0, keep1, send1, token = product_early(features, projection, tile, [token])
    sums = [keep0 + over_core(send0), keep1 + over_core(send1)]
    early = [over_chip(x) for x in sums]

    *chosen, second, names, token = select(
        pool_slot, variant_list, expand_pool, cuts[:1], cuts[1:], True, n_rep, cap, sums
    )
    first = [chosen[0]] + [None] * (n_rep - 1)
    for s in shifts:
        first[s] = over_rep(chosen[s], s)
    second = lax.all_to_all(second, "rep", 0, 0, tiled=True).reshape(n_rep * cap * rank, cut)

    late_keep, late_send, keep, send, token = product_columns(features, projection, tile, [*sums, token])
    late = (late_keep, over_core(late_send))
    near_base = (keep, over_core(send))

    part = score(names, request_variant, features, shrink, rank, [token, early[0]])
    shrunk = lax.all_gather(part, "tp")

    common = (names, request_variant, shrunk, late)
    straight, cross, *before = delta(*common, first, cuts[0], n_rep, *sizes, own, (), [early[1]])
    far = [over_chip(straight), over_both(cross)]
    straight, cross, mine, send = delta(*common, [second], cuts[1], n_rep, *sizes, own, before, [near_base[1]])
    last = [over_chip(straight), over_both(cross)]
    theirs = over_core(send)
    keep, send, token = product(features, projection, False, True, 0, 2 * width, tile, 2, [mine])
    far_base = (keep, over_core(send))
    far = gate(far, [token])
    out = finish(None, stream, near_base, 0, width, True, [*early, mine, theirs], far)
    out = finish(out, stream, far_base, *cuts[0], False, far)
    out = finish(out, stream, far_base, *cuts[1], False, last)
    return out[None]


def general(
    head_outputs, residual, projection, shrink_pool, expand_pool, pool_slot, variant_list, request_variant
):
    split_count = lax.axis_size("tp")
    split_index = lax.axis_index("tp")
    replica_index = lax.axis_index("rep")
    row_count = head_outputs.shape[1]
    local_width = head_outputs.shape[2]
    rank_size = shrink_pool.shape[1]
    listed = variant_list.shape[1]
    own_rows = row_count // split_count
    flat_size = rank_size * local_width
    features = head_outputs[0]
    wanted = request_variant[0]
    my_list = lax.dynamic_index_in_dim(variant_list, replica_index, 0, keepdims=False)
    my_positions = jnp.take(pool_slot, my_list, axis=0)
    pieces = (
        lax.all_gather(shrink_pool, "rep", axis=0, tiled=True),
        lax.all_gather(expand_pool, "rep", axis=0, tiled=True),
    )
    piece_rows = pieces[0].shape[0]
    matches = (my_positions[:, None] == jnp.arange(piece_rows, dtype=jnp.int32)[None, :]).astype(BF16)
    shrink_sel = jnp.dot(matches, pieces[0].reshape(piece_rows, flat_size), preferred_element_type=F32)
    expand_sel = jnp.dot(matches, pieces[1].reshape(piece_rows, flat_size), preferred_element_type=F32)
    shrink_sel = shrink_sel.astype(BF16).reshape(listed * rank_size, local_width)
    expand_sel = expand_sel.astype(BF16).reshape(listed, rank_size, local_width)
    member = wanted[:, None] == my_list[None, :]
    scores = lax.dot_general(
        features, shrink_sel, (((1,), (1,)), ((), ())), preferred_element_type=F32
    )
    shrunk = jnp.sum(scores.reshape(row_count, listed, rank_size) * member[:, :, None], axis=1)
    own_shrunk = lax.psum_scatter(shrunk.astype(BF16), "tp", scatter_dimension=0, tiled=True)
    own_member = lax.dynamic_slice_in_dim(member, split_index * own_rows, own_rows, 0)
    spread = own_member[:, :, None] * own_shrunk[:, None, :]
    spread = spread.reshape(own_rows, listed * rank_size)
    piece = lax.all_gather(expand_sel, "tp", axis=2, tiled=True)
    delta_rows = jnp.dot(
        spread, piece.reshape(listed * rank_size, piece.shape[2]), preferred_element_type=F32
    )
    base_rows = lax.psum_scatter(
        jnp.dot(features, projection, preferred_element_type=F32).astype(BF16),
        "tp",
        scatter_dimension=0,
        tiled=True,
    ).astype(F32)
    return (residual[0].astype(F32) + base_rows + delta_rows).astype(BF16)[None]


def solution(mesh):
    in_specs = (
        P(("groups", "rep"), None, "tp"),
        P(("groups", "rep"), "tp", None),
        P("tp", None),
        P(("groups", "rep"), None, "tp"),
        P(("groups", "rep"), None, "tp"),
        P("groups"),
        P("groups", None),
        P(("groups", "rep"), None),
    )
    out_specs = P(("groups", "rep"), "tp", None)
    local = paired if mesh.shape["tp"] == 4 else general
    return jax.shard_map(local, mesh=mesh, in_specs=in_specs, out_specs=out_specs, check_vma=False)
```

```python
import functools
import math

import jax
import jax.numpy as jnp
from jax import lax
from jax.experimental import pallas as pl
from jax.experimental.pallas import tpu as pltpu
from jax.sharding import PartitionSpec as P

ANY = pl.BlockSpec(memory_space=pl.ANY)
HBM = pl.BlockSpec(memory_space=pltpu.HBM)
SMEM = pl.BlockSpec(memory_space=pltpu.SMEM)
VMEM = pl.BlockSpec(memory_space=pltpu.VMEM)
BF16 = jnp.bfloat16
F32 = jnp.float32
TILE = 1024


def order(us):
    return pl.CostEstimate(flops=int(us * 1.15e9) + 1, bytes_accessed=1, transcendentals=0)


def position():
    index = lax.axis_index("tp")
    return lax.div(index, 2), lax.rem(index, 2), lax.axis_index("rep")


def placed(spec):
    if spec.index_map is None:
        return spec
    return pl.BlockSpec(spec.block_shape, lambda *ids: spec.index_map(*ids, position()))


def grid_spec(grid, in_specs, out_specs):
    specs = out_specs if isinstance(out_specs, list) else [out_specs]
    specs = [placed(x) for x in specs]
    return pl.GridSpec(
        grid=grid,
        in_specs=[placed(x) for x in in_specs],
        out_specs=specs if isinstance(out_specs, list) else specs[0],
    )


def params(mib=48):
    return pltpu.CompilerParams(vmem_limit_bytes=mib * 2**20)


def sds(shape, dtype=BF16):
    return jax.ShapeDtypeStruct(shape, dtype)


def in_hbm(shape, dtype=BF16):
    return pltpu.HBM(shape, dtype)


def pin(*arrays):
    return [pltpu.with_memory_space_constraint(x, pltpu.HBM) for x in arrays]


TOKEN = in_hbm((8, 128), F32)


def select_kernel(by_shift, by_target, named, n_rep, cap, pool_dev, rank, slot, lists, pool, *rest):
    token, idx, counts, sems = rest[-4:]
    outs = rest[:-4]
    direct = not by_shift
    copies = []
    outs = outs[-(n_rep * len(by_shift) + len(by_target) + named) :]
    token[...] = jnp.zeros_like(token)
    me = lax.axis_index("rep")
    base = me * pool_dev
    for shift in range(n_rep):
        target = lax.rem(me + shift, n_rep)
        for k in range(cap + 1):
            idx[k] = 0
        count = jnp.int32(0)
        for place in [slot[lists[target, l]] - base for l in range(lists.shape[1])]:
            idx[jnp.minimum(count, cap)] = place
            count = count + jnp.where((place >= 0) & (place < pool_dev), 1, 0)
        for k in range(cap):
            entry = jnp.clip(idx[k], 0, pool_dev - 1)
            rows = pl.ds(k * rank, rank)
            if direct:
                copy = pltpu.make_async_copy(
                    pool.at[entry], outs[0].at[target, rows, :], sems.at[shift * cap + k]
                )
                copy.start()
                copies.append(copy)
                continue
            for c, (start, stop) in enumerate(by_shift):
                outs[c * n_rep + shift][rows, :] = pool[entry, :, start:stop]
            for c, (start, stop) in enumerate(by_target):
                outs[len(by_shift) * n_rep + c][target, rows, :] = pool[entry, :, start:stop]
    for copy in copies:
        copy.wait()
    if named:
        names = outs[-1]
        for i in range(n_rep * cap):
            names[i] = -1
        for s in range(n_rep):
            counts[s] = 0
        for l in range(lists.shape[1]):
            variant = lists[me, l]
            owner = slot[variant] // pool_dev
            k = counts[owner]
            counts[owner] = k + 1
            names[owner * cap + jnp.minimum(k, cap - 1)] = variant


def select(slot, lists, pool, by_shift, by_target, named, n_rep, cap, after=()):
    pool_dev, rank, width = pool.shape
    shapes = [in_hbm((cap * rank, stop - start)) for start, stop in by_shift for _ in range(n_rep)]
    shapes += [in_hbm((n_rep, cap * rank, stop - start)) for start, stop in by_target]
    specs = [VMEM if by_shift else ANY] * len(shapes)
    if named:
        shapes.append(in_hbm((n_rep * cap,), jnp.int32))
        specs.append(SMEM)
    return pl.pallas_call(
        functools.partial(select_kernel, by_shift, by_target, int(named), n_rep, cap, pool_dev, rank),
        out_shape=[*shapes, TOKEN],
        in_specs=[SMEM, SMEM, VMEM] + [ANY] * len(after),
        out_specs=[*specs, VMEM],
        scratch_shapes=[
            pltpu.SMEM((cap + 1,), jnp.int32),
            pltpu.SMEM((n_rep,), jnp.int32),
            pltpu.SemaphoreType.DMA((n_rep * cap,)),
        ],
        compiler_params=params(16),
        cost_estimate=order(0),
        name="select",
    )(*pin(slot, lists, pool), *pin(*after))


def product_early_kernel(per, pos, features, weights, keep0, send0, keep1, send1, token):
    token[...] = jnp.zeros_like(token)
    j = pl.program_id(0)
    own = features.shape[0] // 2
    result = jnp.dot(features[...], weights[...], preferred_element_type=F32).astype(BF16)
    for core in range(2):
        a, b = core * own, (1 - core) * own
        for block, keep, send in ((0, keep0, send0), (1, keep1, send1)):

            @pl.when((pos[1] == core) & (j // per == block))
            def _():
                keep[...] = result[a : a + own]
                send[...] = result[b : b + own]


def product_early(features, projection, tile, after=()):
    rows, depth = features.shape
    width = projection.shape[1] // 4
    half = rows // 2
    per = width // tile

    def kernel(features, weights, *rest):
        product_early_kernel(per, position(), features, weights, *rest[-5:])

    low = pl.BlockSpec((half // 2, tile), lambda j, pos: (0, jnp.minimum(j, per - 1)))
    high = pl.BlockSpec((half // 2, tile), lambda j, pos: (0, jnp.maximum(j - per, 0)))
    return pl.pallas_call(
        kernel,
        out_shape=[sds((half // 2, width))] * 4 + [TOKEN],
        grid_spec=grid_spec(
            grid=(2 * per,),
            in_specs=[
                pl.BlockSpec((half, depth), lambda j, pos: (1 - pos[0], 0)),
                pl.BlockSpec((depth, tile), lambda j, pos: (0, 2 * (1 - pos[0]) * per + j)),
            ]
            + [ANY] * len(after),
            out_specs=[low, low, high, high, pl.BlockSpec((8, 128), lambda j, pos: (0, 0))],
        ),
        compiler_params=params(),
        cost_estimate=order(0),
        name="product",
    )(features, projection, *pin(*after))


def product_columns_kernel(per, pos, features, weights, late, late_send, keep, send, token):
    token[...] = jnp.zeros_like(token)
    j = pl.program_id(0)
    half = features.shape[0] // 2
    own = half // 2
    result = jnp.dot(features[...], weights[...], preferred_element_type=F32).astype(BF16)
    for chip in range(2):
        here = pos[0] == chip
        other = result[(1 - chip) * half : (2 - chip) * half]

        @pl.when(here & (j < per))
        def _():
            late[...] = other

        @pl.when(here & (j >= per))
        def _():
            late_send[...] = other

        for core in range(2):

            @pl.when(here & (pos[1] == core))
            def _():
                keep[...] = result[chip * half + core * own : chip * half + (core + 1) * own][None]
                send[...] = result[chip * half + (1 - core) * own : chip * half + (2 - core) * own][None]


def product_columns(features, projection, tile, after=()):
    rows, depth = features.shape
    width = projection.shape[1] // 4
    half = rows // 2
    per = width // tile

    def block(j, pos):
        return jnp.where(j < per, pos[1], 1 - pos[1])

    rest = pl.BlockSpec((1, half // 2, tile), lambda j, pos: (block(j, pos), 0, lax.rem(j, per)))

    def kernel(features, weights, *rest):
        product_columns_kernel(per, position(), features, weights, *rest[-5:])

    return pl.pallas_call(
        kernel,
        out_shape=[in_hbm((half, width))] * 2 + [in_hbm((2, half // 2, width))] * 2 + [TOKEN],
        grid_spec=grid_spec(
            grid=(2 * per,),
            in_specs=[
                pl.BlockSpec((rows, depth), lambda j, pos: (0, 0)),
                pl.BlockSpec((depth, tile), lambda j, pos: (0, (2 * pos[0] + block(j, pos)) * per + lax.rem(j, per))),
            ]
            + [ANY] * len(after),
            out_specs=[
                pl.BlockSpec((half, tile), lambda j, pos: (0, jnp.minimum(j, per - 1))),
                pl.BlockSpec((half, tile), lambda j, pos: (0, jnp.maximum(j - per, 0))),
                rest,
                rest,
                pl.BlockSpec((8, 128), lambda j, pos: (0, 0)),
            ],
        ),
        compiler_params=params(),
        cost_estimate=order(0),
        name="product",
    )(features, projection, *pin(*after))


def product_kernel(split, pos, features, weights, keep, send, token):
    token[...] = jnp.zeros_like(token)
    own = features.shape[0] // 2
    result = jnp.dot(features[...], weights[...], preferred_element_type=F32).astype(BF16)
    low, high = result[:own], result[own:]
    if split:
        low, high = low[None], high[None]

    @pl.when(pos[1] == 0)
    def _():
        keep[...] = low
        send[...] = high

    @pl.when(pos[1] == 1)
    def _():
        keep[...] = high
        send[...] = low


def product(features, projection, other_rows, other_cols, first, count, tile, blocks, after=()):
    rows, depth = features.shape
    width = projection.shape[1]
    half = rows // 2
    own = half // 2
    tiles = count // tile

    def row_block(j, pos):
        return ((1 - pos[0]) if other_rows else pos[0], 0)

    def col_block(j, pos):
        if other_cols is None:
            return (0, j + first // tile)
        chip = (1 - pos[0]) if other_cols else pos[0]
        return (0, chip * (width // 2 // tile) + j + first // tile)

    if blocks > 1:
        per = tiles // blocks
        shape = (blocks, own, count // blocks)
        out_spec = pl.BlockSpec((1, own, tile), lambda j, pos: (j // per, 0, j % per))
    else:
        shape = (own, count)
        out_spec = pl.BlockSpec((own, tile), lambda j, pos: (0, j))
    body = functools.partial(product_kernel, blocks > 1)

    def kernel(features, weights, *rest):
        body(position(), features, weights, *rest[-3:])

    return pl.pallas_call(
        kernel,
        out_shape=[in_hbm(shape) if blocks > 1 else sds(shape)] * 2 + [TOKEN],
        grid_spec=grid_spec(
            grid=(tiles,),
            in_specs=[pl.BlockSpec((half, depth), row_block), pl.BlockSpec((depth, tile), col_block)]
            + [ANY] * len(after),
            out_specs=[out_spec] * 2 + [pl.BlockSpec((8, 128), lambda j, pos: (0, 0))],
        ),
        compiler_params=params(),
        cost_estimate=order(0),
        name="product",
    )(features, projection, *pin(*after))


def score_kernel(rank, names, wanted, features, factors, *rest):
    out, scores = rest[-2:]
    scores[...] = lax.dot_general(
        factors[...], features[...], (((1,), (1,)), ((), ())), preferred_element_type=F32
    )
    total = jnp.zeros(out.shape, F32)
    for i in range(factors.shape[0] // rank):
        total += jnp.where(wanted[...] == names[i], scores[i * rank : (i + 1) * rank, :], 0.0)
    out[...] = total


def score(names, wanted, features, factors, rank, after=()):
    rows = features.shape[0]
    return pl.pallas_call(
        functools.partial(score_kernel, rank),
        out_shape=sds((rank, rows), F32),
        in_specs=[SMEM] + [VMEM] * 3 + [ANY] * len(after),
        out_specs=VMEM,
        scratch_shapes=[pltpu.VMEM((factors.shape[0], rows), F32)],
        compiler_params=params(),
        cost_estimate=order(40),
        name="score",
    )(*pin(names, wanted), features, *pin(factors), *pin(*after))


def delta_kernel(n_blocks, n_before, n_rep, cap, rank, names, wanted, shrunk, late_own, late_recv, *rest):
    blocks, before = rest[:n_blocks], rest[n_blocks : n_blocks + n_before]
    straight, cross = rest[-7:-5] if before else rest[-5:-3]
    member, expand, result = rest[-3:]
    chip, core, me = position()
    listed = n_rep * cap
    half = late_own.shape[0]
    own = half // 2

    def product_of(factors, rows):
        columns = pl.ds(pl.multiple_of(rows * half, half), half)
        asked = wanted[:, columns]
        member[...] = jnp.zeros_like(member)
        for i in range(listed):
            if len(factors) == 1:
                name = names[i]
            else:
                name = names[lax.rem(me - i // cap + n_rep, n_rep) * cap + i % cap]
            member[i : i + 1, :] = jnp.where(asked == name, 1.0, 0.0)
        total = jnp.sum(shrunk[:, :, columns], axis=0).astype(BF16)
        entry = lax.broadcasted_iota(jnp.int32, (member.shape[0], listed * rank), 0)
        column = lax.broadcasted_iota(jnp.int32, (member.shape[0], listed * rank), 1)
        to_entry = jnp.where(column // rank == entry, 1.0, 0.0).astype(BF16)
        part = lax.broadcasted_iota(jnp.int32, (rank, listed * rank), 0)
        column = lax.broadcasted_iota(jnp.int32, (rank, listed * rank), 1)
        to_part = jnp.where(lax.rem(column, rank) == part, 1.0, 0.0).astype(BF16)
        turned = (((0,), (0,)), ((), ()))
        named = lax.dot_general(member[...].astype(BF16), to_entry, turned, preferred_element_type=F32)
        copied = lax.dot_general(total, to_part, turned, preferred_element_type=F32)
        size = listed * rank // len(factors)
        for s, factor in enumerate(factors):
            expand[pl.ds(s * size, size), :] = factor[...]
        result[...] = jnp.dot((named * copied).astype(BF16), expand[...], preferred_element_type=F32)

    product_of(blocks, 1 - chip)
    for out, c in ((straight, core), (cross, 1 - core)):
        rows = pl.ds(pl.multiple_of(c * own, own), own)
        base = late_own[rows, :].astype(F32) + late_recv[rows, :].astype(F32)
        out[...] = (base + result[rows, :]).astype(BF16)
    if before:
        mine, send = rest[-5], rest[-4]
        width = straight.shape[1]
        for start, factors in ((0, before), (mine.shape[1] - width, blocks)):
            product_of(factors, chip)
            for out, c in ((mine, core), (send, 1 - core)):
                rows = pl.ds(pl.multiple_of(c * own, own), own)
                out[:, start : start + width] = result[rows, :].astype(BF16)


def delta(names, wanted, shrunk, late, blocks, cut, n_rep, cap, rank, own, before=(), after=()):
    start, stop = cut
    width = stop - start
    listed = n_rep * cap
    shapes = [in_hbm((own, width))] * 2 + ([in_hbm((own, stop))] * 2 if before else [])
    return pl.pallas_call(
        functools.partial(delta_kernel, len(blocks), len(before), n_rep, cap, rank),
        out_shape=shapes,
        grid=(1,),
        in_specs=[SMEM]
        + [VMEM] * 2
        + [pl.BlockSpec((2 * own, width), lambda i: (0, start // width))] * 2
        + [VMEM] * (len(blocks) + len(before))
        + [ANY] * len(after),
        out_specs=[VMEM] * len(shapes),
        scratch_shapes=[
            pltpu.VMEM((-(-listed // 16) * 16, 2 * own), F32),
            pltpu.VMEM((listed * rank, width), BF16),
            pltpu.VMEM((2 * own, width), F32),
        ],
        compiler_params=params(),
        cost_estimate=order(0),
        name="delta",
    )(*pin(names, wanted), shrunk, *pin(late[0]), *(pin(late[1]) if before else late[1:]), *pin(*blocks, *before, *after))


def gate_kernel(*refs):
    pass


def gate(arrays, after):
    n = len(arrays)
    return pl.pallas_call(
        gate_kernel,
        out_shape=[sds(x.shape, x.dtype) for x in arrays],
        in_specs=[ANY] * (n + len(after)),
        out_specs=[ANY] * n,
        input_output_aliases={i: i for i in range(n)},
        cost_estimate=order(100),
        name="gate",
    )(*arrays, *pin(*after))


def near_kernel(residual, keep, recv, first, second, mine, theirs, *rest):
    out = rest[-1]
    block = pl.program_id(0)
    total = residual[...].astype(F32) + keep[0].astype(F32) + recv[0].astype(F32)
    total += jnp.where(block == 0, first[...], second[...]).astype(F32)
    total += jnp.where(block == position()[1], mine[...], theirs[...]).astype(F32)
    out[...] = total.astype(BF16)


def far_kernel(residual, keep, recv, straight, cross, *rest):
    out = rest[-1]
    total = residual[...].astype(F32) + keep[0].astype(F32) + recv[0].astype(F32)
    total += jnp.where(pl.program_id(0) == position()[1], straight[...], cross[...]).astype(F32)
    out[...] = total.astype(BF16)


def finish(out, residual, base, start, stop, near, pieces, after=()):
    own, full = residual.shape
    width = full // 4
    size = stop - start
    tile = min(TILE, math.gcd(size, start, width))
    count = size // tile
    skip = start // tile

    def place(b, j, pos):
        chip = pos[0] if near else 1 - pos[0]
        return (0, (2 * chip + b) * (width // tile) + skip + j)

    whole = pl.BlockSpec((own, tile), place)
    halves = [
        lambda b, j, pos: (0, skip + jnp.where(b == 0, j, count - 1)),
        lambda b, j, pos: (0, skip + jnp.where(b == 1, j, 0)),
    ]
    by_block = [pl.BlockSpec((own, tile), f) for f in halves]

    def by_core(offset):
        def index(b, j, pos):
            half = pos[1] ^ offset
            return (0, jnp.where(b == half, j, jnp.where(half == 0, count - 1, 0)))

        return pl.BlockSpec((own, tile), index)

    part = pl.BlockSpec((1, own, tile), lambda b, j, pos: (b, 0, skip + j))
    specs = [part, part, *(by_block if near else []), by_core(0), by_core(1)]
    specs = specs + [ANY] * len(after)
    operands = [*pin(residual, *base), *pieces, *pin(*after)]
    aliases = {}
    if out is not None:
        specs = specs + [ANY]
        aliases = {len(operands): 0}
        operands.append(out)
    return pl.pallas_call(
        near_kernel if near else far_kernel,
        out_shape=sds((own, full)),
        grid_spec=grid_spec(
            grid=(2, count),
            in_specs=[whole, *specs],
            out_specs=whole,
        ),
        input_output_aliases=aliases,
        compiler_params=params(),
        cost_estimate=order(60),
        name="near" if near else "far",
    )(*operands)


def paired(
    head_outputs, residual, projection, shrink_pool, expand_pool, pool_slot, variant_list, request_variant
):
    n_rep = lax.axis_size("rep")
    features = head_outputs[0]
    rows = features.shape[0]
    own = rows // 4
    pool_dev, rank, width = shrink_pool.shape
    cap = pool_dev // 4 + 2
    stream = residual[0]
    sizes = (cap, rank)
    tile = min(1024, width)
    cut = width // 2
    cuts = ((0, cut), (cut, width))

    def over_core(x):
        return lax.ppermute(x, "tp", [(0, 1), (1, 0), (2, 3), (3, 2)])

    def over_chip(x):
        return lax.ppermute(x, "tp", [(0, 2), (2, 0), (1, 3), (3, 1)])

    def over_both(x):
        return lax.ppermute(x, "tp", [(0, 3), (3, 0), (1, 2), (2, 1)])

    def over_rep(x, shift):
        return lax.ppermute(x, "rep", [(i, (i + shift) % n_rep) for i in range(n_rep)])

    shifts = [s for s in range(1, n_rep) if s != n_rep // 2] + [n_rep // 2]
    chosen, token = select(pool_slot, variant_list, shrink_pool, (), ((0, width),), False, n_rep, cap)
    shrink = lax.all_to_all(chosen, "rep", 0, 0, tiled=True).reshape(n_rep * cap * rank, width)

    keep0, send0, keep1, send1, token = product_early(features, projection, tile, [token])
    sums = [keep0 + over_core(send0), keep1 + over_core(send1)]
    early = [over_chip(x) for x in sums]

    *chosen, second, names, token = select(
        pool_slot, variant_list, expand_pool, cuts[:1], cuts[1:], True, n_rep, cap, sums
    )
    first = [chosen[0]] + [None] * (n_rep - 1)
    for s in shifts:
        first[s] = over_rep(chosen[s], s)
    second = lax.all_to_all(second, "rep", 0, 0, tiled=True).reshape(n_rep * cap * rank, cut)

    late_keep, late_send, keep, send, token = product_columns(features, projection, tile, [*sums, token])
    late = (late_keep, over_core(late_send))
    near_base = (keep, over_core(send))

    part = score(names, request_variant, features, shrink, rank, [token, early[0]])
    shrunk = lax.all_gather(part, "tp")

    common = (names, request_variant, shrunk, late)
    straight, cross = delta(*common, first, cuts[0], n_rep, *sizes, own, (), [early[1]])
    far = [over_chip(straight), over_both(cross)]
    straight, cross, mine, send = delta(*common, [second], cuts[1], n_rep, *sizes, own, first, [near_base[1], straight])
    last = [over_chip(straight), over_both(cross)]
    theirs = over_core(send)
    keep, send, token = product(features, projection, False, True, 0, 2 * width, tile, 2, [mine])
    far_base = (keep, over_core(send))
    far = gate(far, [token])
    out = finish(None, stream, near_base, 0, width, True, [*early, mine, theirs], far)
    out = finish(out, stream, far_base, *cuts[0], False, far)
    out = finish(out, stream, far_base, *cuts[1], False, last)
    return out[None]


def general(
    head_outputs, residual, projection, shrink_pool, expand_pool, pool_slot, variant_list, request_variant
):
    split_count = lax.axis_size("tp")
    split_index = lax.axis_index("tp")
    replica_index = lax.axis_index("rep")
    row_count = head_outputs.shape[1]
    local_width = head_outputs.shape[2]
    rank_size = shrink_pool.shape[1]
    listed = variant_list.shape[1]
    own_rows = row_count // split_count
    flat_size = rank_size * local_width
    features = head_outputs[0]
    wanted = request_variant[0]
    my_list = lax.dynamic_index_in_dim(variant_list, replica_index, 0, keepdims=False)
    my_positions = jnp.take(pool_slot, my_list, axis=0)
    pieces = (
        lax.all_gather(shrink_pool, "rep", axis=0, tiled=True),
        lax.all_gather(expand_pool, "rep", axis=0, tiled=True),
    )
    piece_rows = pieces[0].shape[0]
    matches = (my_positions[:, None] == jnp.arange(piece_rows, dtype=jnp.int32)[None, :]).astype(BF16)
    shrink_sel = jnp.dot(matches, pieces[0].reshape(piece_rows, flat_size), preferred_element_type=F32)
    expand_sel = jnp.dot(matches, pieces[1].reshape(piece_rows, flat_size), preferred_element_type=F32)
    shrink_sel = shrink_sel.astype(BF16).reshape(listed * rank_size, local_width)
    expand_sel = expand_sel.astype(BF16).reshape(listed, rank_size, local_width)
    member = wanted[:, None] == my_list[None, :]
    scores = lax.dot_general(
        features, shrink_sel, (((1,), (1,)), ((), ())), preferred_element_type=F32
    )
    shrunk = jnp.sum(scores.reshape(row_count, listed, rank_size) * member[:, :, None], axis=1)
    own_shrunk = lax.psum_scatter(shrunk.astype(BF16), "tp", scatter_dimension=0, tiled=True)
    own_member = lax.dynamic_slice_in_dim(member, split_index * own_rows, own_rows, 0)
    spread = own_member[:, :, None] * own_shrunk[:, None, :]
    spread = spread.reshape(own_rows, listed * rank_size)
    piece = lax.all_gather(expand_sel, "tp", axis=2, tiled=True)
    delta_rows = jnp.dot(
        spread, piece.reshape(listed * rank_size, piece.shape[2]), preferred_element_type=F32
    )
    base_rows = lax.psum_scatter(
        jnp.dot(features, projection, preferred_element_type=F32).astype(BF16),
        "tp",
        scatter_dimension=0,
        tiled=True,
    ).astype(F32)
    return (residual[0].astype(F32) + base_rows + delta_rows).astype(BF16)[None]


def solution(mesh):
    in_specs = (
        P(("groups", "rep"), None, "tp"),
        P(("groups", "rep"), "tp", None),
        P("tp", None),
        P(("groups", "rep"), None, "tp"),
        P(("groups", "rep"), None, "tp"),
        P("groups"),
        P("groups", None),
        P(("groups", "rep"), None),
    )
    out_specs = P(("groups", "rep"), "tp", None)
    local = paired if mesh.shape["tp"] == 4 else general
    return jax.shard_map(local, mesh=mesh, in_specs=in_specs, out_specs=out_specs, check_vma=False)
```

```python
import functools
import math

import jax
import jax.numpy as jnp
from jax import lax
from jax.experimental import pallas as pl
from jax.experimental.pallas import tpu as pltpu
from jax.sharding import PartitionSpec as P

ANY = pl.BlockSpec(memory_space=pl.ANY)
HBM = pl.BlockSpec(memory_space=pltpu.HBM)
SMEM = pl.BlockSpec(memory_space=pltpu.SMEM)
VMEM = pl.BlockSpec(memory_space=pltpu.VMEM)
BF16 = jnp.bfloat16
F32 = jnp.float32
TILE = 1024


def order(us):
    return pl.CostEstimate(flops=int(us * 1.15e9) + 1, bytes_accessed=1, transcendentals=0)


def position():
    index = lax.axis_index("tp")
    return lax.div(index, 2), lax.rem(index, 2), lax.axis_index("rep")


def placed(spec):
    if spec.index_map is None:
        return spec
    return pl.BlockSpec(spec.block_shape, lambda *ids: spec.index_map(*ids, position()))


def grid_spec(grid, in_specs, out_specs):
    specs = out_specs if isinstance(out_specs, list) else [out_specs]
    specs = [placed(x) for x in specs]
    return pl.GridSpec(
        grid=grid,
        in_specs=[placed(x) for x in in_specs],
        out_specs=specs if isinstance(out_specs, list) else specs[0],
    )


def params(mib=48):
    return pltpu.CompilerParams(vmem_limit_bytes=mib * 2**20)


def sds(shape, dtype=BF16):
    return jax.ShapeDtypeStruct(shape, dtype)


def in_hbm(shape, dtype=BF16):
    return pltpu.HBM(shape, dtype)


def pin(*arrays):
    return [pltpu.with_memory_space_constraint(x, pltpu.HBM) for x in arrays]


TOKEN = in_hbm((8, 128), F32)


def select_kernel(by_shift, by_target, named, n_rep, cap, pool_dev, rank, slot, lists, pool, *rest):
    token, idx, counts = rest[-3:]
    outs = rest[: -3]
    outs = outs[-(n_rep * len(by_shift) + len(by_target) + named) :]
    token[...] = jnp.zeros_like(token)
    me = lax.axis_index("rep")
    base = me * pool_dev
    for shift in range(n_rep):
        target = lax.rem(me + shift, n_rep)
        for k in range(cap + 1):
            idx[k] = 0
        count = jnp.int32(0)
        for l in range(lists.shape[1]):
            place = slot[lists[target, l]] - base
            idx[jnp.minimum(count, cap)] = place
            count = count + jnp.where((place >= 0) & (place < pool_dev), 1, 0)
        for k in range(cap):
            entry = jnp.clip(idx[k], 0, pool_dev - 1)
            rows = pl.ds(k * rank, rank)
            for c, (start, stop) in enumerate(by_shift):
                outs[c * n_rep + shift][rows, :] = pool[entry, :, start:stop]
            for c, (start, stop) in enumerate(by_target):
                outs[len(by_shift) * n_rep + c][target, rows, :] = pool[entry, :, start:stop]
    if named:
        names = outs[-1]
        for i in range(n_rep * cap):
            names[i] = -1
        for s in range(n_rep):
            counts[s] = 0
        for l in range(lists.shape[1]):
            variant = lists[me, l]
            owner = slot[variant] // pool_dev
            k = counts[owner]
            counts[owner] = k + 1
            names[owner * cap + jnp.minimum(k, cap - 1)] = variant


def select(slot, lists, pool, by_shift, by_target, named, n_rep, cap, after=()):
    pool_dev, rank, width = pool.shape
    shapes = [in_hbm((cap * rank, stop - start)) for start, stop in by_shift for _ in range(n_rep)]
    shapes += [in_hbm((n_rep, cap * rank, stop - start)) for start, stop in by_target]
    specs = [VMEM] * len(shapes)
    if named:
        shapes.append(in_hbm((n_rep * cap,), jnp.int32))
        specs.append(SMEM)
    return pl.pallas_call(
        functools.partial(select_kernel, by_shift, by_target, int(named), n_rep, cap, pool_dev, rank),
        out_shape=[*shapes, TOKEN],
        in_specs=[SMEM, SMEM, VMEM] + [ANY] * len(after),
        out_specs=[*specs, VMEM],
        scratch_shapes=[pltpu.SMEM((cap + 1,), jnp.int32), pltpu.SMEM((n_rep,), jnp.int32)],
        compiler_params=params(16),
        cost_estimate=order(0),
        name="select",
    )(*pin(slot, lists, pool), *pin(*after))


def product_early_kernel(per, pos, features, weights, keep0, send0, keep1, send1, token):
    token[...] = jnp.zeros_like(token)
    j = pl.program_id(0)
    own = features.shape[0] // 2
    result = jnp.dot(features[...], weights[...], preferred_element_type=F32).astype(BF16)
    for core in range(2):
        a, b = core * own, (1 - core) * own
        for block, keep, send in ((0, keep0, send0), (1, keep1, send1)):

            @pl.when((pos[1] == core) & (j // per == block))
            def _():
                keep[...] = result[a : a + own]
                send[...] = result[b : b + own]


def product_early(features, projection, tile, after=()):
    rows, depth = features.shape
    width = projection.shape[1] // 4
    half = rows // 2
    per = width // tile

    def kernel(features, weights, *rest):
        product_early_kernel(per, position(), features, weights, *rest[-5:])

    low = pl.BlockSpec((half // 2, tile), lambda j, pos: (0, jnp.minimum(j, per - 1)))
    high = pl.BlockSpec((half // 2, tile), lambda j, pos: (0, jnp.maximum(j - per, 0)))
    return pl.pallas_call(
        kernel,
        out_shape=[sds((half // 2, width))] * 4 + [TOKEN],
        grid_spec=grid_spec(
            grid=(2 * per,),
            in_specs=[
                pl.BlockSpec((half, depth), lambda j, pos: (1 - pos[0], 0)),
                pl.BlockSpec((depth, tile), lambda j, pos: (0, 2 * (1 - pos[0]) * per + j)),
            ]
            + [ANY] * len(after),
            out_specs=[low, low, high, high, pl.BlockSpec((8, 128), lambda j, pos: (0, 0))],
        ),
        compiler_params=params(),
        cost_estimate=order(0),
        name="product",
    )(features, projection, *pin(*after))


def product_columns_kernel(per, pos, features, weights, late, late_send, keep, send, token):
    token[...] = jnp.zeros_like(token)
    j = pl.program_id(0)
    half = features.shape[0] // 2
    own = half // 2
    result = jnp.dot(features[...], weights[...], preferred_element_type=F32).astype(BF16)
    for chip in range(2):
        here = pos[0] == chip
        other = result[(1 - chip) * half : (2 - chip) * half]

        @pl.when(here & (j < per))
        def _():
            late[...] = other

        @pl.when(here & (j >= per))
        def _():
            late_send[...] = other

        for core in range(2):

            @pl.when(here & (pos[1] == core))
            def _():
                keep[...] = result[chip * half + core * own : chip * half + (core + 1) * own][None]
                send[...] = result[chip * half + (1 - core) * own : chip * half + (2 - core) * own][None]


def product_columns(features, projection, tile, after=()):
    rows, depth = features.shape
    width = projection.shape[1] // 4
    half = rows // 2
    per = width // tile

    def block(j, pos):
        return jnp.where(j < per, pos[1], 1 - pos[1])

    rest = pl.BlockSpec((1, half // 2, tile), lambda j, pos: (block(j, pos), 0, lax.rem(j, per)))

    def kernel(features, weights, *rest):
        product_columns_kernel(per, position(), features, weights, *rest[-5:])

    return pl.pallas_call(
        kernel,
        out_shape=[in_hbm((half, width))] * 2 + [in_hbm((2, half // 2, width))] * 2 + [TOKEN],
        grid_spec=grid_spec(
            grid=(2 * per,),
            in_specs=[
                pl.BlockSpec((rows, depth), lambda j, pos: (0, 0)),
                pl.BlockSpec((depth, tile), lambda j, pos: (0, (2 * pos[0] + block(j, pos)) * per + lax.rem(j, per))),
            ]
            + [ANY] * len(after),
            out_specs=[
                pl.BlockSpec((half, tile), lambda j, pos: (0, jnp.minimum(j, per - 1))),
                pl.BlockSpec((half, tile), lambda j, pos: (0, jnp.maximum(j - per, 0))),
                rest,
                rest,
                pl.BlockSpec((8, 128), lambda j, pos: (0, 0)),
            ],
        ),
        compiler_params=params(),
        cost_estimate=order(0),
        name="product",
    )(features, projection, *pin(*after))


def product_kernel(split, pos, features, weights, keep, send, token):
    token[...] = jnp.zeros_like(token)
    own = features.shape[0] // 2
    result = jnp.dot(features[...], weights[...], preferred_element_type=F32).astype(BF16)
    low, high = result[:own], result[own:]
    if split:
        low, high = low[None], high[None]

    @pl.when(pos[1] == 0)
    def _():
        keep[...] = low
        send[...] = high

    @pl.when(pos[1] == 1)
    def _():
        keep[...] = high
        send[...] = low


def product(features, projection, other_rows, other_cols, first, count, tile, blocks, after=()):
    rows, depth = features.shape
    width = projection.shape[1]
    half = rows // 2
    own = half // 2
    tiles = count // tile

    def row_block(j, pos):
        return ((1 - pos[0]) if other_rows else pos[0], 0)

    def col_block(j, pos):
        if other_cols is None:
            return (0, j + first // tile)
        chip = (1 - pos[0]) if other_cols else pos[0]
        return (0, chip * (width // 2 // tile) + j + first // tile)

    if blocks > 1:
        per = tiles // blocks
        shape = (blocks, own, count // blocks)
        out_spec = pl.BlockSpec((1, own, tile), lambda j, pos: (j // per, 0, j % per))
    else:
        shape = (own, count)
        out_spec = pl.BlockSpec((own, tile), lambda j, pos: (0, j))
    body = functools.partial(product_kernel, blocks > 1)

    def kernel(features, weights, *rest):
        body(position(), features, weights, *rest[-3:])

    return pl.pallas_call(
        kernel,
        out_shape=[in_hbm(shape) if blocks > 1 else sds(shape)] * 2 + [TOKEN],
        grid_spec=grid_spec(
            grid=(tiles,),
            in_specs=[pl.BlockSpec((half, depth), row_block), pl.BlockSpec((depth, tile), col_block)]
            + [ANY] * len(after),
            out_specs=[out_spec] * 2 + [pl.BlockSpec((8, 128), lambda j, pos: (0, 0))],
        ),
        compiler_params=params(),
        cost_estimate=order(0),
        name="product",
    )(features, projection, *pin(*after))


def score_kernel(rank, names, wanted, features, factors, *rest):
    out, scores = rest[-2:]
    scores[...] = lax.dot_general(
        factors[...], features[...], (((1,), (1,)), ((), ())), preferred_element_type=F32
    )
    total = jnp.zeros(out.shape, F32)
    for i in range(factors.shape[0] // rank):
        total += jnp.where(wanted[...] == names[i], scores[i * rank : (i + 1) * rank, :], 0.0)
    out[...] = total


def score(names, wanted, features, factors, rank, after=()):
    rows = features.shape[0]
    return pl.pallas_call(
        functools.partial(score_kernel, rank),
        out_shape=sds((rank, rows), F32),
        in_specs=[SMEM] + [VMEM] * 3 + [ANY] * len(after),
        out_specs=VMEM,
        scratch_shapes=[pltpu.VMEM((factors.shape[0], rows), F32)],
        compiler_params=params(),
        cost_estimate=order(40),
        name="score",
    )(*pin(names, wanted), features, *pin(factors), *pin(*after))


def delta_kernel(n_blocks, n_before, n_rep, cap, rank, names, wanted, shrunk, late_own, late_recv, *rest):
    blocks, before = rest[:n_blocks], rest[n_blocks : n_blocks + n_before]
    straight, cross = rest[-7:-5] if before else rest[-5:-3]
    member, expand, result = rest[-3:]
    chip, core, me = position()
    listed = n_rep * cap
    half = late_own.shape[0]
    own = half // 2

    def product_of(factors, rows):
        columns = pl.ds(pl.multiple_of(rows * half, half), half)
        asked = wanted[:, columns]
        member[...] = jnp.zeros_like(member)
        for i in range(listed):
            if len(factors) == 1:
                name = names[i]
            else:
                name = names[lax.rem(me - i // cap + n_rep, n_rep) * cap + i % cap]
            member[i : i + 1, :] = jnp.where(asked == name, 1.0, 0.0)
        total = jnp.sum(shrunk[:, :, columns], axis=0).astype(BF16)
        entry = lax.broadcasted_iota(jnp.int32, (member.shape[0], listed * rank), 0)
        column = lax.broadcasted_iota(jnp.int32, (member.shape[0], listed * rank), 1)
        to_entry = jnp.where(column // rank == entry, 1.0, 0.0).astype(BF16)
        part = lax.broadcasted_iota(jnp.int32, (rank, listed * rank), 0)
        column = lax.broadcasted_iota(jnp.int32, (rank, listed * rank), 1)
        to_part = jnp.where(lax.rem(column, rank) == part, 1.0, 0.0).astype(BF16)
        turned = (((0,), (0,)), ((), ()))
        named = lax.dot_general(member[...].astype(BF16), to_entry, turned, preferred_element_type=F32)
        copied = lax.dot_general(total, to_part, turned, preferred_element_type=F32)
        size = listed * rank // len(factors)
        for s, factor in enumerate(factors):
            expand[pl.ds(s * size, size), :] = factor[...]
        result[...] = jnp.dot((named * copied).astype(BF16), expand[...], preferred_element_type=F32)

    product_of(blocks, 1 - chip)
    for out, c in ((straight, core), (cross, 1 - core)):
        rows = pl.ds(pl.multiple_of(c * own, own), own)
        base = late_own[rows, :].astype(F32) + late_recv[rows, :].astype(F32)
        out[...] = (base + result[rows, :]).astype(BF16)
    if before:
        mine, send = rest[-5], rest[-4]
        width = straight.shape[1]
        for start, factors in ((0, before), (mine.shape[1] - width, blocks)):
            product_of(factors, chip)
            for out, c in ((mine, core), (send, 1 - core)):
                rows = pl.ds(pl.multiple_of(c * own, own), own)
                out[:, start : start + width] = result[rows, :].astype(BF16)


def delta(names, wanted, shrunk, late, blocks, cut, n_rep, cap, rank, own, before=(), after=()):
    start, stop = cut
    width = stop - start
    listed = n_rep * cap
    shapes = [in_hbm((own, width))] * 2 + ([in_hbm((own, stop))] * 2 if before else [])
    return pl.pallas_call(
        functools.partial(delta_kernel, len(blocks), len(before), n_rep, cap, rank),
        out_shape=shapes,
        grid=(1,),
        in_specs=[SMEM]
        + [VMEM] * 2
        + [pl.BlockSpec((2 * own, width), lambda i: (0, start // width))] * 2
        + [VMEM] * (len(blocks) + len(before))
        + [ANY] * len(after),
        out_specs=[VMEM] * len(shapes),
        scratch_shapes=[
            pltpu.VMEM((-(-listed // 16) * 16, 2 * own), F32),
            pltpu.VMEM((listed * rank, width), BF16),
            pltpu.VMEM((2 * own, width), F32),
        ],
        compiler_params=params(),
        cost_estimate=order(0),
        name="delta",
    )(*pin(names, wanted), shrunk, *pin(late[0]), *(pin(late[1]) if before else late[1:]), *pin(*blocks, *before, *after))


def gate_kernel(*refs):
    pass


def gate(arrays, after):
    n = len(arrays)
    return pl.pallas_call(
        gate_kernel,
        out_shape=[sds(x.shape, x.dtype) for x in arrays],
        in_specs=[ANY] * (n + len(after)),
        out_specs=[ANY] * n,
        input_output_aliases={i: i for i in range(n)},
        cost_estimate=order(100),
        name="gate",
    )(*arrays, *pin(*after))


def near_kernel(residual, keep, recv, first, second, mine, theirs, *rest):
    out = rest[-1]
    block = pl.program_id(0)
    total = residual[...].astype(F32) + keep[0].astype(F32) + recv[0].astype(F32)
    total += jnp.where(block == 0, first[...], second[...]).astype(F32)
    total += jnp.where(block == position()[1], mine[...], theirs[...]).astype(F32)
    out[...] = total.astype(BF16)


def far_kernel(residual, keep, recv, straight, cross, *rest):
    out = rest[-1]
    total = residual[...].astype(F32) + keep[0].astype(F32) + recv[0].astype(F32)
    total += jnp.where(pl.program_id(0) == position()[1], straight[...], cross[...]).astype(F32)
    out[...] = total.astype(BF16)


def finish(out, residual, base, start, stop, near, pieces, after=()):
    own, full = residual.shape
    width = full // 4
    size = stop - start
    tile = min(TILE, math.gcd(size, start, width))
    count = size // tile
    skip = start // tile

    def place(b, j, pos):
        chip = pos[0] if near else 1 - pos[0]
        return (0, (2 * chip + b) * (width // tile) + skip + j)

    whole = pl.BlockSpec((own, tile), place)
    halves = [
        lambda b, j, pos: (0, skip + jnp.where(b == 0, j, count - 1)),
        lambda b, j, pos: (0, skip + jnp.where(b == 1, j, 0)),
    ]
    by_block = [pl.BlockSpec((own, tile), f) for f in halves]

    def by_core(offset):
        def index(b, j, pos):
            half = pos[1] ^ offset
            return (0, jnp.where(b == half, j, jnp.where(half == 0, count - 1, 0)))

        return pl.BlockSpec((own, tile), index)

    part = pl.BlockSpec((1, own, tile), lambda b, j, pos: (b, 0, skip + j))
    specs = [part, part, *(by_block if near else []), by_core(0), by_core(1)]
    specs = specs + [ANY] * len(after)
    operands = [*pin(residual, *base), *pieces, *pin(*after)]
    aliases = {}
    if out is not None:
        specs = specs + [ANY]
        aliases = {len(operands): 0}
        operands.append(out)
    return pl.pallas_call(
        near_kernel if near else far_kernel,
        out_shape=sds((own, full)),
        grid_spec=grid_spec(
            grid=(2, count),
            in_specs=[whole, *specs],
            out_specs=whole,
        ),
        input_output_aliases=aliases,
        compiler_params=params(),
        cost_estimate=order(60),
        name="near" if near else "far",
    )(*operands)


def paired(
    head_outputs, residual, projection, shrink_pool, expand_pool, pool_slot, variant_list, request_variant
):
    n_rep = lax.axis_size("rep")
    features = head_outputs[0]
    rows = features.shape[0]
    own = rows // 4
    pool_dev, rank, width = shrink_pool.shape
    cap = pool_dev // 4 + 2
    stream = residual[0]
    sizes = (cap, rank)
    tile = min(1024, width)
    cut = width // 2
    cuts = ((0, cut), (cut, width))

    def over_core(x):
        return lax.ppermute(x, "tp", [(0, 1), (1, 0), (2, 3), (3, 2)])

    def over_chip(x):
        return lax.ppermute(x, "tp", [(0, 2), (2, 0), (1, 3), (3, 1)])

    def over_both(x):
        return lax.ppermute(x, "tp", [(0, 3), (3, 0), (1, 2), (2, 1)])

    def over_rep(x, shift):
        return lax.ppermute(x, "rep", [(i, (i + shift) % n_rep) for i in range(n_rep)])

    shifts = [s for s in range(1, n_rep) if s != n_rep // 2] + [n_rep // 2]
    chosen, token = select(pool_slot, variant_list, shrink_pool, (), ((0, width),), False, n_rep, cap)
    shrink = lax.all_to_all(chosen, "rep", 0, 0, tiled=True).reshape(n_rep * cap * rank, width)

    keep0, send0, keep1, send1, token = product_early(features, projection, tile, [token])
    sums = [keep0 + over_core(send0), keep1 + over_core(send1)]
    early = [over_chip(x) for x in sums]

    *chosen, second, names, token = select(
        pool_slot, variant_list, expand_pool, cuts[:1], cuts[1:], True, n_rep, cap, sums
    )
    first = [chosen[0]] + [None] * (n_rep - 1)
    for s in shifts:
        first[s] = over_rep(chosen[s], s)
    second = lax.all_to_all(second, "rep", 0, 0, tiled=True).reshape(n_rep * cap * rank, cut)

    late_keep, late_send, keep, send, token = product_columns(features, projection, tile, [*sums, token])
    late = (late_keep, over_core(late_send))
    near_base = (keep, over_core(send))

    part = score(names, request_variant, features, shrink, rank, [token, early[0]])
    shrunk = lax.all_gather(part, "tp")

    common = (names, request_variant, shrunk, late)
    straight, cross = delta(*common, first, cuts[0], n_rep, *sizes, own, (), [early[1]])
    far = [over_chip(straight), over_both(cross)]
    straight, cross, mine, send = delta(*common, [second], cuts[1], n_rep, *sizes, own, first, [near_base[1], straight])
    last = [over_chip(straight), over_both(cross)]
    theirs = over_core(send)
    keep, send, token = product(features, projection, False, True, 0, 2 * width, tile, 2, [mine])
    far_base = (keep, over_core(send))
    far = gate(far, [token])
    out = finish(None, stream, near_base, 0, width, True, [*early, mine, theirs], far)
    out = finish(out, stream, far_base, *cuts[0], False, far)
    out = finish(out, stream, far_base, *cuts[1], False, last)
    return out[None]


def general(
    head_outputs, residual, projection, shrink_pool, expand_pool, pool_slot, variant_list, request_variant
):
    split_count = lax.axis_size("tp")
    split_index = lax.axis_index("tp")
    replica_index = lax.axis_index("rep")
    row_count = head_outputs.shape[1]
    local_width = head_outputs.shape[2]
    rank_size = shrink_pool.shape[1]
    listed = variant_list.shape[1]
    own_rows = row_count // split_count
    flat_size = rank_size * local_width
    features = head_outputs[0]
    wanted = request_variant[0]
    my_list = lax.dynamic_index_in_dim(variant_list, replica_index, 0, keepdims=False)
    my_positions = jnp.take(pool_slot, my_list, axis=0)
    pieces = (
        lax.all_gather(shrink_pool, "rep", axis=0, tiled=True),
        lax.all_gather(expand_pool, "rep", axis=0, tiled=True),
    )
    piece_rows = pieces[0].shape[0]
    matches = (my_positions[:, None] == jnp.arange(piece_rows, dtype=jnp.int32)[None, :]).astype(BF16)
    shrink_sel = jnp.dot(matches, pieces[0].reshape(piece_rows, flat_size), preferred_element_type=F32)
    expand_sel = jnp.dot(matches, pieces[1].reshape(piece_rows, flat_size), preferred_element_type=F32)
    shrink_sel = shrink_sel.astype(BF16).reshape(listed * rank_size, local_width)
    expand_sel = expand_sel.astype(BF16).reshape(listed, rank_size, local_width)
    member = wanted[:, None] == my_list[None, :]
    scores = lax.dot_general(
        features, shrink_sel, (((1,), (1,)), ((), ())), preferred_element_type=F32
    )
    shrunk = jnp.sum(scores.reshape(row_count, listed, rank_size) * member[:, :, None], axis=1)
    own_shrunk = lax.psum_scatter(shrunk.astype(BF16), "tp", scatter_dimension=0, tiled=True)
    own_member = lax.dynamic_slice_in_dim(member, split_index * own_rows, own_rows, 0)
    spread = own_member[:, :, None] * own_shrunk[:, None, :]
    spread = spread.reshape(own_rows, listed * rank_size)
    piece = lax.all_gather(expand_sel, "tp", axis=2, tiled=True)
    delta_rows = jnp.dot(
        spread, piece.reshape(listed * rank_size, piece.shape[2]), preferred_element_type=F32
    )
    base_rows = lax.psum_scatter(
        jnp.dot(features, projection, preferred_element_type=F32).astype(BF16),
        "tp",
        scatter_dimension=0,
        tiled=True,
    ).astype(F32)
    return (residual[0].astype(F32) + base_rows + delta_rows).astype(BF16)[None]


def solution(mesh):
    in_specs = (
        P(("groups", "rep"), None, "tp"),
        P(("groups", "rep"), "tp", None),
        P("tp", None),
        P(("groups", "rep"), None, "tp"),
        P(("groups", "rep"), None, "tp"),
        P("groups"),
        P("groups", None),
        P(("groups", "rep"), None),
    )
    out_specs = P(("groups", "rep"), "tp", None)
    local = paired if mesh.shape["tp"] == 4 else general
    return jax.shard_map(local, mesh=mesh, in_specs=in_specs, out_specs=out_specs, check_vma=False)
```

```python
import functools
import math

import jax
import jax.numpy as jnp
from jax import lax
from jax.experimental import pallas as pl
from jax.experimental.pallas import tpu as pltpu
from jax.sharding import PartitionSpec as P

ANY = pl.BlockSpec(memory_space=pl.ANY)
HBM = pl.BlockSpec(memory_space=pltpu.HBM)
SMEM = pl.BlockSpec(memory_space=pltpu.SMEM)
VMEM = pl.BlockSpec(memory_space=pltpu.VMEM)
BF16 = jnp.bfloat16
F32 = jnp.float32
TILE = 1024


def order(us):
    return pl.CostEstimate(flops=int(us * 1.15e9) + 1, bytes_accessed=1, transcendentals=0)


def position():
    index = lax.axis_index("tp")
    return lax.div(index, 2), lax.rem(index, 2), lax.axis_index("rep")


def placed(spec):
    if spec.index_map is None:
        return spec
    return pl.BlockSpec(spec.block_shape, lambda *ids: spec.index_map(*ids, position()))


def grid_spec(grid, in_specs, out_specs):
    specs = out_specs if isinstance(out_specs, list) else [out_specs]
    specs = [placed(x) for x in specs]
    return pl.GridSpec(
        grid=grid,
        in_specs=[placed(x) for x in in_specs],
        out_specs=specs if isinstance(out_specs, list) else specs[0],
    )


def params(mib=48):
    return pltpu.CompilerParams(vmem_limit_bytes=mib * 2**20)


def sds(shape, dtype=BF16):
    return jax.ShapeDtypeStruct(shape, dtype)


def in_hbm(shape, dtype=BF16):
    return pltpu.HBM(shape, dtype)


def pin(*arrays):
    return [pltpu.with_memory_space_constraint(x, pltpu.HBM) for x in arrays]


TOKEN = in_hbm((8, 128), F32)


def asked_entries(names, wanted, member, place, listed, rank):
    member[...] = jnp.zeros_like(member)
    for i in range(listed):
        member[i : i + 1, :] = jnp.where(wanted == names[place(i)], 1.0, 0.0)
    entry = lax.broadcasted_iota(jnp.int32, (member.shape[0], listed * rank), 0)
    column = lax.broadcasted_iota(jnp.int32, (member.shape[0], listed * rank), 1)
    to_entry = jnp.where(column // rank == entry, 1.0, 0.0).astype(BF16)
    return lax.dot_general(
        member[...].astype(BF16), to_entry, (((0,), (0,)), ((), ())), preferred_element_type=F32
    )


def select_kernel(by_shift, by_target, named, n_rep, cap, pool_dev, rank, slot, lists, pool, *rest):
    token, idx, counts, member = rest[-4:]
    outs = rest[:-4]
    outs = outs[-(n_rep * len(by_shift) + len(by_target) + 2 * named) :]
    token[...] = jnp.zeros_like(token)
    me = lax.axis_index("rep")
    base = me * pool_dev
    for shift in range(n_rep):
        target = lax.rem(me + shift, n_rep)
        for k in range(cap + 1):
            idx[k] = 0
        count = jnp.int32(0)
        for l in range(lists.shape[1]):
            place = slot[lists[target, l]] - base
            idx[jnp.minimum(count, cap)] = place
            count = count + jnp.where((place >= 0) & (place < pool_dev), 1, 0)
        for k in range(cap):
            entry = jnp.clip(idx[k], 0, pool_dev - 1)
            rows = pl.ds(k * rank, rank)
            for c, (start, stop) in enumerate(by_shift):
                outs[c * n_rep + shift][rows, :] = pool[entry, :, start:stop]
            for c, (start, stop) in enumerate(by_target):
                outs[len(by_shift) * n_rep + c][target, rows, :] = pool[entry, :, start:stop]
    if named:
        names, asked, wanted = outs[-2], outs[-1], rest[0]
        for i in range(n_rep * cap):
            names[i] = -1
        for s in range(n_rep):
            counts[s] = 0
        for l in range(lists.shape[1]):
            variant = lists[me, l]
            owner = slot[variant] // pool_dev
            k = counts[owner]
            counts[owner] = k + 1
            names[owner * cap + jnp.minimum(k, cap - 1)] = variant

        def place(i):
            return lax.rem(me - i // cap + n_rep, n_rep) * cap + i % cap

        asked[...] = asked_entries(names, wanted[...], member, place, n_rep * cap, rank).astype(BF16)


def select(slot, lists, pool, by_shift, by_target, wanted, n_rep, cap, after=()):
    pool_dev, rank, width = pool.shape
    shapes = [in_hbm((cap * rank, stop - start)) for start, stop in by_shift for _ in range(n_rep)]
    shapes += [in_hbm((n_rep, cap * rank, stop - start)) for start, stop in by_target]
    specs = [VMEM] * len(shapes)
    rows = 128
    for x in wanted:
        rows = x.shape[1]
        shapes += [in_hbm((n_rep * cap,), jnp.int32), in_hbm((rows, n_rep * cap * rank))]
        specs += [SMEM, VMEM]
    return pl.pallas_call(
        functools.partial(select_kernel, by_shift, by_target, len(wanted), n_rep, cap, pool_dev, rank),
        out_shape=[*shapes, TOKEN],
        in_specs=[SMEM, SMEM, VMEM] + [VMEM] * len(wanted) + [ANY] * len(after),
        out_specs=[*specs, VMEM],
        scratch_shapes=[
            pltpu.SMEM((cap + 1,), jnp.int32),
            pltpu.SMEM((n_rep,), jnp.int32),
            pltpu.VMEM((-(-n_rep * cap // 16) * 16, rows), F32),
        ],
        compiler_params=params(16),
        cost_estimate=order(0),
        name="select",
    )(*pin(slot, lists, pool, *wanted), *pin(*after))


def product_early_kernel(per, pos, features, weights, keep0, send0, keep1, send1, token):
    token[...] = jnp.zeros_like(token)
    j = pl.program_id(0)
    own = features.shape[0] // 2
    result = jnp.dot(features[...], weights[...], preferred_element_type=F32).astype(BF16)
    for core in range(2):
        a, b = core * own, (1 - core) * own
        for block, keep, send in ((0, keep0, send0), (1, keep1, send1)):

            @pl.when((pos[1] == core) & (j // per == block))
            def _():
                keep[...] = result[a : a + own]
                send[...] = result[b : b + own]


def product_early(features, projection, tile, after=()):
    rows, depth = features.shape
    width = projection.shape[1] // 4
    half = rows // 2
    per = width // tile

    def kernel(features, weights, *rest):
        product_early_kernel(per, position(), features, weights, *rest[-5:])

    low = pl.BlockSpec((half // 2, tile), lambda j, pos: (0, jnp.minimum(j, per - 1)))
    high = pl.BlockSpec((half // 2, tile), lambda j, pos: (0, jnp.maximum(j - per, 0)))
    return pl.pallas_call(
        kernel,
        out_shape=[sds((half // 2, width))] * 4 + [TOKEN],
        grid_spec=grid_spec(
            grid=(2 * per,),
            in_specs=[
                pl.BlockSpec((half, depth), lambda j, pos: (1 - pos[0], 0)),
                pl.BlockSpec((depth, tile), lambda j, pos: (0, 2 * (1 - pos[0]) * per + j)),
            ]
            + [ANY] * len(after),
            out_specs=[low, low, high, high, pl.BlockSpec((8, 128), lambda j, pos: (0, 0))],
        ),
        compiler_params=params(),
        cost_estimate=order(0),
        name="product",
    )(features, projection, *pin(*after))


def product_columns_kernel(per, pos, features, weights, late, late_send, keep, send, token):
    token[...] = jnp.zeros_like(token)
    j = pl.program_id(0)
    half = features.shape[0] // 2
    own = half // 2
    result = jnp.dot(features[...], weights[...], preferred_element_type=F32).astype(BF16)
    for chip in range(2):
        here = pos[0] == chip
        other = result[(1 - chip) * half : (2 - chip) * half]

        @pl.when(here & (j < per))
        def _():
            late[...] = other

        @pl.when(here & (j >= per))
        def _():
            late_send[...] = other

        for core in range(2):

            @pl.when(here & (pos[1] == core))
            def _():
                keep[...] = result[chip * half + core * own : chip * half + (core + 1) * own][None]
                send[...] = result[chip * half + (1 - core) * own : chip * half + (2 - core) * own][None]


def product_columns(features, projection, tile, after=()):
    rows, depth = features.shape
    width = projection.shape[1] // 4
    half = rows // 2
    per = width // tile

    def block(j, pos):
        return jnp.where(j < per, pos[1], 1 - pos[1])

    rest = pl.BlockSpec((1, half // 2, tile), lambda j, pos: (block(j, pos), 0, lax.rem(j, per)))

    def kernel(features, weights, *rest):
        product_columns_kernel(per, position(), features, weights, *rest[-5:])

    return pl.pallas_call(
        kernel,
        out_shape=[in_hbm((half, width))] * 2 + [in_hbm((2, half // 2, width))] * 2 + [TOKEN],
        grid_spec=grid_spec(
            grid=(2 * per,),
            in_specs=[
                pl.BlockSpec((rows, depth), lambda j, pos: (0, 0)),
                pl.BlockSpec((depth, tile), lambda j, pos: (0, (2 * pos[0] + block(j, pos)) * per + lax.rem(j, per))),
            ]
            + [ANY] * len(after),
            out_specs=[
                pl.BlockSpec((half, tile), lambda j, pos: (0, jnp.minimum(j, per - 1))),
                pl.BlockSpec((half, tile), lambda j, pos: (0, jnp.maximum(j - per, 0))),
                rest,
                rest,
                pl.BlockSpec((8, 128), lambda j, pos: (0, 0)),
            ],
        ),
        compiler_params=params(),
        cost_estimate=order(0),
        name="product",
    )(features, projection, *pin(*after))


def product_kernel(split, pos, features, weights, keep, send, token):
    token[...] = jnp.zeros_like(token)
    own = features.shape[0] // 2
    result = jnp.dot(features[...], weights[...], preferred_element_type=F32).astype(BF16)
    low, high = result[:own], result[own:]
    if split:
        low, high = low[None], high[None]

    @pl.when(pos[1] == 0)
    def _():
        keep[...] = low
        send[...] = high

    @pl.when(pos[1] == 1)
    def _():
        keep[...] = high
        send[...] = low


def product(features, projection, other_rows, other_cols, first, count, tile, blocks, after=()):
    rows, depth = features.shape
    width = projection.shape[1]
    half = rows // 2
    own = half // 2
    tiles = count // tile

    def row_block(j, pos):
        return ((1 - pos[0]) if other_rows else pos[0], 0)

    def col_block(j, pos):
        if other_cols is None:
            return (0, j + first // tile)
        chip = (1 - pos[0]) if other_cols else pos[0]
        return (0, chip * (width // 2 // tile) + j + first // tile)

    if blocks > 1:
        per = tiles // blocks
        shape = (blocks, own, count // blocks)
        out_spec = pl.BlockSpec((1, own, tile), lambda j, pos: (j // per, 0, j % per))
    else:
        shape = (own, count)
        out_spec = pl.BlockSpec((own, tile), lambda j, pos: (0, j))
    body = functools.partial(product_kernel, blocks > 1)

    def kernel(features, weights, *rest):
        body(position(), features, weights, *rest[-3:])

    return pl.pallas_call(
        kernel,
        out_shape=[in_hbm(shape) if blocks > 1 else sds(shape)] * 2 + [TOKEN],
        grid_spec=grid_spec(
            grid=(tiles,),
            in_specs=[pl.BlockSpec((half, depth), row_block), pl.BlockSpec((depth, tile), col_block)]
            + [ANY] * len(after),
            out_specs=[out_spec] * 2 + [pl.BlockSpec((8, 128), lambda j, pos: (0, 0))],
        ),
        compiler_params=params(),
        cost_estimate=order(0),
        name="product",
    )(features, projection, *pin(*after))


def score_kernel(rank, names, wanted, features, factors, *rest):
    out, scores = rest[-2:]
    scores[...] = lax.dot_general(
        factors[...], features[...], (((1,), (1,)), ((), ())), preferred_element_type=F32
    )
    total = jnp.zeros(out.shape, F32)
    for i in range(factors.shape[0] // rank):
        total += jnp.where(wanted[...] == names[i], scores[i * rank : (i + 1) * rank, :], 0.0)
    out[...] = total


def score(names, wanted, features, factors, rank, after=()):
    rows = features.shape[0]
    return pl.pallas_call(
        functools.partial(score_kernel, rank),
        out_shape=sds((rank, rows), F32),
        in_specs=[SMEM] + [VMEM] * 3 + [ANY] * len(after),
        out_specs=VMEM,
        scratch_shapes=[pltpu.VMEM((factors.shape[0], rows), F32)],
        compiler_params=params(),
        cost_estimate=order(40),
        name="score",
    )(*pin(names, wanted), features, *pin(factors), *pin(*after))


def delta_kernel(n_blocks, n_before, known, n_rep, cap, rank, names, wanted, shrunk, late_own, late_recv, *rest):
    blocks, before = rest[:n_blocks], rest[n_blocks : n_blocks + n_before]
    straight, cross = rest[-7:-5] if before else rest[-5:-3]
    member, expand, result = rest[-3:]
    chip, core, me = position()
    listed = n_rep * cap
    half = late_own.shape[0]
    own = half // 2

    def product_of(factors, rows, known=None):
        columns = pl.ds(pl.multiple_of(rows * half, half), half)
        if known is None:
            by_owner = len(factors) == 1

            def place(i):
                return i if by_owner else lax.rem(me - i // cap + n_rep, n_rep) * cap + i % cap

            named = asked_entries(names, wanted[:, columns], member, place, listed, rank)
        else:
            named = known[...].astype(F32)
        total = jnp.sum(shrunk[:, :, columns], axis=0).astype(BF16)
        part = lax.broadcasted_iota(jnp.int32, (rank, listed * rank), 0)
        column = lax.broadcasted_iota(jnp.int32, (rank, listed * rank), 1)
        to_part = jnp.where(lax.rem(column, rank) == part, 1.0, 0.0).astype(BF16)
        turned = (((0,), (0,)), ((), ()))
        copied = lax.dot_general(total, to_part, turned, preferred_element_type=F32)
        size = listed * rank // len(factors)
        for s, factor in enumerate(factors):
            expand[pl.ds(s * size, size), :] = factor[...]
        result[...] = jnp.dot((named * copied).astype(BF16), expand[...], preferred_element_type=F32)

    product_of(blocks, 1 - chip, rest[n_blocks + n_before] if known else None)
    for out, c in ((straight, core), (cross, 1 - core)):
        rows = pl.ds(pl.multiple_of(c * own, own), own)
        base = late_own[rows, :].astype(F32) + late_recv[rows, :].astype(F32)
        out[...] = (base + result[rows, :]).astype(BF16)
    if before:
        mine, send = rest[-5], rest[-4]
        width = straight.shape[1]
        for start, factors in ((0, before), (mine.shape[1] - width, blocks)):
            product_of(factors, chip)
            for out, c in ((mine, core), (send, 1 - core)):
                rows = pl.ds(pl.multiple_of(c * own, own), own)
                out[:, start : start + width] = result[rows, :].astype(BF16)


def delta(names, wanted, shrunk, late, blocks, cut, n_rep, cap, rank, own, before=(), after=(), asked=()):
    start, stop = cut
    width = stop - start
    listed = n_rep * cap
    shapes = [in_hbm((own, width))] * 2 + ([in_hbm((own, stop))] * 2 if before else [])
    return pl.pallas_call(
        functools.partial(delta_kernel, len(blocks), len(before), len(asked), n_rep, cap, rank),
        out_shape=shapes,
        grid=(1,),
        in_specs=[SMEM]
        + [VMEM] * 2
        + [pl.BlockSpec((2 * own, width), lambda i: (0, start // width))] * 2
        + [VMEM] * (len(blocks) + len(before))
        + [pl.BlockSpec((2 * own, listed * rank), lambda i: (1 - position()[0], 0))] * len(asked)
        + [ANY] * len(after),
        out_specs=[VMEM] * len(shapes),
        scratch_shapes=[
            pltpu.VMEM((-(-listed // 16) * 16, 2 * own), F32),
            pltpu.VMEM((listed * rank, width), BF16),
            pltpu.VMEM((2 * own, width), F32),
        ],
        compiler_params=params(),
        cost_estimate=order(0),
        name="delta",
    )(*pin(names, wanted), shrunk, *pin(late[0]), *(pin(late[1]) if before else late[1:]), *pin(*blocks, *before, *asked, *after))


def gate_kernel(*refs):
    pass


def gate(arrays, after):
    n = len(arrays)
    return pl.pallas_call(
        gate_kernel,
        out_shape=[sds(x.shape, x.dtype) for x in arrays],
        in_specs=[ANY] * (n + len(after)),
        out_specs=[ANY] * n,
        input_output_aliases={i: i for i in range(n)},
        cost_estimate=order(100),
        name="gate",
    )(*arrays, *pin(*after))


def near_kernel(residual, keep, recv, first, second, mine, theirs, *rest):
    out = rest[-1]
    block = pl.program_id(0)
    total = residual[...].astype(F32) + keep[0].astype(F32) + recv[0].astype(F32)
    total += jnp.where(block == 0, first[...], second[...]).astype(F32)
    total += jnp.where(block == position()[1], mine[...], theirs[...]).astype(F32)
    out[...] = total.astype(BF16)


def far_kernel(residual, keep, recv, straight, cross, *rest):
    out = rest[-1]
    total = residual[...].astype(F32) + keep[0].astype(F32) + recv[0].astype(F32)
    total += jnp.where(pl.program_id(0) == position()[1], straight[...], cross[...]).astype(F32)
    out[...] = total.astype(BF16)


def finish(out, residual, base, start, stop, near, pieces, after=()):
    own, full = residual.shape
    width = full // 4
    size = stop - start
    tile = min(TILE, math.gcd(size, start, width))
    count = size // tile
    skip = start // tile

    def place(b, j, pos):
        chip = pos[0] if near else 1 - pos[0]
        return (0, (2 * chip + b) * (width // tile) + skip + j)

    whole = pl.BlockSpec((own, tile), place)
    halves = [
        lambda b, j, pos: (0, skip + jnp.where(b == 0, j, count - 1)),
        lambda b, j, pos: (0, skip + jnp.where(b == 1, j, 0)),
    ]
    by_block = [pl.BlockSpec((own, tile), f) for f in halves]

    def by_core(offset):
        def index(b, j, pos):
            half = pos[1] ^ offset
            return (0, jnp.where(b == half, j, jnp.where(half == 0, count - 1, 0)))

        return pl.BlockSpec((own, tile), index)

    part = pl.BlockSpec((1, own, tile), lambda b, j, pos: (b, 0, skip + j))
    specs = [part, part, *(by_block if near else []), by_core(0), by_core(1)]
    specs = specs + [ANY] * len(after)
    operands = [*pin(residual, *base), *pieces, *pin(*after)]
    aliases = {}
    if out is not None:
        specs = specs + [ANY]
        aliases = {len(operands): 0}
        operands.append(out)
    return pl.pallas_call(
        near_kernel if near else far_kernel,
        out_shape=sds((own, full)),
        grid_spec=grid_spec(
            grid=(2, count),
            in_specs=[whole, *specs],
            out_specs=whole,
        ),
        input_output_aliases=aliases,
        compiler_params=params(),
        cost_estimate=order(60),
        name="near" if near else "far",
    )(*operands)


def paired(
    head_outputs, residual, projection, shrink_pool, expand_pool, pool_slot, variant_list, request_variant
):
    n_rep = lax.axis_size("rep")
    features = head_outputs[0]
    rows = features.shape[0]
    own = rows // 4
    pool_dev, rank, width = shrink_pool.shape
    cap = pool_dev // 4 + 2
    stream = residual[0]
    sizes = (cap, rank)
    tile = min(1024, width)
    cut = width // 2
    cuts = ((0, cut), (cut, width))

    def over_core(x):
        return lax.ppermute(x, "tp", [(0, 1), (1, 0), (2, 3), (3, 2)])

    def over_chip(x):
        return lax.ppermute(x, "tp", [(0, 2), (2, 0), (1, 3), (3, 1)])

    def over_both(x):
        return lax.ppermute(x, "tp", [(0, 3), (3, 0), (1, 2), (2, 1)])

    def over_rep(x, shift):
        return lax.ppermute(x, "rep", [(i, (i + shift) % n_rep) for i in range(n_rep)])

    shifts = [s for s in range(1, n_rep) if s != n_rep // 2] + [n_rep // 2]
    chosen, token = select(pool_slot, variant_list, shrink_pool, (), ((0, width),), (), n_rep, cap)
    shrink = lax.all_to_all(chosen, "rep", 0, 0, tiled=True).reshape(n_rep * cap * rank, width)

    keep0, send0, keep1, send1, token = product_early(features, projection, tile, [token])
    sums = [keep0 + over_core(send0), keep1 + over_core(send1)]
    early = [over_chip(x) for x in sums]

    *chosen, second, names, asked, token = select(
        pool_slot, variant_list, expand_pool, cuts[:1], cuts[1:], [request_variant], n_rep, cap, sums
    )
    first = [chosen[0]] + [None] * (n_rep - 1)
    for s in shifts:
        first[s] = over_rep(chosen[s], s)
    second = lax.all_to_all(second, "rep", 0, 0, tiled=True).reshape(n_rep * cap * rank, cut)

    late_keep, late_send, keep, send, token = product_columns(features, projection, tile, [*sums, token])
    late = (late_keep, over_core(late_send))
    near_base = (keep, over_core(send))

    part = score(names, request_variant, features, shrink, rank, [token, early[0]])
    shrunk = lax.all_gather(part, "tp")

    common = (names, request_variant, shrunk, late)
    straight, cross = delta(*common, first, cuts[0], n_rep, *sizes, own, (), [early[1]], [asked])
    far = [over_chip(straight), over_both(cross)]
    straight, cross, mine, send = delta(*common, [second], cuts[1], n_rep, *sizes, own, first, [near_base[1], straight])
    last = [over_chip(straight), over_both(cross)]
    theirs = over_core(send)
    keep, send, token = product(features, projection, False, True, 0, 2 * width, tile, 2, [mine])
    far_base = (keep, over_core(send))
    far = gate(far, [token])
    out = finish(None, stream, near_base, 0, width, True, [*early, mine, theirs], far)
    out = finish(out, stream, far_base, *cuts[0], False, far)
    out = finish(out, stream, far_base, *cuts[1], False, last)
    return out[None]


def general(
    head_outputs, residual, projection, shrink_pool, expand_pool, pool_slot, variant_list, request_variant
):
    split_count = lax.axis_size("tp")
    split_index = lax.axis_index("tp")
    replica_index = lax.axis_index("rep")
    row_count = head_outputs.shape[1]
    local_width = head_outputs.shape[2]
    rank_size = shrink_pool.shape[1]
    listed = variant_list.shape[1]
    own_rows = row_count // split_count
    flat_size = rank_size * local_width
    features = head_outputs[0]
    wanted = request_variant[0]
    my_list = lax.dynamic_index_in_dim(variant_list, replica_index, 0, keepdims=False)
    my_positions = jnp.take(pool_slot, my_list, axis=0)
    pieces = (
        lax.all_gather(shrink_pool, "rep", axis=0, tiled=True),
        lax.all_gather(expand_pool, "rep", axis=0, tiled=True),
    )
    piece_rows = pieces[0].shape[0]
    matches = (my_positions[:, None] == jnp.arange(piece_rows, dtype=jnp.int32)[None, :]).astype(BF16)
    shrink_sel = jnp.dot(matches, pieces[0].reshape(piece_rows, flat_size), preferred_element_type=F32)
    expand_sel = jnp.dot(matches, pieces[1].reshape(piece_rows, flat_size), preferred_element_type=F32)
    shrink_sel = shrink_sel.astype(BF16).reshape(listed * rank_size, local_width)
    expand_sel = expand_sel.astype(BF16).reshape(listed, rank_size, local_width)
    member = wanted[:, None] == my_list[None, :]
    scores = lax.dot_general(
        features, shrink_sel, (((1,), (1,)), ((), ())), preferred_element_type=F32
    )
    shrunk = jnp.sum(scores.reshape(row_count, listed, rank_size) * member[:, :, None], axis=1)
    own_shrunk = lax.psum_scatter(shrunk.astype(BF16), "tp", scatter_dimension=0, tiled=True)
    own_member = lax.dynamic_slice_in_dim(member, split_index * own_rows, own_rows, 0)
    spread = own_member[:, :, None] * own_shrunk[:, None, :]
    spread = spread.reshape(own_rows, listed * rank_size)
    piece = lax.all_gather(expand_sel, "tp", axis=2, tiled=True)
    delta_rows = jnp.dot(
        spread, piece.reshape(listed * rank_size, piece.shape[2]), preferred_element_type=F32
    )
    base_rows = lax.psum_scatter(
        jnp.dot(features, projection, preferred_element_type=F32).astype(BF16),
        "tp",
        scatter_dimension=0,
        tiled=True,
    ).astype(F32)
    return (residual[0].astype(F32) + base_rows + delta_rows).astype(BF16)[None]


def solution(mesh):
    in_specs = (
        P(("groups", "rep"), None, "tp"),
        P(("groups", "rep"), "tp", None),
        P("tp", None),
        P(("groups", "rep"), None, "tp"),
        P(("groups", "rep"), None, "tp"),
        P("groups"),
        P("groups", None),
        P(("groups", "rep"), None),
    )
    out_specs = P(("groups", "rep"), "tp", None)
    local = paired if mesh.shape["tp"] == 4 else general
    return jax.shard_map(local, mesh=mesh, in_specs=in_specs, out_specs=out_specs, check_vma=False)
```

```python
import functools
import math

import jax
import jax.numpy as jnp
from jax import lax
from jax.experimental import pallas as pl
from jax.experimental.pallas import tpu as pltpu
from jax.sharding import PartitionSpec as P

ANY = pl.BlockSpec(memory_space=pl.ANY)
HBM = pl.BlockSpec(memory_space=pltpu.HBM)
SMEM = pl.BlockSpec(memory_space=pltpu.SMEM)
VMEM = pl.BlockSpec(memory_space=pltpu.VMEM)
BF16 = jnp.bfloat16
F32 = jnp.float32
TILE = 1024


def order(us):
    return pl.CostEstimate(flops=int(us * 1.15e9) + 1, bytes_accessed=1, transcendentals=0)


def position():
    index = lax.axis_index("tp")
    return lax.div(index, 2), lax.rem(index, 2), lax.axis_index("rep")


def placed(spec):
    if spec.index_map is None:
        return spec
    return pl.BlockSpec(spec.block_shape, lambda *ids: spec.index_map(*ids, position()))


def grid_spec(grid, in_specs, out_specs):
    specs = out_specs if isinstance(out_specs, list) else [out_specs]
    specs = [placed(x) for x in specs]
    return pl.GridSpec(
        grid=grid,
        in_specs=[placed(x) for x in in_specs],
        out_specs=specs if isinstance(out_specs, list) else specs[0],
    )


def params(mib=48):
    return pltpu.CompilerParams(vmem_limit_bytes=mib * 2**20)


def sds(shape, dtype=BF16):
    return jax.ShapeDtypeStruct(shape, dtype)


def in_hbm(shape, dtype=BF16):
    return pltpu.HBM(shape, dtype)


def pin(*arrays):
    return [pltpu.with_memory_space_constraint(x, pltpu.HBM) for x in arrays]


TOKEN = in_hbm((8, 128), F32)


def asked_entries(names, wanted, member, place, listed, rank):
    member[...] = jnp.zeros_like(member)
    for i in range(listed):
        member[i : i + 1, :] = jnp.where(wanted == names[place(i)], 1.0, 0.0)
    entry = lax.broadcasted_iota(jnp.int32, (member.shape[0], listed * rank), 0)
    column = lax.broadcasted_iota(jnp.int32, (member.shape[0], listed * rank), 1)
    to_entry = jnp.where(column // rank == entry, 1.0, 0.0).astype(BF16)
    return lax.dot_general(
        member[...].astype(BF16), to_entry, (((0,), (0,)), ((), ())), preferred_element_type=F32
    )


def select_kernel(by_shift, by_target, named, n_rep, cap, pool_dev, rank, slot, lists, pool, *rest):
    token, idx, counts, member = rest[-4:]
    outs = rest[:-4]
    outs = outs[-(n_rep * len(by_shift) + len(by_target) + 2 * named) :]
    token[...] = jnp.zeros_like(token)
    me = lax.axis_index("rep")
    base = me * pool_dev
    for shift in range(n_rep):
        target = lax.rem(me + shift, n_rep)
        for k in range(cap + 1):
            idx[k] = 0
        count = jnp.int32(0)
        for l in range(lists.shape[1]):
            place = slot[lists[target, l]] - base
            idx[jnp.minimum(count, cap)] = place
            count = count + jnp.where((place >= 0) & (place < pool_dev), 1, 0)
        for k in range(cap):
            entry = jnp.clip(idx[k], 0, pool_dev - 1)
            rows = pl.ds(k * rank, rank)
            for c, (start, stop) in enumerate(by_shift):
                outs[c * n_rep + shift][rows, :] = pool[entry, :, start:stop]
            for c, (start, stop) in enumerate(by_target):
                outs[len(by_shift) * n_rep + c][target, rows, :] = pool[entry, :, start:stop]
    if named:
        names, asked, wanted = outs[-2], outs[-1], rest[0]
        for i in range(n_rep * cap):
            names[i] = -1
        for s in range(n_rep):
            counts[s] = 0
        for l in range(lists.shape[1]):
            variant = lists[me, l]
            owner = slot[variant] // pool_dev
            k = counts[owner]
            counts[owner] = k + 1
            names[owner * cap + jnp.minimum(k, cap - 1)] = variant

        def place(i):
            return lax.rem(me - i // cap + n_rep, n_rep) * cap + i % cap

        asked[...] = asked_entries(names, wanted[...], member, place, n_rep * cap, rank).astype(BF16)


def select(slot, lists, pool, by_shift, by_target, wanted, n_rep, cap, after=()):
    pool_dev, rank, width = pool.shape
    shapes = [in_hbm((cap * rank, stop - start)) for start, stop in by_shift for _ in range(n_rep)]
    shapes += [in_hbm((n_rep, cap * rank, stop - start)) for start, stop in by_target]
    specs = [VMEM] * len(shapes)
    rows = 128
    for x in wanted:
        rows = x.shape[1]
        shapes += [in_hbm((n_rep * cap,), jnp.int32), in_hbm((rows, n_rep * cap * rank))]
        specs += [SMEM, VMEM]
    return pl.pallas_call(
        functools.partial(select_kernel, by_shift, by_target, len(wanted), n_rep, cap, pool_dev, rank),
        out_shape=[*shapes, TOKEN],
        in_specs=[SMEM, SMEM, VMEM] + [VMEM] * len(wanted) + [ANY] * len(after),
        out_specs=[*specs, VMEM],
        scratch_shapes=[
            pltpu.SMEM((cap + 1,), jnp.int32),
            pltpu.SMEM((n_rep,), jnp.int32),
            pltpu.VMEM((-(-n_rep * cap // 16) * 16, rows), F32),
        ],
        compiler_params=params(16),
        cost_estimate=order(0),
        name="select",
    )(*pin(slot, lists, pool, *wanted), *pin(*after))


def product_early_kernel(per, pos, features, weights, keep0, send0, keep1, send1, token):
    token[...] = jnp.zeros_like(token)
    j = pl.program_id(0)
    own = features.shape[0] // 2
    result = jnp.dot(features[...], weights[...], preferred_element_type=F32).astype(BF16)
    for core in range(2):
        a, b = core * own, (1 - core) * own
        for block, keep, send in ((0, keep0, send0), (1, keep1, send1)):

            @pl.when((pos[1] == core) & (j // per == block))
            def _():
                keep[...] = result[a : a + own]
                send[...] = result[b : b + own]


def product_early(features, projection, tile, after=()):
    rows, depth = features.shape
    width = projection.shape[1] // 4
    half = rows // 2
    per = width // tile

    def kernel(features, weights, *rest):
        product_early_kernel(per, position(), features, weights, *rest[-5:])

    low = pl.BlockSpec((half // 2, tile), lambda j, pos: (0, jnp.minimum(j, per - 1)))
    high = pl.BlockSpec((half // 2, tile), lambda j, pos: (0, jnp.maximum(j - per, 0)))
    return pl.pallas_call(
        kernel,
        out_shape=[sds((half // 2, width))] * 4 + [TOKEN],
        grid_spec=grid_spec(
            grid=(2 * per,),
            in_specs=[
                pl.BlockSpec((half, depth), lambda j, pos: (1 - pos[0], 0)),
                pl.BlockSpec((depth, tile), lambda j, pos: (0, 2 * (1 - pos[0]) * per + j)),
            ]
            + [ANY] * len(after),
            out_specs=[low, low, high, high, pl.BlockSpec((8, 128), lambda j, pos: (0, 0))],
        ),
        compiler_params=params(),
        cost_estimate=order(0),
        name="product",
    )(features, projection, *pin(*after))


def product_columns_kernel(per, pos, features, weights, late, late_send, keep, send, token):
    token[...] = jnp.zeros_like(token)
    j = pl.program_id(0)
    half = features.shape[0] // 2
    own = half // 2
    result = jnp.dot(features[...], weights[...], preferred_element_type=F32).astype(BF16)
    for chip in range(2):
        here = pos[0] == chip
        other = result[(1 - chip) * half : (2 - chip) * half]

        @pl.when(here & (j < per))
        def _():
            late[...] = other

        @pl.when(here & (j >= per))
        def _():
            late_send[...] = other

        for core in range(2):

            @pl.when(here & (pos[1] == core))
            def _():
                keep[...] = result[chip * half + core * own : chip * half + (core + 1) * own][None]
                send[...] = result[chip * half + (1 - core) * own : chip * half + (2 - core) * own][None]


def product_columns(features, projection, tile, after=()):
    rows, depth = features.shape
    width = projection.shape[1] // 4
    half = rows // 2
    per = width // tile

    def block(j, pos):
        return jnp.where(j < per, pos[1], 1 - pos[1])

    rest = pl.BlockSpec((1, half // 2, tile), lambda j, pos: (block(j, pos), 0, lax.rem(j, per)))

    def kernel(features, weights, *rest):
        product_columns_kernel(per, position(), features, weights, *rest[-5:])

    return pl.pallas_call(
        kernel,
        out_shape=[in_hbm((half, width))] * 2 + [in_hbm((2, half // 2, width))] * 2 + [TOKEN],
        grid_spec=grid_spec(
            grid=(2 * per,),
            in_specs=[
                pl.BlockSpec((rows, depth), lambda j, pos: (0, 0)),
                pl.BlockSpec((depth, tile), lambda j, pos: (0, (2 * pos[0] + block(j, pos)) * per + lax.rem(j, per))),
            ]
            + [ANY] * len(after),
            out_specs=[
                pl.BlockSpec((half, tile), lambda j, pos: (0, jnp.minimum(j, per - 1))),
                pl.BlockSpec((half, tile), lambda j, pos: (0, jnp.maximum(j - per, 0))),
                rest,
                rest,
                pl.BlockSpec((8, 128), lambda j, pos: (0, 0)),
            ],
        ),
        compiler_params=params(),
        cost_estimate=order(0),
        name="product",
    )(features, projection, *pin(*after))


def product_kernel(split, pos, features, weights, keep, send, token):
    token[...] = jnp.zeros_like(token)
    own = features.shape[0] // 2
    result = jnp.dot(features[...], weights[...], preferred_element_type=F32).astype(BF16)
    low, high = result[:own], result[own:]
    if split:
        low, high = low[None], high[None]

    @pl.when(pos[1] == 0)
    def _():
        keep[...] = low
        send[...] = high

    @pl.when(pos[1] == 1)
    def _():
        keep[...] = high
        send[...] = low


def product(features, projection, other_rows, other_cols, first, count, tile, blocks, after=()):
    rows, depth = features.shape
    width = projection.shape[1]
    half = rows // 2
    own = half // 2
    tiles = count // tile

    def row_block(j, pos):
        return ((1 - pos[0]) if other_rows else pos[0], 0)

    def col_block(j, pos):
        if other_cols is None:
            return (0, j + first // tile)
        chip = (1 - pos[0]) if other_cols else pos[0]
        return (0, chip * (width // 2 // tile) + j + first // tile)

    if blocks > 1:
        per = tiles // blocks
        shape = (blocks, own, count // blocks)
        out_spec = pl.BlockSpec((1, own, tile), lambda j, pos: (j // per, 0, j % per))
    else:
        shape = (own, count)
        out_spec = pl.BlockSpec((own, tile), lambda j, pos: (0, j))
    body = functools.partial(product_kernel, blocks > 1)

    def kernel(features, weights, *rest):
        body(position(), features, weights, *rest[-3:])

    return pl.pallas_call(
        kernel,
        out_shape=[in_hbm(shape) if blocks > 1 else sds(shape)] * 2 + [TOKEN],
        grid_spec=grid_spec(
            grid=(tiles,),
            in_specs=[pl.BlockSpec((half, depth), row_block), pl.BlockSpec((depth, tile), col_block)]
            + [ANY] * len(after),
            out_specs=[out_spec] * 2 + [pl.BlockSpec((8, 128), lambda j, pos: (0, 0))],
        ),
        compiler_params=params(),
        cost_estimate=order(0),
        name="product",
    )(features, projection, *pin(*after))


def score_kernel(rank, names, wanted, features, factors, *rest):
    out, scores = rest[-2:]
    scores[...] = lax.dot_general(
        factors[...], features[...], (((1,), (1,)), ((), ())), preferred_element_type=F32
    )
    total = jnp.zeros(out.shape, F32)
    for i in range(factors.shape[0] // rank):
        total += jnp.where(wanted[...] == names[i], scores[i * rank : (i + 1) * rank, :], 0.0)
    out[...] = total


def score(names, wanted, features, factors, rank, after=()):
    rows = features.shape[0]
    return pl.pallas_call(
        functools.partial(score_kernel, rank),
        out_shape=sds((rank, rows), F32),
        in_specs=[SMEM] + [VMEM] * 3 + [ANY] * len(after),
        out_specs=VMEM,
        scratch_shapes=[pltpu.VMEM((factors.shape[0], rows), F32)],
        compiler_params=params(),
        cost_estimate=order(40),
        name="score",
    )(*pin(names, wanted), features, *pin(factors), *pin(*after))


def delta_kernel(n_blocks, n_before, known, n_rep, cap, rank, names, wanted, shrunk, late_own, late_recv, *rest):
    blocks, before = rest[:n_blocks], rest[n_blocks : n_blocks + n_before]
    straight, cross = rest[-7:-5] if before else rest[-5:-3]
    member, expand, result = rest[-3:]
    chip, core, me = position()
    listed = n_rep * cap
    half = late_own.shape[0]
    own = half // 2

    def product_of(factors, rows, known=None):
        columns = pl.ds(pl.multiple_of(rows * half, half), half)
        if known is None:
            by_owner = len(factors) == 1

            def place(i):
                return i if by_owner else lax.rem(me - i // cap + n_rep, n_rep) * cap + i % cap

            named = asked_entries(names, wanted[:, columns], member, place, listed, rank)
        else:
            named = known[...].astype(F32)
        total = jnp.sum(shrunk[:, :, columns], axis=0).astype(BF16)
        part = lax.broadcasted_iota(jnp.int32, (rank, listed * rank), 0)
        column = lax.broadcasted_iota(jnp.int32, (rank, listed * rank), 1)
        to_part = jnp.where(lax.rem(column, rank) == part, 1.0, 0.0).astype(BF16)
        turned = (((0,), (0,)), ((), ()))
        copied = lax.dot_general(total, to_part, turned, preferred_element_type=F32)
        size = listed * rank // len(factors)
        for s, factor in enumerate(factors):
            expand[pl.ds(s * size, size), :] = factor[...]
        result[...] = jnp.dot((named * copied).astype(BF16), expand[...], preferred_element_type=F32)

    product_of(blocks, 1 - chip, rest[n_blocks + n_before] if known else None)
    for out, c in ((straight, core), (cross, 1 - core)):
        rows = pl.ds(pl.multiple_of(c * own, own), own)
        base = late_own[rows, :].astype(F32) + late_recv[rows, :].astype(F32)
        out[...] = (base + result[rows, :]).astype(BF16)
    if before:
        mine, send = rest[-5], rest[-4]
        width = straight.shape[1]
        for start, factors in ((0, before), (mine.shape[1] - width, blocks)):
            product_of(factors, chip)
            for out, c in ((mine, core), (send, 1 - core)):
                rows = pl.ds(pl.multiple_of(c * own, own), own)
                out[:, start : start + width] = result[rows, :].astype(BF16)


def delta(names, wanted, shrunk, late, blocks, cut, n_rep, cap, rank, own, before=(), after=(), asked=()):
    start, stop = cut
    width = stop - start
    listed = n_rep * cap
    shapes = [in_hbm((own, width))] * 2 + ([in_hbm((own, stop))] * 2 if before else [])
    return pl.pallas_call(
        functools.partial(delta_kernel, len(blocks), len(before), len(asked), n_rep, cap, rank),
        out_shape=shapes,
        grid=(1,),
        in_specs=[SMEM]
        + [VMEM] * 2
        + [pl.BlockSpec((2 * own, width), lambda i: (0, start // width))] * 2
        + [VMEM] * (len(blocks) + len(before))
        + [pl.BlockSpec((2 * own, listed * rank), lambda i: (1 - position()[0], 0))] * len(asked)
        + [ANY] * len(after),
        out_specs=[VMEM] * len(shapes),
        scratch_shapes=[
            pltpu.VMEM((-(-listed // 16) * 16, 2 * own), F32),
            pltpu.VMEM((listed * rank, width), BF16),
            pltpu.VMEM((2 * own, width), F32),
        ],
        compiler_params=params(),
        cost_estimate=order(0),
        name="delta",
    )(*pin(names, wanted), shrunk, *pin(late[0]), *(pin(late[1]) if before else late[1:]), *pin(*blocks, *before, *asked, *after))


def gate_kernel(*refs):
    pass


def gate(arrays, after):
    n = len(arrays)
    return pl.pallas_call(
        gate_kernel,
        out_shape=[sds(x.shape, x.dtype) for x in arrays],
        in_specs=[ANY] * (n + len(after)),
        out_specs=[ANY] * n,
        input_output_aliases={i: i for i in range(n)},
        cost_estimate=order(100),
        name="gate",
    )(*arrays, *pin(*after))


def near_kernel(residual, keep, recv, first, second, mine, theirs, *rest):
    out = rest[-1]
    block = pl.program_id(0)
    total = residual[...].astype(F32) + keep[0].astype(F32) + recv[0].astype(F32)
    total += jnp.where(block == 0, first[...], second[...]).astype(F32)
    total += jnp.where(block == position()[1], mine[...], theirs[...]).astype(F32)
    out[...] = total.astype(BF16)


def far_kernel(residual, keep, recv, straight, cross, *rest):
    out = rest[-1]
    total = residual[...].astype(F32) + keep[0].astype(F32) + recv[0].astype(F32)
    total += jnp.where(pl.program_id(0) == position()[1], straight[...], cross[...]).astype(F32)
    out[...] = total.astype(BF16)


def finish(out, residual, base, start, stop, near, pieces, after=(), pinned=True):
    own, full = residual.shape
    width = full // 4
    size = stop - start
    tile = min(TILE, math.gcd(size, start, width))
    count = size // tile
    skip = start // tile

    def place(b, j, pos):
        chip = pos[0] if near else 1 - pos[0]
        return (0, (2 * chip + b) * (width // tile) + skip + j)

    whole = pl.BlockSpec((own, tile), place)
    halves = [
        lambda b, j, pos: (0, skip + jnp.where(b == 0, j, count - 1)),
        lambda b, j, pos: (0, skip + jnp.where(b == 1, j, 0)),
    ]
    by_block = [pl.BlockSpec((own, tile), f) for f in halves]

    def by_core(offset):
        def index(b, j, pos):
            half = pos[1] ^ offset
            return (0, jnp.where(b == half, j, jnp.where(half == 0, count - 1, 0)))

        return pl.BlockSpec((own, tile), index)

    part = pl.BlockSpec((1, own, tile), lambda b, j, pos: (b, 0, skip + j))
    specs = [part, part, *(by_block if near else []), by_core(0), by_core(1)]
    specs = specs + [ANY] * len(after)
    fixed = pin(residual, *base) if pinned else [residual, *base]
    operands = [*fixed, *pieces, *pin(*after)]
    aliases = {}
    if out is not None:
        specs = specs + [ANY]
        aliases = {len(operands): 0}
        operands.append(out)
    return pl.pallas_call(
        near_kernel if near else far_kernel,
        out_shape=sds((own, full)),
        grid_spec=grid_spec(
            grid=(2, count),
            in_specs=[whole, *specs],
            out_specs=whole,
        ),
        input_output_aliases=aliases,
        compiler_params=params(),
        cost_estimate=order(60),
        name="near" if near else "far",
    )(*operands)


def paired(
    head_outputs, residual, projection, shrink_pool, expand_pool, pool_slot, variant_list, request_variant
):
    n_rep = lax.axis_size("rep")
    features = head_outputs[0]
    rows = features.shape[0]
    own = rows // 4
    pool_dev, rank, width = shrink_pool.shape
    cap = pool_dev // 4 + 2
    stream = residual[0]
    sizes = (cap, rank)
    tile = min(1024, width)
    cut = width // 2
    cuts = ((0, cut), (cut, width))

    def over_core(x):
        return lax.ppermute(x, "tp", [(0, 1), (1, 0), (2, 3), (3, 2)])

    def over_chip(x):
        return lax.ppermute(x, "tp", [(0, 2), (2, 0), (1, 3), (3, 1)])

    def over_both(x):
        return lax.ppermute(x, "tp", [(0, 3), (3, 0), (1, 2), (2, 1)])

    def over_rep(x, shift):
        return lax.ppermute(x, "rep", [(i, (i + shift) % n_rep) for i in range(n_rep)])

    shifts = [s for s in range(1, n_rep) if s != n_rep // 2] + [n_rep // 2]
    chosen, token = select(pool_slot, variant_list, shrink_pool, (), ((0, width),), (), n_rep, cap)
    shrink = lax.all_to_all(chosen, "rep", 0, 0, tiled=True).reshape(n_rep * cap * rank, width)

    keep0, send0, keep1, send1, token = product_early(features, projection, tile, [token])
    sums = [keep0 + over_core(send0), keep1 + over_core(send1)]
    early = [over_chip(x) for x in sums]

    *chosen, second, names, asked, token = select(
        pool_slot, variant_list, expand_pool, cuts[:1], cuts[1:], [request_variant], n_rep, cap, sums
    )
    first = [chosen[0]] + [None] * (n_rep - 1)
    for s in shifts:
        first[s] = over_rep(chosen[s], s)
    second = lax.all_to_all(second, "rep", 0, 0, tiled=True).reshape(n_rep * cap * rank, cut)

    late_keep, late_send, keep, send, token = product_columns(features, projection, tile, [*sums, token])
    late = (late_keep, over_core(late_send))
    near_base = (keep, over_core(send))

    part = score(names, request_variant, features, shrink, rank, [token, early[0]])
    shrunk = lax.all_gather(part, "tp")

    common = (names, request_variant, shrunk, late)
    straight, cross = delta(*common, first, cuts[0], n_rep, *sizes, own, (), [early[1]], [asked])
    far = [over_chip(straight), over_both(cross)]
    straight, cross, mine, send = delta(*common, [second], cuts[1], n_rep, *sizes, own, first, [near_base[1], straight])
    last = [over_chip(straight), over_both(cross)]
    theirs = over_core(send)
    keep, send, token = product(features, projection, False, True, 0, 2 * width, tile, 2, [mine])
    far_base = (keep, over_core(send))
    far = gate(far, [token])
    out = finish(None, stream, near_base, 0, width, True, [*early, mine, theirs], far)
    out = finish(out, stream, far_base, *cuts[0], False, far)
    out = finish(out, stream, far_base, *cuts[1], False, last, pinned=False)
    return out[None]


def general(
    head_outputs, residual, projection, shrink_pool, expand_pool, pool_slot, variant_list, request_variant
):
    split_count = lax.axis_size("tp")
    split_index = lax.axis_index("tp")
    replica_index = lax.axis_index("rep")
    row_count = head_outputs.shape[1]
    local_width = head_outputs.shape[2]
    rank_size = shrink_pool.shape[1]
    listed = variant_list.shape[1]
    own_rows = row_count // split_count
    flat_size = rank_size * local_width
    features = head_outputs[0]
    wanted = request_variant[0]
    my_list = lax.dynamic_index_in_dim(variant_list, replica_index, 0, keepdims=False)
    my_positions = jnp.take(pool_slot, my_list, axis=0)
    pieces = (
        lax.all_gather(shrink_pool, "rep", axis=0, tiled=True),
        lax.all_gather(expand_pool, "rep", axis=0, tiled=True),
    )
    piece_rows = pieces[0].shape[0]
    matches = (my_positions[:, None] == jnp.arange(piece_rows, dtype=jnp.int32)[None, :]).astype(BF16)
    shrink_sel = jnp.dot(matches, pieces[0].reshape(piece_rows, flat_size), preferred_element_type=F32)
    expand_sel = jnp.dot(matches, pieces[1].reshape(piece_rows, flat_size), preferred_element_type=F32)
    shrink_sel = shrink_sel.astype(BF16).reshape(listed * rank_size, local_width)
    expand_sel = expand_sel.astype(BF16).reshape(listed, rank_size, local_width)
    member = wanted[:, None] == my_list[None, :]
    scores = lax.dot_general(
        features, shrink_sel, (((1,), (1,)), ((), ())), preferred_element_type=F32
    )
    shrunk = jnp.sum(scores.reshape(row_count, listed, rank_size) * member[:, :, None], axis=1)
    own_shrunk = lax.psum_scatter(shrunk.astype(BF16), "tp", scatter_dimension=0, tiled=True)
    own_member = lax.dynamic_slice_in_dim(member, split_index * own_rows, own_rows, 0)
    spread = own_member[:, :, None] * own_shrunk[:, None, :]
    spread = spread.reshape(own_rows, listed * rank_size)
    piece = lax.all_gather(expand_sel, "tp", axis=2, tiled=True)
    delta_rows = jnp.dot(
        spread, piece.reshape(listed * rank_size, piece.shape[2]), preferred_element_type=F32
    )
    base_rows = lax.psum_scatter(
        jnp.dot(features, projection, preferred_element_type=F32).astype(BF16),
        "tp",
        scatter_dimension=0,
        tiled=True,
    ).astype(F32)
    return (residual[0].astype(F32) + base_rows + delta_rows).astype(BF16)[None]


def solution(mesh):
    in_specs = (
        P(("groups", "rep"), None, "tp"),
        P(("groups", "rep"), "tp", None),
        P("tp", None),
        P(("groups", "rep"), None, "tp"),
        P(("groups", "rep"), None, "tp"),
        P("groups"),
        P("groups", None),
        P(("groups", "rep"), None),
    )
    out_specs = P(("groups", "rep"), "tp", None)
    local = paired if mesh.shape["tp"] == 4 else general
    return jax.shard_map(local, mesh=mesh, in_specs=in_specs, out_specs=out_specs, check_vma=False)
```

```python
import functools
import math

import jax
import jax.numpy as jnp
from jax import lax
from jax.experimental import pallas as pl
from jax.experimental.pallas import tpu as pltpu
from jax.sharding import PartitionSpec as P

ANY = pl.BlockSpec(memory_space=pl.ANY)
HBM = pl.BlockSpec(memory_space=pltpu.HBM)
SMEM = pl.BlockSpec(memory_space=pltpu.SMEM)
VMEM = pl.BlockSpec(memory_space=pltpu.VMEM)
BF16 = jnp.bfloat16
F32 = jnp.float32
TILE = 1024


def order(us):
    return pl.CostEstimate(flops=int(us * 1.15e9) + 1, bytes_accessed=1, transcendentals=0)


def position():
    index = lax.axis_index("tp")
    return lax.div(index, 2), lax.rem(index, 2), lax.axis_index("rep")


def placed(spec):
    if spec.index_map is None:
        return spec
    return pl.BlockSpec(spec.block_shape, lambda *ids: spec.index_map(*ids, position()))


def grid_spec(grid, in_specs, out_specs):
    specs = out_specs if isinstance(out_specs, list) else [out_specs]
    specs = [placed(x) for x in specs]
    return pl.GridSpec(
        grid=grid,
        in_specs=[placed(x) for x in in_specs],
        out_specs=specs if isinstance(out_specs, list) else specs[0],
    )


def params(mib=48):
    return pltpu.CompilerParams(vmem_limit_bytes=mib * 2**20)


def sds(shape, dtype=BF16):
    return jax.ShapeDtypeStruct(shape, dtype)


def in_hbm(shape, dtype=BF16):
    return pltpu.HBM(shape, dtype)


def pin(*arrays):
    return [pltpu.with_memory_space_constraint(x, pltpu.HBM) for x in arrays]


TOKEN = in_hbm((8, 128), F32)


def asked_entries(names, wanted, member, place, listed, rank):
    member[...] = jnp.zeros_like(member)
    for i in range(listed):
        member[i : i + 1, :] = jnp.where(wanted == names[place(i)], 1.0, 0.0)
    entry = lax.broadcasted_iota(jnp.int32, (member.shape[0], listed * rank), 0)
    column = lax.broadcasted_iota(jnp.int32, (member.shape[0], listed * rank), 1)
    to_entry = jnp.where(column // rank == entry, 1.0, 0.0).astype(BF16)
    return lax.dot_general(
        member[...].astype(BF16), to_entry, (((0,), (0,)), ((), ())), preferred_element_type=F32
    )


def select_kernel(by_shift, by_target, named, n_rep, cap, pool_dev, rank, slot, lists, pool, *rest):
    token, idx, counts, member = rest[-4:]
    outs = rest[:-4]
    outs = outs[-(n_rep * len(by_shift) + len(by_target) + 2 * named) :]
    token[...] = jnp.zeros_like(token)
    me = lax.axis_index("rep")
    base = me * pool_dev
    for shift in range(n_rep):
        target = lax.rem(me + shift, n_rep)
        for k in range(cap + 1):
            idx[k] = 0
        count = jnp.int32(0)
        for l in range(lists.shape[1]):
            place = slot[lists[target, l]] - base
            idx[jnp.minimum(count, cap)] = place
            count = count + jnp.where((place >= 0) & (place < pool_dev), 1, 0)
        for k in range(cap):
            entry = jnp.clip(idx[k], 0, pool_dev - 1)
            rows = pl.ds(k * rank, rank)
            for c, (start, stop) in enumerate(by_shift):
                outs[c * n_rep + shift][rows, :] = pool[entry, :, start:stop]
            for c, (start, stop) in enumerate(by_target):
                outs[len(by_shift) * n_rep + c][target, rows, :] = pool[entry, :, start:stop]
    if named:
        names, asked, wanted = outs[-2], outs[-1], rest[0]
        for i in range(n_rep * cap):
            names[i] = -1
        for s in range(n_rep):
            counts[s] = 0
        for l in range(lists.shape[1]):
            variant = lists[me, l]
            owner = slot[variant] // pool_dev
            k = counts[owner]
            counts[owner] = k + 1
            names[owner * cap + jnp.minimum(k, cap - 1)] = variant

        def place(i):
            return lax.rem(me - i // cap + n_rep, n_rep) * cap + i % cap

        asked[...] = asked_entries(names, wanted[...], member, place, n_rep * cap, rank).astype(BF16)


def select(slot, lists, pool, by_shift, by_target, wanted, n_rep, cap, after=()):
    pool_dev, rank, width = pool.shape
    shapes = [in_hbm((cap * rank, stop - start)) for start, stop in by_shift for _ in range(n_rep)]
    shapes += [in_hbm((n_rep, cap * rank, stop - start)) for start, stop in by_target]
    specs = [VMEM] * len(shapes)
    rows = 128
    for x in wanted:
        rows = x.shape[1]
        shapes += [in_hbm((n_rep * cap,), jnp.int32), in_hbm((rows, n_rep * cap * rank))]
        specs += [SMEM, VMEM]
    return pl.pallas_call(
        functools.partial(select_kernel, by_shift, by_target, len(wanted), n_rep, cap, pool_dev, rank),
        out_shape=[*shapes, TOKEN],
        in_specs=[SMEM, SMEM, VMEM] + [VMEM] * len(wanted) + [ANY] * len(after),
        out_specs=[*specs, VMEM],
        scratch_shapes=[
            pltpu.SMEM((cap + 1,), jnp.int32),
            pltpu.SMEM((n_rep,), jnp.int32),
            pltpu.VMEM((-(-n_rep * cap // 16) * 16, rows), F32),
        ],
        compiler_params=params(16),
        cost_estimate=order(0),
        name="select",
    )(*pin(slot, lists, pool, *wanted), *pin(*after))


def product_early_kernel(per, pos, features, weights, keep0, send0, keep1, send1, token):
    token[...] = jnp.zeros_like(token)
    j = pl.program_id(0)
    own = features.shape[0] // 2
    result = jnp.dot(features[...], weights[...], preferred_element_type=F32).astype(BF16)
    for core in range(2):
        a, b = core * own, (1 - core) * own
        for block, keep, send in ((0, keep0, send0), (1, keep1, send1)):

            @pl.when((pos[1] == core) & (j // per == block))
            def _():
                keep[...] = result[a : a + own]
                send[...] = result[b : b + own]


def product_early(features, projection, tile, after=()):
    rows, depth = features.shape
    width = projection.shape[1] // 4
    half = rows // 2
    per = width // tile

    def kernel(features, weights, *rest):
        product_early_kernel(per, position(), features, weights, *rest[-5:])

    low = pl.BlockSpec((half // 2, tile), lambda j, pos: (0, jnp.minimum(j, per - 1)))
    high = pl.BlockSpec((half // 2, tile), lambda j, pos: (0, jnp.maximum(j - per, 0)))
    return pl.pallas_call(
        kernel,
        out_shape=[sds((half // 2, width))] * 4 + [TOKEN],
        grid_spec=grid_spec(
            grid=(2 * per,),
            in_specs=[
                pl.BlockSpec((half, depth), lambda j, pos: (1 - pos[0], 0)),
                pl.BlockSpec((depth, tile), lambda j, pos: (0, 2 * (1 - pos[0]) * per + j)),
            ]
            + [ANY] * len(after),
            out_specs=[low, low, high, high, pl.BlockSpec((8, 128), lambda j, pos: (0, 0))],
        ),
        compiler_params=params(),
        cost_estimate=order(0),
        name="product",
    )(features, projection, *pin(*after))


def product_columns_kernel(per, pos, features, weights, late, late_send, keep, send, token):
    token[...] = jnp.zeros_like(token)
    j = pl.program_id(0)
    half = features.shape[0] // 2
    own = half // 2
    result = jnp.dot(features[...], weights[...], preferred_element_type=F32).astype(BF16)
    for chip in range(2):
        here = pos[0] == chip
        other = result[(1 - chip) * half : (2 - chip) * half]

        @pl.when(here & (j < per))
        def _():
            late[...] = other

        @pl.when(here & (j >= per))
        def _():
            late_send[...] = other

        for core in range(2):

            @pl.when(here & (pos[1] == core))
            def _():
                keep[...] = result[chip * half + core * own : chip * half + (core + 1) * own][None]
                send[...] = result[chip * half + (1 - core) * own : chip * half + (2 - core) * own][None]


def product_columns(features, projection, tile, after=()):
    rows, depth = features.shape
    width = projection.shape[1] // 4
    half = rows // 2
    per = width // tile

    def block(j, pos):
        return jnp.where(j < per, pos[1], 1 - pos[1])

    rest = pl.BlockSpec((1, half // 2, tile), lambda j, pos: (block(j, pos), 0, lax.rem(j, per)))

    def kernel(features, weights, *rest):
        product_columns_kernel(per, position(), features, weights, *rest[-5:])

    return pl.pallas_call(
        kernel,
        out_shape=[in_hbm((half, width))] * 2 + [in_hbm((2, half // 2, width))] * 2 + [TOKEN],
        grid_spec=grid_spec(
            grid=(2 * per,),
            in_specs=[
                pl.BlockSpec((rows, depth), lambda j, pos: (0, 0)),
                pl.BlockSpec((depth, tile), lambda j, pos: (0, (2 * pos[0] + block(j, pos)) * per + lax.rem(j, per))),
            ]
            + [ANY] * len(after),
            out_specs=[
                pl.BlockSpec((half, tile), lambda j, pos: (0, jnp.minimum(j, per - 1))),
                pl.BlockSpec((half, tile), lambda j, pos: (0, jnp.maximum(j - per, 0))),
                rest,
                rest,
                pl.BlockSpec((8, 128), lambda j, pos: (0, 0)),
            ],
        ),
        compiler_params=params(),
        cost_estimate=order(0),
        name="product",
    )(features, projection, *pin(*after))


def product_kernel(split, pos, features, weights, keep, send, token):
    token[...] = jnp.zeros_like(token)
    own = features.shape[0] // 2
    result = jnp.dot(features[...], weights[...], preferred_element_type=F32).astype(BF16)
    low, high = result[:own], result[own:]
    if split:
        low, high = low[None], high[None]

    @pl.when(pos[1] == 0)
    def _():
        keep[...] = low
        send[...] = high

    @pl.when(pos[1] == 1)
    def _():
        keep[...] = high
        send[...] = low


def product(features, projection, other_rows, other_cols, first, count, tile, blocks, after=()):
    rows, depth = features.shape
    width = projection.shape[1]
    half = rows // 2
    own = half // 2
    tiles = count // tile

    def row_block(j, pos):
        return ((1 - pos[0]) if other_rows else pos[0], 0)

    def col_block(j, pos):
        if other_cols is None:
            return (0, j + first // tile)
        chip = (1 - pos[0]) if other_cols else pos[0]
        return (0, chip * (width // 2 // tile) + j + first // tile)

    if blocks > 1:
        per = tiles // blocks
        shape = (blocks, own, count // blocks)
        out_spec = pl.BlockSpec((1, own, tile), lambda j, pos: (j // per, 0, j % per))
    else:
        shape = (own, count)
        out_spec = pl.BlockSpec((own, tile), lambda j, pos: (0, j))
    body = functools.partial(product_kernel, blocks > 1)

    def kernel(features, weights, *rest):
        body(position(), features, weights, *rest[-3:])

    return pl.pallas_call(
        kernel,
        out_shape=[in_hbm(shape) if blocks > 1 else sds(shape)] * 2 + [TOKEN],
        grid_spec=grid_spec(
            grid=(tiles,),
            in_specs=[pl.BlockSpec((half, depth), row_block), pl.BlockSpec((depth, tile), col_block)]
            + [ANY] * len(after),
            out_specs=[out_spec] * 2 + [pl.BlockSpec((8, 128), lambda j, pos: (0, 0))],
        ),
        compiler_params=params(),
        cost_estimate=order(0),
        name="product",
    )(features, projection, *pin(*after))


def score_kernel(rank, names, wanted, features, factors, *rest):
    out, scores = rest[-2:]
    scores[...] = lax.dot_general(
        factors[...], features[...], (((1,), (1,)), ((), ())), preferred_element_type=F32
    )
    total = jnp.zeros(out.shape, F32)
    for i in range(factors.shape[0] // rank):
        total += jnp.where(wanted[...] == names[i], scores[i * rank : (i + 1) * rank, :], 0.0)
    out[...] = total


def score(names, wanted, features, factors, rank, after=()):
    rows = features.shape[0]
    return pl.pallas_call(
        functools.partial(score_kernel, rank),
        out_shape=sds((rank, rows), F32),
        in_specs=[SMEM] + [VMEM] * 3 + [ANY] * len(after),
        out_specs=VMEM,
        scratch_shapes=[pltpu.VMEM((factors.shape[0], rows), F32)],
        compiler_params=params(),
        cost_estimate=order(40),
        name="score",
    )(*pin(names, wanted), features, *pin(factors), *pin(*after))


def delta_kernel(n_blocks, n_before, known, n_rep, cap, rank, names, wanted, shrunk, late_own, late_recv, *rest):
    blocks, before = rest[:n_blocks], rest[n_blocks : n_blocks + n_before]
    straight, cross = rest[-7:-5] if before else rest[-5:-3]
    member, expand, result = rest[-3:]
    chip, core, me = position()
    listed = n_rep * cap
    half = late_own.shape[0]
    own = half // 2

    def product_of(factors, rows, known=None):
        columns = pl.ds(pl.multiple_of(rows * half, half), half)
        if known is None:
            by_owner = len(factors) == 1

            def place(i):
                return i if by_owner else lax.rem(me - i // cap + n_rep, n_rep) * cap + i % cap

            named = asked_entries(names, wanted[:, columns], member, place, listed, rank)
        else:
            named = known[...].astype(F32)
        total = jnp.sum(shrunk[:, :, columns], axis=0).astype(BF16)
        part = lax.broadcasted_iota(jnp.int32, (rank, listed * rank), 0)
        column = lax.broadcasted_iota(jnp.int32, (rank, listed * rank), 1)
        to_part = jnp.where(lax.rem(column, rank) == part, 1.0, 0.0).astype(BF16)
        turned = (((0,), (0,)), ((), ()))
        copied = lax.dot_general(total, to_part, turned, preferred_element_type=F32)
        size = listed * rank // len(factors)
        for s, factor in enumerate(factors):
            expand[pl.ds(s * size, size), :] = factor[...]
        result[...] = jnp.dot((named * copied).astype(BF16), expand[...], preferred_element_type=F32)

    product_of(blocks, 1 - chip, rest[n_blocks + n_before] if known else None)
    for out, c in ((straight, core), (cross, 1 - core)):
        rows = pl.ds(pl.multiple_of(c * own, own), own)
        base = late_own[rows, :].astype(F32) + late_recv[rows, :].astype(F32)
        out[...] = (base + result[rows, :]).astype(BF16)
    if before:
        mine, send = rest[-5], rest[-4]
        width = straight.shape[1]
        for start, factors in ((0, before), (mine.shape[1] - width, blocks)):
            product_of(factors, chip)
            for out, c in ((mine, core), (send, 1 - core)):
                rows = pl.ds(pl.multiple_of(c * own, own), own)
                out[:, start : start + width] = result[rows, :].astype(BF16)


def delta(names, wanted, shrunk, late, blocks, cut, n_rep, cap, rank, own, before=(), after=(), asked=()):
    start, stop = cut
    width = stop - start
    listed = n_rep * cap
    shapes = [in_hbm((own, width))] * 2 + ([in_hbm((own, stop))] * 2 if before else [])
    return pl.pallas_call(
        functools.partial(delta_kernel, len(blocks), len(before), len(asked), n_rep, cap, rank),
        out_shape=shapes,
        grid=(1,),
        in_specs=[SMEM]
        + [VMEM] * 2
        + [pl.BlockSpec((2 * own, width), lambda i: (0, start // width))] * 2
        + [VMEM] * (len(blocks) + len(before))
        + [pl.BlockSpec((2 * own, listed * rank), lambda i: (1 - position()[0], 0))] * len(asked)
        + [ANY] * len(after),
        out_specs=[VMEM] * len(shapes),
        scratch_shapes=[
            pltpu.VMEM((-(-listed // 16) * 16, 2 * own), F32),
            pltpu.VMEM((listed * rank, width), BF16),
            pltpu.VMEM((2 * own, width), F32),
        ],
        compiler_params=params(),
        cost_estimate=order(0),
        name="delta",
    )(*pin(names, wanted), shrunk, *(pin(*late, *blocks) if before else [*late, blocks[0], *pin(*blocks[1:])]), *pin(*before), *asked, *pin(*after))


def gate_kernel(*refs):
    pass


def gate(arrays, after):
    n = len(arrays)
    return pl.pallas_call(
        gate_kernel,
        out_shape=[sds(x.shape, x.dtype) for x in arrays],
        in_specs=[ANY] * (n + len(after)),
        out_specs=[ANY] * n,
        input_output_aliases={i: i for i in range(n)},
        cost_estimate=order(100),
        name="gate",
    )(*arrays, *pin(*after))


def near_kernel(residual, keep, recv, first, second, mine, theirs, *rest):
    out = rest[-1]
    block = pl.program_id(0)
    total = residual[...].astype(F32) + keep[0].astype(F32) + recv[0].astype(F32)
    total += jnp.where(block == 0, first[...], second[...]).astype(F32)
    total += jnp.where(block == position()[1], mine[...], theirs[...]).astype(F32)
    out[...] = total.astype(BF16)


def far_kernel(residual, keep, recv, straight, cross, *rest):
    out = rest[-1]
    total = residual[...].astype(F32) + keep[0].astype(F32) + recv[0].astype(F32)
    total += jnp.where(pl.program_id(0) == position()[1], straight[...], cross[...]).astype(F32)
    out[...] = total.astype(BF16)


def finish(out, residual, base, start, stop, near, pieces, after=(), pinned=True):
    own, full = residual.shape
    width = full // 4
    size = stop - start
    tile = min(TILE, math.gcd(size, start, width))
    count = size // tile
    skip = start // tile

    def place(b, j, pos):
        chip = pos[0] if near else 1 - pos[0]
        return (0, (2 * chip + b) * (width // tile) + skip + j)

    whole = pl.BlockSpec((own, tile), place)
    halves = [
        lambda b, j, pos: (0, skip + jnp.where(b == 0, j, count - 1)),
        lambda b, j, pos: (0, skip + jnp.where(b == 1, j, 0)),
    ]
    by_block = [pl.BlockSpec((own, tile), f) for f in halves]

    def by_core(offset):
        def index(b, j, pos):
            half = pos[1] ^ offset
            return (0, jnp.where(b == half, j, jnp.where(half == 0, count - 1, 0)))

        return pl.BlockSpec((own, tile), index)

    part = pl.BlockSpec((1, own, tile), lambda b, j, pos: (b, 0, skip + j))
    specs = [part, part, *(by_block if near else []), by_core(0), by_core(1)]
    specs = specs + [ANY] * len(after)
    fixed = pin(residual, *base) if pinned else [residual, *base]
    operands = [*fixed, *pieces, *pin(*after)]
    aliases = {}
    if out is not None:
        specs = specs + [ANY]
        aliases = {len(operands): 0}
        operands.append(out)
    return pl.pallas_call(
        near_kernel if near else far_kernel,
        out_shape=sds((own, full)),
        grid_spec=grid_spec(
            grid=(2, count),
            in_specs=[whole, *specs],
            out_specs=whole,
        ),
        input_output_aliases=aliases,
        compiler_params=params(),
        cost_estimate=order(60),
        name="near" if near else "far",
    )(*operands)


def paired(
    head_outputs, residual, projection, shrink_pool, expand_pool, pool_slot, variant_list, request_variant
):
    n_rep = lax.axis_size("rep")
    features = head_outputs[0]
    rows = features.shape[0]
    own = rows // 4
    pool_dev, rank, width = shrink_pool.shape
    cap = pool_dev // 4 + 2
    stream = residual[0]
    sizes = (cap, rank)
    tile = min(1024, width)
    cut = width // 2
    cuts = ((0, cut), (cut, width))

    def over_core(x):
        return lax.ppermute(x, "tp", [(0, 1), (1, 0), (2, 3), (3, 2)])

    def over_chip(x):
        return lax.ppermute(x, "tp", [(0, 2), (2, 0), (1, 3), (3, 1)])

    def over_both(x):
        return lax.ppermute(x, "tp", [(0, 3), (3, 0), (1, 2), (2, 1)])

    def over_rep(x, shift):
        return lax.ppermute(x, "rep", [(i, (i + shift) % n_rep) for i in range(n_rep)])

    shifts = [s for s in range(1, n_rep) if s != n_rep // 2] + [n_rep // 2]
    chosen, token = select(pool_slot, variant_list, shrink_pool, (), ((0, width),), (), n_rep, cap)
    shrink = lax.all_to_all(chosen, "rep", 0, 0, tiled=True).reshape(n_rep * cap * rank, width)

    keep0, send0, keep1, send1, token = product_early(features, projection, tile, [token])
    sums = [keep0 + over_core(send0), keep1 + over_core(send1)]
    early = [over_chip(x) for x in sums]

    *chosen, second, names, asked, token = select(
        pool_slot, variant_list, expand_pool, cuts[:1], cuts[1:], [request_variant], n_rep, cap, sums
    )
    first = [chosen[0]] + [None] * (n_rep - 1)
    for s in shifts:
        first[s] = over_rep(chosen[s], s)
    second = lax.all_to_all(second, "rep", 0, 0, tiled=True).reshape(n_rep * cap * rank, cut)

    late_keep, late_send, keep, send, token = product_columns(features, projection, tile, [*sums, token])
    late = (late_keep, over_core(late_send))
    near_base = (keep, over_core(send))

    part = score(names, request_variant, features, shrink, rank, [token, early[0]])
    shrunk = lax.all_gather(part, "tp")

    common = (names, request_variant, shrunk, late)
    straight, cross = delta(*common, first, cuts[0], n_rep, *sizes, own, (), [early[1]], [asked])
    far = [over_chip(straight), over_both(cross)]
    straight, cross, mine, send = delta(*common, [second], cuts[1], n_rep, *sizes, own, first, [near_base[1], straight])
    last = [over_chip(straight), over_both(cross)]
    theirs = over_core(send)
    keep, send, token = product(features, projection, False, True, 0, 2 * width, tile, 2, [mine])
    far_base = (keep, over_core(send))
    far = gate(far, [token])
    out = finish(None, stream, near_base, 0, width, True, [*early, mine, theirs], far)
    out = finish(out, stream, far_base, *cuts[0], False, far)
    out = finish(out, stream, far_base, *cuts[1], False, last, pinned=False)
    return out[None]


def general(
    head_outputs, residual, projection, shrink_pool, expand_pool, pool_slot, variant_list, request_variant
):
    split_count = lax.axis_size("tp")
    split_index = lax.axis_index("tp")
    replica_index = lax.axis_index("rep")
    row_count = head_outputs.shape[1]
    local_width = head_outputs.shape[2]
    rank_size = shrink_pool.shape[1]
    listed = variant_list.shape[1]
    own_rows = row_count // split_count
    flat_size = rank_size * local_width
    features = head_outputs[0]
    wanted = request_variant[0]
    my_list = lax.dynamic_index_in_dim(variant_list, replica_index, 0, keepdims=False)
    my_positions = jnp.take(pool_slot, my_list, axis=0)
    pieces = (
        lax.all_gather(shrink_pool, "rep", axis=0, tiled=True),
        lax.all_gather(expand_pool, "rep", axis=0, tiled=True),
    )
    piece_rows = pieces[0].shape[0]
    matches = (my_positions[:, None] == jnp.arange(piece_rows, dtype=jnp.int32)[None, :]).astype(BF16)
    shrink_sel = jnp.dot(matches, pieces[0].reshape(piece_rows, flat_size), preferred_element_type=F32)
    expand_sel = jnp.dot(matches, pieces[1].reshape(piece_rows, flat_size), preferred_element_type=F32)
    shrink_sel = shrink_sel.astype(BF16).reshape(listed * rank_size, local_width)
    expand_sel = expand_sel.astype(BF16).reshape(listed, rank_size, local_width)
    member = wanted[:, None] == my_list[None, :]
    scores = lax.dot_general(
        features, shrink_sel, (((1,), (1,)), ((), ())), preferred_element_type=F32
    )
    shrunk = jnp.sum(scores.reshape(row_count, listed, rank_size) * member[:, :, None], axis=1)
    own_shrunk = lax.psum_scatter(shrunk.astype(BF16), "tp", scatter_dimension=0, tiled=True)
    own_member = lax.dynamic_slice_in_dim(member, split_index * own_rows, own_rows, 0)
    spread = own_member[:, :, None] * own_shrunk[:, None, :]
    spread = spread.reshape(own_rows, listed * rank_size)
    piece = lax.all_gather(expand_sel, "tp", axis=2, tiled=True)
    delta_rows = jnp.dot(
        spread, piece.reshape(listed * rank_size, piece.shape[2]), preferred_element_type=F32
    )
    base_rows = lax.psum_scatter(
        jnp.dot(features, projection, preferred_element_type=F32).astype(BF16),
        "tp",
        scatter_dimension=0,
        tiled=True,
    ).astype(F32)
    return (residual[0].astype(F32) + base_rows + delta_rows).astype(BF16)[None]


def solution(mesh):
    in_specs = (
        P(("groups", "rep"), None, "tp"),
        P(("groups", "rep"), "tp", None),
        P("tp", None),
        P(("groups", "rep"), None, "tp"),
        P(("groups", "rep"), None, "tp"),
        P("groups"),
        P("groups", None),
        P(("groups", "rep"), None),
    )
    out_specs = P(("groups", "rep"), "tp", None)
    local = paired if mesh.shape["tp"] == 4 else general
    return jax.shard_map(local, mesh=mesh, in_specs=in_specs, out_specs=out_specs, check_vma=False)
```
